256 devices in a mesh: dom: 32 (over y, z), esplit: 8 (over x, core).
Axes of the slice: x: 4, y: 4, z: 8, core: 2. Of those that a mesh axis runs over, the one named last changes fastest.
Arguments:
- node_state: bfloat16 [32768, 512], P(('dom', 'esplit')), may hold values from -6 to 6
- edge_state: bfloat16 [131072, 512], P(('dom', 'esplit')), may hold values from -6 to 6
- senders: int32 [131072], P(('dom', 'esplit')), may hold values from 0 to 1535
- receivers: int32 [131072], P(('dom', 'esplit')), may hold values from 0 to 1023
- send_rows: int32 [32, 32, 16], P('dom'), may hold values from 0 to 1023
- edge_in: bfloat16 [1, 3, 512, 512], replicated, may hold values from -0.15625 to 0.15625
- edge_out: bfloat16 [1, 512, 512], replicated, may hold values from -0.25 to 0.25
- edge_gain: float32 [1, 512], replicated, may hold values from 0.1 to 1.9
- node_in: bfloat16 [1, 2, 512, 512], replicated, may hold values from -0.1875 to 0.1875
- node_out: bfloat16 [1, 512, 512], replicated, may hold values from -0.25 to 0.25
- node_gain: float32 [1, 512], replicated, may hold values from 0.1 to 1.9
- node_cot: bfloat16 [32768, 512], P(('dom', 'esplit')), may hold values from -6 to 6
- edge_cot: bfloat16 [131072, 512], P(('dom', 'esplit')), may hold values from -24 to 24
Outputs:
- nodes_out: bfloat16 [32768, 512], P(('dom', 'esplit'))
- edges_out: bfloat16 [131072, 512], P(('dom', 'esplit'))
- node_grad: bfloat16 [32768, 512], P(('dom', 'esplit'))
- edge_grad: bfloat16 [131072, 512], P(('dom', 'esplit'))
- weight_grads: float32 [1, 1835008], P(None, ('dom', 'esplit'))
The draws below stay inside these ranges and needn't reach their ends.
Inputs may be any that keep to these rules, and one draw needn't show every extreme that they name: An edge of partition d sends from row senders of table_d: below 1024 a node of partition d, else ghost slot k from partition p at 1024 + p * 16 + k. `receivers`: A node of the edge's own partition. send_rows[p, d, k] is a node of partition p that fills ghost slot k of partition d; lists are padded, so rows may repeat.
All inputs are finite; a program needn't handle non-finite values.
Results may differ from the reference program's by a relative error of at most 0.018.
Values may be sent and summed in bfloat16 or wider, within the bound.
A program may use at most 128 MiB of HBM per device.

```python
import jax
import jax.numpy as jnp
from jax import lax

D = 512
H = 512
GHOST = 16
LAYERS = 1
PART_NODES = 1024
PART_EDGES = 4096
TABLE_ROWS = 1536
NODES_ALL = 32768
EDGES_ALL = 131072
N_DOM = 32


def plant(entries, rng, smallest, top_value):
    spot = [jax.random.randint(jax.random.fold_in(rng, axis), (), 0, length) for axis, length in enumerate(entries.shape)]
    widest = entries.shape.index(max(entries.shape))
    next_to = spot[:widest] + [(spot[widest] + 1) % entries.shape[widest]] + spot[widest + 1:]
    return entries.at[tuple(spot)].set(smallest).at[tuple(next_to)].set(top_value)


def with_spikes(result, own_key, source, target, shards_of, factor):
    owner, partner = [(jnp.arange(result.shape[axis_at]) // (result.shape[axis_at] // shards_of)).reshape([-1 if axis == axis_at else 1 for axis in range(result.ndim)]) for axis_at in (source, target)]
    chosen = jax.random.permutation(own_key, shards_of)[partner]
    strong = (owner == chosen) | (owner == (partner + shards_of // 2) % shards_of)
    return jnp.where(strong, factor * result, result)


def block_scale(stream_key, shape, split, smallest, high):
    def one(axis_at, parts):
        draws = jax.random.uniform(jax.random.fold_in(jax.random.fold_in(stream_key, 6), axis_at), (parts,), jnp.float32, smallest / len(split), high / len(split))
        return jnp.repeat(jnp.exp(draws), shape[axis_at] // parts).reshape((-1,) + (1,) * (len(shape) - axis_at - 1))

    factor_of = one(*split[0])
    for cut in split[1:]:
        factor_of = factor_of * one(*cut)
    return factor_of


def gaussian(rng, shape, scale, bound, pieces=(), kind=jnp.bfloat16):
    array = scale * jax.random.normal(rng, shape, jnp.float32)
    if pieces:
        array = array * block_scale(rng, shape, pieces, -0.22, 0.18)
    return jnp.clip(array, -bound, bound).astype(kind)


def gaussian_with(own_key, dims, scale, limit, shards, heavy, kind=jnp.bfloat16):
    drawn = scale * jax.random.normal(own_key, dims, jnp.float32)
    if shards:
        drawn = drawn * block_scale(own_key, dims, shards, -0.22, 0.18)
    return jnp.clip(with_spikes(drawn, jax.random.fold_in(own_key, 3), *heavy), -limit, limit).astype(kind)


def setup_inputs(seed: int = 0) -> dict:
    arg_keys = jax.random.split(jax.random.key(seed), 14)
    return {
        "node_state": gaussian(arg_keys[0], (NODES_ALL, D), 1.0, 6.0, ((0, 256),)),
        "edge_state": gaussian(arg_keys[1], (EDGES_ALL, D), 1.0, 6.0, ((0, 256),)),
        "senders": plant(jax.random.randint(arg_keys[2], (EDGES_ALL,), 0, TABLE_ROWS), jax.random.fold_in(arg_keys[2], 1), 0, TABLE_ROWS - 1).astype(jnp.int32),
        "receivers": plant(jax.random.randint(arg_keys[3], (EDGES_ALL,), 0, PART_NODES), jax.random.fold_in(arg_keys[3], 1), 0, PART_NODES - 1).astype(jnp.int32),
        "send_rows": plant(jax.random.randint(arg_keys[4], (N_DOM, N_DOM, GHOST), 0, PART_NODES), jax.random.fold_in(arg_keys[4], 1), 0, PART_NODES - 1).astype(jnp.int32),
        "edge_in": gaussian(arg_keys[5], (LAYERS, 3, D, H), (3 * D) ** -0.5, 0.15625),
        "edge_out": gaussian(arg_keys[6], (LAYERS, H, D), H ** -0.5, 0.25),
        "edge_gain": jnp.clip(1.0 + 0.18 * jax.random.normal(arg_keys[7], (LAYERS, D), jnp.float32), 0.1, 1.9),
        "node_in": gaussian(arg_keys[8], (LAYERS, 2, D, H), (2 * D) ** -0.5, 0.1875),
        "node_out": gaussian(arg_keys[9], (LAYERS, H, D), H ** -0.5, 0.25),
        "node_gain": jnp.clip(1.0 + 0.18 * jax.random.normal(arg_keys[10], (LAYERS, D), jnp.float32), 0.1, 1.9),
        "node_cot": gaussian(arg_keys[11], (NODES_ALL, D), 1.0, 6.0, ((0, 256),)),
        "edge_cot": gaussian_with(arg_keys[12], (EDGES_ALL, D), 1.0, 24.0, ((0, 256),), (0, 1, 256, 6.0)),
    }


EPSILON = 1e-05

def normalize(values, gain):
    average = lax.optimization_barrier(jnp.mean(values, axis=-1, keepdims=True))
    centered = values - average
    inv_scale = lax.rsqrt(lax.optimization_barrier(jnp.mean(centered * centered, axis=-1, keepdims=True)) + EPSILON)
    return gain * centered * inv_scale

def normalize_back(values, gain, upstream):
    average = lax.optimization_barrier(jnp.mean(values, axis=-1, keepdims=True))
    centered = values - average
    inv_scale = lax.rsqrt(lax.optimization_barrier(jnp.mean(centered * centered, axis=-1, keepdims=True)) + EPSILON)
    scaled = centered * inv_scale
    grad_scaled = upstream * gain
    first = lax.optimization_barrier(jnp.mean(grad_scaled, axis=-1, keepdims=True))
    second = lax.optimization_barrier(jnp.mean(grad_scaled * scaled, axis=-1, keepdims=True))
    return inv_scale * (grad_scaled - first - scaled * second)

def swish_slope(values):
    sigma = jax.nn.sigmoid(values)
    return sigma * (1.0 + values * (1.0 - sigma))

def outer_sum(left, right):
    return lax.dot_general(left, right, (((0,), (0,)), ((), ())), preferred_element_type=jnp.float32)

def project_back(grad, weight):
    return lax.dot_general(grad, weight, (((1,), (1,)), ((), ())), preferred_element_type=jnp.float32)

def edge_forward(edges, sent_rows, recv_rows, w_in, w_out, gain):
    pre_act = jnp.dot(edges, w_in[0], preferred_element_type=jnp.float32)
    pre_act = pre_act + jnp.dot(sent_rows, w_in[1], preferred_element_type=jnp.float32)
    pre_act = pre_act + jnp.dot(recv_rows, w_in[2], preferred_element_type=jnp.float32)
    hidden = jax.nn.silu(pre_act).astype(jnp.bfloat16)
    message = jnp.dot(hidden, w_out, preferred_element_type=jnp.float32)
    updated = (edges.astype(jnp.float32) + normalize(message, gain)).astype(jnp.bfloat16)
    return (updated, pre_act, message, hidden)

def edge_backward(edges, sent_rows, recv_rows, pre_act, message, hidden, w_in, w_out, gain, upstream):
    grad_message = normalize_back(message, gain, upstream).astype(jnp.bfloat16)
    grad_out = outer_sum(hidden, grad_message)
    grad_pre = (project_back(grad_message, w_out) * swish_slope(pre_act)).astype(jnp.bfloat16)
    grad_in = jnp.stack([outer_sum(edges, grad_pre), outer_sum(sent_rows, grad_pre), outer_sum(recv_rows, grad_pre)])
    grad_edges = upstream + project_back(grad_pre, w_in[0])
    return (grad_edges, project_back(grad_pre, w_in[1]), project_back(grad_pre, w_in[2]), grad_in, grad_out)

def node_forward(nodes, aggregate, w_in, w_out, gain):
    pre_act = jnp.dot(nodes, w_in[0], preferred_element_type=jnp.float32)
    pre_act = pre_act + jnp.dot(aggregate, w_in[1], preferred_element_type=jnp.float32)
    hidden = jax.nn.silu(pre_act).astype(jnp.bfloat16)
    message = jnp.dot(hidden, w_out, preferred_element_type=jnp.float32)
    updated = (nodes.astype(jnp.float32) + normalize(message, gain)).astype(jnp.bfloat16)
    return (updated, pre_act, message, hidden)

def node_backward(nodes, aggregate, pre_act, message, hidden, w_in, w_out, gain, upstream):
    grad_message = normalize_back(message, gain, upstream).astype(jnp.bfloat16)
    grad_out = outer_sum(hidden, grad_message)
    grad_pre = (project_back(grad_message, w_out) * swish_slope(pre_act)).astype(jnp.bfloat16)
    grad_in = jnp.stack([outer_sum(nodes, grad_pre), outer_sum(aggregate, grad_pre)])
    grad_nodes = upstream + project_back(grad_pre, w_in[0])
    grad_aggregate = project_back(grad_pre, w_in[1]).astype(jnp.bfloat16)
    return (grad_nodes, grad_aggregate, grad_in, grad_out)

def build_tables(part_view, send_rows):
    owners = jnp.arange(N_DOM, dtype=jnp.int32)[:, None, None]
    picked = part_view[owners, send_rows]
    ghosts = jnp.transpose(picked, (1, 0, 2, 3)).reshape(N_DOM, N_DOM * GHOST, D)
    return jnp.concatenate([part_view, ghosts], axis=1)

def reference(node_state, edge_state, senders, receivers, send_rows, edge_in, edge_out, edge_gain, node_in, node_out, node_gain, node_cot, edge_cot):
    send_part = senders.reshape(N_DOM, PART_EDGES)
    recv_part = receivers.reshape(N_DOM, PART_EDGES)
    nodes = node_state
    edges = edge_state.reshape(N_DOM, PART_EDGES, D)
    saved = []
    for layer in range(LAYERS):
        tables = build_tables(nodes.reshape(N_DOM, PART_NODES, D), send_rows)

        def forward_part(item):
            edge_rows, table, send_ids, recv_ids = item
            updated = edge_forward(edge_rows, table[send_ids], table[recv_ids], edge_in[layer], edge_out[layer], edge_gain[layer])[0]
            summed = jax.ops.segment_sum(updated.astype(jnp.float32), recv_ids, num_segments=PART_NODES)
            return (updated, summed)
        new_edges, summed = lax.map(forward_part, (edges, tables, send_part, recv_part))
        aggregate = summed.reshape(NODES_ALL, D).astype(jnp.bfloat16)
        new_nodes = node_forward(nodes, aggregate, node_in[layer], node_out[layer], node_gain[layer])[0]
        saved.append((nodes, edges, tables, aggregate))
        nodes, edges = (new_nodes, new_edges)
    nodes_out = nodes
    edges_out = edges.reshape(EDGES_ALL, D)
    grad_nodes = node_cot.astype(jnp.float32)
    grad_edges = edge_cot.astype(jnp.float32).reshape(N_DOM, PART_EDGES, D)
    flats = []
    for layer in reversed(range(LAYERS)):
        nodes, edges, tables, aggregate = saved[layer]
        _, npre, nmsg, nhid = node_forward(nodes, aggregate, node_in[layer], node_out[layer], node_gain[layer])
        direct, grad_agg, gn_in, gn_out = node_backward(nodes, aggregate, npre, nmsg, nhid, node_in[layer], node_out[layer], node_gain[layer], grad_nodes)
        grad_agg_part = grad_agg.reshape(N_DOM, PART_NODES, D)

        def backward_part(item):
            edge_rows, table, send_ids, recv_ids, upstream, agg_grad = item
            sent_rows = table[send_ids]
            recv_rows = table[recv_ids]
            _, pre_act, message, hidden = edge_forward(edge_rows, sent_rows, recv_rows, edge_in[layer], edge_out[layer], edge_gain[layer])
            total = upstream + agg_grad[recv_ids].astype(jnp.float32)
            new_grad, grad_sent, grad_recv, gi, go = edge_backward(edge_rows, sent_rows, recv_rows, pre_act, message, hidden, edge_in[layer], edge_out[layer], edge_gain[layer], total)
            dtable = jax.ops.segment_sum(jnp.concatenate([grad_sent, grad_recv]), jnp.concatenate([send_ids, recv_ids]), num_segments=TABLE_ROWS)
            return (new_grad, dtable, gi, go)
        grad_edges, dtables, gi_all, go_all = lax.map(backward_part, (edges, tables, send_part, recv_part, grad_edges, grad_agg_part))
        own = dtables[:, :PART_NODES].reshape(NODES_ALL, D)
        ghost = dtables[:, PART_NODES:].reshape(N_DOM * N_DOM * GHOST, D)
        target = jnp.arange(N_DOM, dtype=jnp.int32)[None, :, None] * PART_NODES + jnp.transpose(send_rows, (1, 0, 2))
        own = own.at[target.reshape(-1)].add(ghost)
        grad_nodes = direct + own
        flat = jnp.concatenate([lax.optimization_barrier(jnp.sum(gi_all, axis=0)).reshape(-1), lax.optimization_barrier(jnp.sum(go_all, axis=0)).reshape(-1), gn_in.reshape(-1), gn_out.reshape(-1)])
        flats.insert(0, flat)
    return (nodes_out, edges_out, grad_nodes.astype(jnp.bfloat16), grad_edges.reshape(EDGES_ALL, D).astype(jnp.bfloat16), jnp.stack(flats))
```

```python
import functools

import jax
import jax.numpy as jnp
from jax import lax
from jax.experimental import pallas as pl
from jax.experimental.pallas import tpu as pltpu
from jax.sharding import PartitionSpec as P

EPSILON = 1e-05
BF = jnp.bfloat16
F32 = jnp.float32
MESH = pl.DeviceIdType.MESH

NZ = 8
NY = 4
NX = 4
DOM = NY * NZ
S = NX * 2
D = 512
N = 128
PN = N * S
E = 512
GH = 16
SLAB = DOM // S * GH
NJ = DOM // S
HALF = D // 2
NMAT = 7
OUT_ROWS = 14


def dot(a, b):
    return lax.dot_general(a, b, (((1,), (0,)), ((), ())), preferred_element_type=F32)


def dot_nt(a, b):
    return lax.dot_general(a, b, (((1,), (1,)), ((), ())), preferred_element_type=F32)


def dot_tn(a, b):
    return lax.dot_general(a, b, (((0,), (0,)), ((), ())), preferred_element_type=F32)


def normalize(values, gain):
    average = jnp.mean(values, axis=-1, keepdims=True)
    centered = values - average
    inv_scale = lax.rsqrt(jnp.mean(centered * centered, axis=-1, keepdims=True) + EPSILON)
    return gain * centered * inv_scale


def normalize_back(values, gain, upstream):
    average = jnp.mean(values, axis=-1, keepdims=True)
    centered = values - average
    inv_scale = lax.rsqrt(jnp.mean(centered * centered, axis=-1, keepdims=True) + EPSILON)
    scaled = centered * inv_scale
    grad_scaled = upstream * gain
    first = jnp.mean(grad_scaled, axis=-1, keepdims=True)
    second = jnp.mean(grad_scaled * scaled, axis=-1, keepdims=True)
    return inv_scale * (grad_scaled - first - scaled * second)


def swish(values):
    return values * jax.nn.sigmoid(values)


def swish_slope(values):
    sigma = jax.nn.sigmoid(values)
    return sigma * (1.0 + values * (1.0 - sigma))


def rows_loop(total, step, fn):
    def one(i, carry):
        fn(pl.multiple_of(i * step, step))
        return carry

    lax.fori_loop(0, total // step, one, 0)


class Sems:
    def __init__(self, ref):
        self.ref = ref
        self.used = 0

    def take(self, count):
        base = self.used
        self.used += count
        return lambda i: self.ref.at[base + i]


N_SEM = 200


def kernel(
    nodes_in, snd_row, rcv_row, lst_row, egain, ngain, ncot,
    edges_hbm, ein_hbm, eout_hbm, nin_hbm, nout_hbm, ecot_hbm,
    nodes_out, edges_out, ngrad, egrad, wout,
    edges, ein, eout, nin, nout, ecot,
    ps, pr, pst, prt, tbl, sent_acc, sent, recv, pre, msg, hid,
    gsend, aggs_send, aggs_recv, aggx_send, aggx_recv, agg_own,
    agg, npre, nhid, gdirect, dnpre, dnmsg, dagg_own, dagg,
    gedge, dmsg, dpre, dsent, drecv,
    gg_ssend, gg_srecv, gg_xsend, gg_xrecv, gg_own, a2_send, retg,
    own_ssend, own_srecv, own_xsend, own_xrecv, own_own,
    fn_ssend, fn_srecv, fn_own, fn_ysend, fn_yrecv, fn_zsend, fn_zrecv,
    fe_ssend, fe_srecv, fe_own, fe_ysend, fe_yrecv, fe_zsend, fe_zrecv,
    fin, g1_recv, g2_src, g2_recv,
    sem_ref,
):
    d = lax.axis_index("dom")
    s = lax.axis_index("esplit")
    y = d // NZ
    z = d % NZ
    x = s // 2
    c = s % 2
    lin = d * S + s
    sib = s + 1 - 2 * c
    t_mine = (s - d + DOM) % S
    sems = Sems(sem_ref)
    pending = []

    def remote(src, dst, send_sem, recv_sem, dom, split):
        return pltpu.make_async_remote_copy(
            src_ref=src, dst_ref=dst, send_sem=send_sem, recv_sem=recv_sem,
            device_id=(dom, split), device_id_type=MESH,
        )

    bar = pltpu.get_barrier_semaphore()

    def greet(dom, split):
        pl.semaphore_signal(bar, inc=1, device_id=(dom, split), device_id_type=MESH)

    for k in range(1, S):
        greet(d, (s + k) % S)
    for k in range(1, NY):
        greet((y + k) % NY * NZ + z, s)
    for k in range(1, NZ):
        greet(y * NZ + (z + k) % NZ, s)
    for j in range(NJ):
        pl.when(t_mine + S * j != d)(functools.partial(greet, t_mine + S * j, s))
    first_row = OUT_ROWS * lin
    b_first = first_row // 16
    b_last = (first_row + OUT_ROWS - 1) // 16
    b_mine = DOM * s + d
    l_first = (16 * b_mine) // OUT_ROWS
    l_last = (16 * b_mine + 15) // OUT_ROWS

    def block_lin(b):
        return (b % DOM) * S + b // DOM

    pl.when(block_lin(b_first) != lin)(
        functools.partial(greet, b_first % DOM, b_first // DOM))
    pl.when((b_last != b_first) & (block_lin(b_last) != lin))(
        functools.partial(greet, b_last % DOM, b_last // DOM))

    lsem = sems.take(6)
    loads = [
        pltpu.make_async_copy(a, b, lsem(i))
        for i, (a, b) in enumerate(
            ((edges_hbm, edges), (ein_hbm, ein), (eout_hbm, eout), (nin_hbm, nin),
             (nout_hbm, nout), (ecot_hbm, ecot)))
    ]
    for load in loads:
        load.start()

    tbl[pl.ds(pl.multiple_of(s * N, N), N), :] = nodes_in[...]

    def g2_valid(i):
        return (s < NMAT) & (l_first + i <= l_last) & (l_first + i != lin)

    arrivals = (S - 1) + (NY - 1) + (NZ - 1)
    for j in range(NJ):
        arrivals = arrivals + jnp.where(t_mine + S * j != d, 1, 0)
    for i in range(3):
        arrivals = arrivals + jnp.where(g2_valid(i), 1, 0)
    pl.semaphore_wait(bar, arrivals)

    class Gather:
        def __init__(self, buf, offset, rows):
            self.buf, self.offset, self.rows = buf, offset, rows
            self.ss, self.rs = sems.take(7), sems.take(7)

        def block(self, split):
            return self.buf.at[pl.ds(pl.multiple_of(self.offset(split), self.rows), self.rows), :]

        def copy(self, origin, k, split, src=None):
            blk = self.block(origin)
            return remote(blk if src is None else src, blk, self.ss(k), self.rs(k), d, split)

        def start(self, src=None):
            for dx in (2, 1, 3):
                cp = self.copy(s, dx - 1, (x + dx) % NX * 2 + c, src)
                cp.start()
                pending.append(cp)
            cp = self.copy(s, 3, sib, src)
            cp.start()
            pending.append(cp)

        def forward(self, dx):
            origin = (x - dx + NX) % NX * 2 + c
            self.copy(origin, dx - 1, sib).wait_recv()
            cp = self.copy(origin, 3 + dx, sib)
            cp.start()
            pending.append(cp)

        def from_sib(self, dx):
            if dx == 0:
                self.copy(sib, 3, sib).wait_recv()
            else:
                self.copy((x - dx + NX) % NX * 2 + 1 - c, 3 + dx, sib).wait_recv()

        def finish(self):
            for dx in (1, 3, 2):
                self.forward(dx)
            for dx in (0, 1, 3, 2):
                self.from_sib(dx)

    class Scatter:
        def __init__(self, compute, own, ssend, srecv, xsend, xrecv):
            self.compute, self.own = compute, own
            self.ssend, self.srecv, self.xsend, self.xrecv = ssend, srecv, xsend, xrecv
            self.s1, self.r1 = sems.take(4), sems.take(4)
            self.s2, self.r2 = sems.take(3), sems.take(3)

        def to_sib(self, dx):
            return remote(self.ssend.at[dx], self.srecv.at[dx], self.s1(dx), self.r1(dx), d, sib)

        def to_chip(self, dx):
            return remote(
                self.xsend.at[dx - 1], self.xrecv.at[dx - 1], self.s2(dx - 1), self.r2(dx - 1),
                d, (x + dx) % NX * 2 + c)

        def start(self):
            for dx in (2, 1, 3, 0):
                self.ssend[dx] = self.compute((x + dx) % NX * 2 + 1 - c).astype(BF)
                cp = self.to_sib(dx)
                cp.start()
                pending.append(cp)

        def middle(self):
            for dx in (2, 1, 3):
                mine = self.compute((x + dx) % NX * 2 + c)
                self.to_sib(dx).wait_recv()
                self.xsend[dx - 1] = (mine + self.srecv[dx].astype(F32)).astype(BF)
                cp = self.to_chip(dx)
                cp.start()
                pending.append(cp)
            mine = self.compute(s)
            self.to_sib(0).wait_recv()
            self.own[...] = mine + self.srecv[0].astype(F32)

        def finish(self):
            total = self.own[...]
            for dx in (1, 3, 2):
                self.to_chip(dx).wait_recv()
                total = total + self.xrecv[dx - 1].astype(F32)
            return total

    class Swap:
        def __init__(self, src, dst):
            self.src, self.dst = src, dst
            self.ss, self.rs = sems.take(NJ), sems.take(NJ)

        def start(self):
            for j in range(NJ):
                peer = t_mine + S * j
                land = pl.multiple_of((d % S) * SLAB + (d // S) * GH, GH)
                cp = remote(
                    self.src.at[pl.ds(j * GH, GH), :], self.dst.at[pl.ds(land, GH), :],
                    self.ss(j), self.rs(d // S), peer, s)
                pl.when(peer != d)(cp.start)

                @pl.when(peer == d)
                def _():
                    self.dst[pl.ds(land, GH), :] = self.src[pl.ds(j * GH, GH), :]

        def finish(self):
            for j in range(NJ):
                peer = t_mine + S * j
                land = pl.multiple_of(t_mine * SLAB + j * GH, GH)
                cp = remote(
                    self.src.at[pl.ds(j * GH, GH), :], self.dst.at[pl.ds(land, GH), :],
                    self.ss(j), self.rs(j), peer, s)

                @pl.when(peer != d)
                def _():
                    cp.wait_recv()
                    cp.wait_send()

    gather_nodes = Gather(tbl, lambda q: q * N, N)
    gather_nodes.start(nodes_in)

    def permuted(values):
        ghost = values - PN
        part = ghost // GH
        place = PN + (part % S) * SLAB + (part // S) * GH + ghost % GH
        return jnp.where(values >= PN, place, values)

    def column(row):
        size = row.shape[1]
        hit = lax.broadcasted_iota(jnp.int32, (size, size), 0) == lax.broadcasted_iota(
            jnp.int32, (size, size), 1)
        return jnp.sum(jnp.where(hit, row.astype(F32), 0.0), axis=1, keepdims=True).astype(jnp.int32)

    def hot(mask):
        return jnp.where(mask, 1.0, 0.0).astype(BF)

    send_r = permuted(snd_row[...])
    recv_r = rcv_row[...]
    send_c = column(send_r)
    recv_c = column(recv_r)

    def build_t(r0):
        ids = lax.broadcasted_iota(jnp.int32, (256, E), 0) + r0
        pst[pl.ds(r0, 256), :] = hot(ids == send_r)

    rows_loop(PN + S * SLAB, 256, build_t)

    def build_rt(r0):
        ids = lax.broadcasted_iota(jnp.int32, (256, E), 0) + r0
        prt[pl.ds(r0, 256), :] = hot(ids == recv_r)

    rows_loop(PN, 256, build_rt)
    for c0 in range(0, PN + S * SLAB, 256):
        ids = lax.broadcasted_iota(jnp.int32, (E, 256), 1) + c0
        ps[:, c0:c0 + 256] = hot(ids == send_c)
        if c0 < PN:
            pr[:, c0:c0 + 256] = hot(ids == recv_c)
    lists_c = column(lst_row[...])

    loads[0].wait()
    loads[1].wait()

    def edge_part(r0):
        pre[pl.ds(r0, 256), :] = dot(edges[pl.ds(r0, 256), :], ein[0])

    rows_loop(E, 256, edge_part)

    gather_nodes.finish()

    hit = jnp.zeros((SLAB, 1), jnp.int32)
    for t in range(S):
        hit = jnp.where(t_mine == t, lists_c[t * SLAB:(t + 1) * SLAB, :], hit)
    pick = hot(lax.broadcasted_iota(jnp.int32, (SLAB, PN), 1) == hit)
    gsend[...] = dot(pick, tbl[:PN, :]).astype(BF)
    ghosts = tbl.at[pl.ds(PN, S * SLAB), :]
    swap_ghost = Swap(gsend, ghosts)
    swap_ghost.start()

    def gather_rows(r0):
        rows = pl.ds(r0, 256)
        got = dot(pr[rows, :], tbl[:PN, :]).astype(BF)
        recv[rows, :] = got
        pre[rows, :] = pre[rows, :] + dot(got, ein[2])
        sent_acc[rows, :] = dot(ps[rows, :PN], tbl[:PN, :])

    rows_loop(E, 256, gather_rows)
    swap_ghost.finish()
    gather_ghost = Gather(ghosts, lambda q: ((q - d + DOM) % S) * SLAB, SLAB)
    gather_ghost.start()
    gather_ghost.finish()

    loads[2].wait()
    edge_gain = egain[...]

    def edge_forward(r0):
        rows = pl.ds(r0, 256)
        got = (sent_acc[rows, :] + dot(ps[rows, PN:], tbl[PN:, :])).astype(BF)
        sent[rows, :] = got
        act = pre[rows, :] + dot(got, ein[1])
        pre[rows, :] = act
        hidden = swish(act).astype(BF)
        hid[rows, :] = hidden
        message = dot(hidden, eout[...])
        msg[rows, :] = message
        edges_out[rows, :] = (edges[rows, :].astype(F32) + normalize(message, edge_gain)).astype(BF)

    rows_loop(E, 256, edge_forward)

    def agg_block(q):
        return dot(prt[pl.ds(pl.multiple_of(q * N, N), N), :], edges_out[...])

    reduce_agg = Scatter(agg_block, agg_own, aggs_send, aggs_recv, aggx_send, aggx_recv)
    reduce_agg.start()
    reduce_agg.middle()
    loads[3].wait()
    loads[4].wait()
    loads[5].wait()
    npre[...] = dot(nodes_in[...], nin[0])
    agg[...] = reduce_agg.finish().astype(BF)

    node_gain = ngain[...]
    act = npre[...] + dot(agg[...], nin[1])
    hidden = swish(act).astype(BF)
    nhid[...] = hidden
    message = dot(hidden, nout[...])
    nodes_out[...] = (nodes_in[...].astype(F32) + normalize(message, node_gain)).astype(BF)
    upstream = ncot[...].astype(F32)
    grad_message = normalize_back(message, node_gain, upstream).astype(BF)
    dnmsg[...] = grad_message
    grad_pre = (dot_nt(grad_message, nout[...]) * swish_slope(act)).astype(BF)
    dnpre[...] = grad_pre
    dagg_own[...] = dot_nt(grad_pre, nin[1]).astype(BF)
    dagg[pl.ds(pl.multiple_of(s * N, N), N), :] = dagg_own[...]

    gather_dagg = Gather(dagg, lambda q: q * N, N)
    gather_dagg.start(dagg_own)
    gdirect[...] = upstream + dot_nt(grad_pre, nin[0])

    mine_cols = pl.ds(pl.multiple_of(c * HALF, HALF), HALF)
    sib_cols = pl.ds(pl.multiple_of((1 - c) * HALF, HALF), HALF)

    class Weights:
        def __init__(self, base, pairs, ssend, srecv, own, ysend, yrecv, zsend, zrecv):
            self.base, self.pairs = base, pairs
            self.ssend, self.srecv, self.own = ssend, srecv, own
            self.ysend, self.yrecv, self.zsend, self.zrecv = ysend, yrecv, zsend, zrecv
            self.s0, self.r0 = sems.take(len(pairs)), sems.take(len(pairs))
            self.sy, self.ry = sems.take(NY - 1), sems.take(NY - 1)
            self.sz, self.rz = sems.take(NZ - 1), sems.take(NZ - 1)

        def sib_copy(self, i):
            return remote(self.ssend.at[i], self.srecv.at[i], self.s0(i), self.r0(i), d, sib)

        def y_copy(self, k):
            return remote(
                self.ysend.at[k], self.yrecv.at[k - 1], self.sy(k - 1), self.ry(k - 1),
                (y + k) % NY * NZ + z, s)

        def z_copy(self, k):
            return remote(
                self.zsend.at[k], self.zrecv.at[k - 1], self.sz(k - 1), self.rz(k - 1),
                y * NZ + (z + k) % NZ, s)

        def products(self, i):
            left, right = self.pairs[i]
            self.ssend[i] = dot_tn(left[...], right[:, sib_cols]).astype(BF)
            cp = self.sib_copy(i)
            cp.start()
            pending.append(cp)
            self.own[i] = dot_tn(left[...], right[:, mine_cols])

        def to_y(self):
            for i in range(len(self.pairs)):
                self.sib_copy(i).wait_recv()
            for k in (2, 1, 3, 0):
                rows = pl.ds(pl.multiple_of((y + k) % NY * 128, 128), 128)
                for i in range(len(self.pairs)):
                    both = self.own[i, rows, :] + self.srecv[i, rows, :].astype(F32)
                    self.ysend[k, i] = both.astype(BF)
                if k:
                    cp = self.y_copy(k)
                    cp.start()
                    pending.append(cp)

        def to_z(self):
            for k in range(1, NY):
                self.y_copy(k).wait_recv()
            for k in (4, 3, 5, 2, 6, 1, 7, 0):
                rows = pl.ds(pl.multiple_of((z + k) % NZ * 16, 16), 16)
                for i in range(len(self.pairs)):
                    total = self.ysend[0, i, rows, :].astype(F32)
                    for q in range(NY - 1):
                        total = total + self.yrecv[q, i, rows, :].astype(F32)
                    self.zsend[k, i] = total.astype(BF)
                if k:
                    cp = self.z_copy(k)
                    cp.start()
                    pending.append(cp)

        def finish(self):
            for k in range(1, NZ):
                self.z_copy(k).wait_recv()
            for i in range(len(self.pairs)):
                total = self.zsend[0, i].astype(F32)
                for k in range(NZ - 1):
                    total = total + self.zrecv[k, i].astype(F32)
                fin[self.base + i] = total

    node_weights = Weights(
        4, ((nodes_in, dnpre), (agg, dnpre), (nhid, dnmsg)),
        fn_ssend, fn_srecv, fn_own, fn_ysend, fn_yrecv, fn_zsend, fn_zrecv)
    edge_weights = Weights(
        0, ((edges, dpre), (sent, dpre), (recv, dpre), (hid, dmsg)),
        fe_ssend, fe_srecv, fe_own, fe_ysend, fe_yrecv, fe_zsend, fe_zrecv)

    for i in range(3):
        node_weights.products(i)
    for dx in (1, 3, 2):
        gather_dagg.forward(dx)
    node_weights.to_y()
    for dx in (0, 1, 3, 2):
        gather_dagg.from_sib(dx)

    def edge_backward(r0):
        rows = pl.ds(r0, 256)
        up = ecot[rows, :].astype(F32) + dot(pr[rows, :], dagg[...])
        gedge[rows, :] = up
        grad_msg = normalize_back(msg[rows, :], edge_gain, up).astype(BF)
        dmsg[rows, :] = grad_msg
        grad = (dot_nt(grad_msg, eout[...]) * swish_slope(pre[rows, :])).astype(BF)
        dpre[rows, :] = grad
        dsent[rows, :] = dot_nt(grad, ein[1]).astype(BF)

    rows_loop(E, 256, edge_backward)

    def ghost_block(q):
        place = PN + ((q - d + DOM) % S) * SLAB
        return dot(pst[pl.ds(pl.multiple_of(place, SLAB), SLAB), :], dsent[...])

    reduce_ghost = Scatter(
        ghost_block, gg_own, gg_ssend, gg_srecv, gg_xsend, gg_xrecv)
    reduce_ghost.start()
    edge_weights.products(3)
    reduce_ghost.middle()
    for i in range(3):
        edge_weights.products(i)
    edge_weights.to_y()

    def recv_grad(r0):
        rows = pl.ds(r0, 256)
        drecv[rows, :] = dot_nt(dpre[rows, :], ein[2]).astype(BF)

    rows_loop(E, 256, recv_grad)
    a2_send[...] = reduce_ghost.finish().astype(BF)
    swap_back = Swap(a2_send, retg)
    swap_back.start()

    def own_block(q):
        rows = pl.ds(pl.multiple_of(q * N, N), N)
        return dot(pst[rows, :], dsent[...]) + dot(prt[rows, :], drecv[...])

    reduce_own = Scatter(
        own_block, own_own, own_ssend, own_srecv, own_xsend, own_xrecv)
    reduce_own.start()
    swap_back.finish()
    gather_back = Gather(retg, lambda q: ((q - d + DOM) % S) * SLAB, SLAB)
    gather_back.start()
    reduce_own.middle()
    node_weights.to_z()
    for dx in (1, 3, 2):
        gather_back.forward(dx)
    edge_weights.to_z()

    def edge_grad(r0):
        rows = pl.ds(r0, 256)
        egrad[rows, :] = (gedge[rows, :] + dot_nt(dpre[rows, :], ein[0])).astype(BF)

    rows_loop(E, 256, edge_grad)
    place = hot(lax.broadcasted_iota(jnp.int32, (N, S * SLAB), 0) + s * N == lst_row[...])
    for dx in (0, 1, 3, 2):
        gather_back.from_sib(dx)
    ngrad[...] = (gdirect[...] + dot(place, retg[...]) + reduce_own.finish()).astype(BF)

    node_weights.finish()
    edge_weights.finish()
    s_g1, r_g1 = sems.take(S - 1), sems.take(S - 1)

    def g1_copy(k):
        peer = (s + k) % S
        which = jnp.minimum(peer, NMAT - 1)
        return remote(fin.at[which], g1_recv.at[k - 1], s_g1(k - 1), r_g1(k - 1), d, peer)

    for k in range(1, S):
        cp = g1_copy(k)
        pl.when((s + k) % S < NMAT)(cp.start)
    s_g2, r_g2 = sems.take(3), sems.take(2)

    def g2_copy(i, slot):
        to = l_first + i
        to = jnp.minimum(to, DOM * S - 1)
        return remote(g2_src, g2_recv.at[slot], s_g2(i), r_g2(slot), to // S, to % S)

    @pl.when(s < NMAT)
    def _():
        for k in range(1, S):
            g1_copy(k).wait_recv()
        for half in range(2):
            total = fin[jnp.minimum(s, NMAT - 1)]
            total = jnp.where(c == half, total, 0.0)
            for k in range(1, S):
                origin = (s - k + S) % S
                total = total + jnp.where(origin % 2 == half, g1_recv[k - 1], 0.0)
            g2_src[:, half * HALF:(half + 1) * HALF] = total
        for i in range(3):
            to = l_first + i
            slot = b_mine - (OUT_ROWS * to) // 16
            for choice in range(2):
                pl.when(g2_valid(i) & (slot == choice))(g2_copy(i, choice).start)

                @pl.when((to <= l_last) & (to == lin) & (slot == choice))
                def _():
                    g2_recv[choice] = g2_src[...]

    pl.when(block_lin(b_first) != lin)(g2_copy(0, 0).wait_recv)
    pl.when((b_last != b_first) & (block_lin(b_last) != lin))(g2_copy(0, 1).wait_recv)
    shift = first_row % 16
    for choice in range(0, 16, 2):
        @pl.when(shift == choice)
        def _():
            split = min(16 - choice, OUT_ROWS)
            wout[:split, :] = g2_recv[0, choice:choice + split, :]
            if split < OUT_ROWS:
                wout[split:, :] = g2_recv[1, :OUT_ROWS - split, :]

    for cp in pending:
        cp.wait_send()
    for k in range(1, S):
        pl.when((s + k) % S < NMAT)(g1_copy(k).wait_send)
    for i in range(3):
        pl.when(g2_valid(i))(g2_copy(i, 0).wait_send)


def scratch():
    def bf(*shape):
        return pltpu.VMEM(shape, BF)

    def f32(*shape):
        return pltpu.VMEM(shape, F32)

    T = PN + S * SLAB

    def scatter(rows):
        return [bf(NX, rows, D), bf(NX, rows, D), bf(NX - 1, rows, D), bf(NX - 1, rows, D)]

    def weights(count):
        return [
            bf(count, D, HALF), bf(count, D, HALF), f32(count, D, HALF),
            bf(NY, count, 128, HALF), bf(NY - 1, count, 128, HALF),
            bf(NZ, count, 16, HALF), bf(NZ - 1, count, 16, HALF),
        ]

    return [
        bf(E, D), bf(3, D, D), bf(D, D), bf(2, D, D), bf(D, D), bf(E, D),
        bf(E, T), bf(E, PN), bf(T, E), bf(PN, E), bf(T, D), f32(E, D), bf(E, D), bf(E, D),
        f32(E, D), f32(E, D), bf(E, D),
        bf(SLAB, D), *scatter(N), f32(N, D),
        bf(N, D), f32(N, D), bf(N, D), f32(N, D), bf(N, D), bf(N, D), bf(N, D), bf(PN, D),
        f32(E, D), bf(E, D), bf(E, D), bf(E, D), bf(E, D),
        *scatter(SLAB), f32(SLAB, D), bf(SLAB, D), bf(S * SLAB, D),
        *scatter(N), f32(N, D),
        *weights(3), *weights(4),
        f32(NMAT, 16, HALF), f32(S - 1, 16, HALF), f32(16, D), f32(2, 16, D),
        pltpu.SemaphoreType.DMA((N_SEM,)),
    ]


def hand_over(a0, a1, a2, a3, w_in, b0, b1, b2, b3, w_out, sem):
    copies = [
        pltpu.make_async_copy(src, dst, sem.at[i])
        for i, (src, dst) in enumerate(((a0, b0), (a1, b1), (a2, b2), (a3, b3)))
    ]
    for cp in copies:
        cp.start()
    for i in range(OUT_ROWS):
        w_out[:, i * D:(i + 1) * D] = w_in[i:i + 1, :]
    for cp in copies:
        cp.wait()


def body(
    node_state, edge_state, senders, receivers, send_rows, edge_in, edge_out, edge_gain,
    node_in, node_out, node_gain, node_cot, edge_cot,
):
    lists = send_rows.reshape(NJ, S, GH).transpose(1, 0, 2).reshape(1, S * SLAB)
    vmem = pl.BlockSpec(memory_space=pltpu.VMEM)
    hbm = pl.BlockSpec(memory_space=pl.ANY)
    states = (
        jax.ShapeDtypeStruct((N, D), BF),
        jax.ShapeDtypeStruct((E, D), BF),
        jax.ShapeDtypeStruct((N, D), BF),
        jax.ShapeDtypeStruct((E, D), BF),
    )
    results = pl.pallas_call(
        kernel,
        out_shape=states + (jax.ShapeDtypeStruct((OUT_ROWS, D), F32),),
        in_specs=[vmem] * 7 + [hbm] * 6,
        out_specs=[vmem] * 5,
        scratch_shapes=scratch(),
        compiler_params=pltpu.CompilerParams(
            collective_id=0, has_side_effects=True, vmem_limit_bytes=60 * 1024 * 1024),
    )(
        node_state, senders.reshape(1, E), receivers.reshape(1, E), lists,
        edge_gain, node_gain, node_cot,
        edge_state, edge_in[0], edge_out[0], node_in[0], node_out[0], edge_cot,
    )
    return pl.pallas_call(
        hand_over,
        out_shape=states + (jax.ShapeDtypeStruct((1, OUT_ROWS * D), F32),),
        in_specs=[hbm] * 4 + [vmem],
        out_specs=[hbm] * 4 + [vmem],
        scratch_shapes=[pltpu.SemaphoreType.DMA((4,))],
    )(*results)


def solution(mesh):
    both = P(("dom", "esplit"), None)
    in_specs = (
        both, both, P(("dom", "esplit")), P(("dom", "esplit")), P("dom", None, None),
        P(), P(), P(), P(), P(), P(), both, both,
    )
    out_specs = (both, both, both, both, P(None, ("dom", "esplit")))
    return jax.shard_map(body, mesh=mesh, in_specs=in_specs, out_specs=out_specs, check_vma=False)
```

```python
import functools

import jax
import jax.numpy as jnp
from jax import lax
from jax.experimental import pallas as pl
from jax.experimental.pallas import tpu as pltpu
from jax.sharding import PartitionSpec as P

EPSILON = 1e-05
BF = jnp.bfloat16
F32 = jnp.float32
MESH = pl.DeviceIdType.MESH

NZ = 8
NY = 4
NX = 4
DOM = NY * NZ
S = NX * 2
D = 512
N = 128
PN = N * S
E = 512
GH = 16
SLAB = DOM // S * GH
NJ = DOM // S
HALF = D // 2
NMAT = 7
OUT_ROWS = 14


def dot(a, b):
    return lax.dot_general(a, b, (((1,), (0,)), ((), ())), preferred_element_type=F32)


def dot_nt(a, b):
    return lax.dot_general(a, b, (((1,), (1,)), ((), ())), preferred_element_type=F32)


def dot_tn(a, b):
    return lax.dot_general(a, b, (((0,), (0,)), ((), ())), preferred_element_type=F32)


def normalize(values, gain):
    average = jnp.mean(values, axis=-1, keepdims=True)
    centered = values - average
    inv_scale = lax.rsqrt(jnp.mean(centered * centered, axis=-1, keepdims=True) + EPSILON)
    return gain * centered * inv_scale


def normalize_back(values, gain, upstream):
    average = jnp.mean(values, axis=-1, keepdims=True)
    centered = values - average
    inv_scale = lax.rsqrt(jnp.mean(centered * centered, axis=-1, keepdims=True) + EPSILON)
    scaled = centered * inv_scale
    grad_scaled = upstream * gain
    first = jnp.mean(grad_scaled, axis=-1, keepdims=True)
    second = jnp.mean(grad_scaled * scaled, axis=-1, keepdims=True)
    return inv_scale * (grad_scaled - first - scaled * second)


def swish(values):
    return values * jax.nn.sigmoid(values)


def swish_slope(values):
    sigma = jax.nn.sigmoid(values)
    return sigma * (1.0 + values * (1.0 - sigma))


def rows_loop(total, step, fn):
    def one(i, carry):
        fn(pl.multiple_of(i * step, step))
        return carry

    lax.fori_loop(0, total // step, one, 0)


class Sems:
    def __init__(self, ref):
        self.ref = ref
        self.used = 0

    def take(self, count):
        base = self.used
        self.used += count
        return lambda i: self.ref.at[base + i]


N_SEM = 280


def kernel(
    nodes_in, snd_row, rcv_row, snd_lists, egain, ngain, ncot,
    edges_hbm, ein_hbm, eout_hbm, nin_hbm, nout_hbm, ecot_hbm,
    nodes_out, edges_out, ngrad, egrad, wout,
    edges, ein, eout, nin, nout, ecot,
    ps, pr, pst, prt, tbl, sent_acc, sent, recv, pre, msg, hid,
    gsend, agg_keep, aggs_send, aggs_recv, agg_bufs,
    agg, npre, nhid, gdirect, dnpre, dnmsg, dagg_own, dagg,
    gedge, dmsg, dpre, dsent, drecv,
    gg_keep, gg_ssend, gg_srecv, gg_bufs, a2_send, retg,
    own_keep, own_ssend, own_srecv, own_bufs,
    fn_ssend, fn_srecv, fn_own, fn_ybufs, fn_ysum, fn_xbufs, fn_zsend, fn_zrecv,
    fe_ssend, fe_srecv, fe_own, fe_ybufs, fe_ysum, fe_xbufs, fe_zsend, fe_zrecv,
    fz_total, fin, rows_in,
    sem_ref,
):
    d = lax.axis_index("dom")
    s = lax.axis_index("esplit")
    y = d // NZ
    z = d % NZ
    x = s // 2
    c = s % 2
    lin = d * S + s
    sib = s + 1 - 2 * c
    t_mine = (s - d + DOM) % S
    sems = Sems(sem_ref)
    pending = []

    def remote(src, dst, send_sem, recv_sem, dom, split):
        return pltpu.make_async_remote_copy(
            src_ref=src, dst_ref=dst, send_sem=send_sem, recv_sem=recv_sem,
            device_id=(dom, split), device_id_type=MESH,
        )

    bar = pltpu.get_barrier_semaphore()

    def greet(dom, split):
        pl.semaphore_signal(bar, inc=1, device_id=(dom, split), device_id_type=MESH)

    for k in range(1, S):
        greet(d, (s + k) % S)
    for k in range(1, NY):
        greet((y + k) % NY * NZ + z, s)
    for k in range(1, NZ):
        greet(y * NZ + (z + k) % NZ, s)
    for j in range(NJ):
        pl.when(t_mine + S * j != d)(functools.partial(greet, t_mine + S * j, s))
    first_row = OUT_ROWS * lin
    b_first = first_row // 16
    b_last = (first_row + OUT_ROWS - 1) // 16

    def holder(b, half):
        return b % DOM, (b // DOM) % NX * 2 + half

    def from_other(slot, half):
        dom, split = holder(b_first + slot, half)
        here = dom * S + split != lin
        return here if slot == 0 else here & (b_last != b_first)

    for slot in range(2):
        for half in range(2):
            dom, split = holder(b_first + slot, half)
            pl.when(from_other(slot, half))(functools.partial(greet, dom, split))

    lsem = sems.take(6)
    loads = [
        pltpu.make_async_copy(a, b, lsem(i))
        for i, (a, b) in enumerate(
            ((edges_hbm, edges), (ein_hbm, ein), (eout_hbm, eout), (nin_hbm, nin),
             (nout_hbm, nout), (ecot_hbm, ecot)))
    ]
    for load in loads:
        load.start()

    tbl[pl.ds(pl.multiple_of(s * N, N), N), :] = nodes_in[...]

    def owner(group, i):
        b = DOM * (x + NX * group) + d
        to = (16 * b) // OUT_ROWS + i
        valid = to <= (16 * b + 15) // OUT_ROWS
        if group:
            valid = valid & (x < NMAT - NX)
        return to, b - (OUT_ROWS * to) // 16, valid

    arrivals = (S - 1) + (NY - 1) + (NZ - 1)
    for j in range(NJ):
        arrivals = arrivals + jnp.where(t_mine + S * j != d, 1, 0)
    for group in range(2):
        for i in range(3):
            to, _, valid = owner(group, i)
            arrivals = arrivals + jnp.where(valid & (to != lin), 1, 0)
    pl.semaphore_wait(bar, arrivals)

    def on_x(dx):
        return (x + dx + NX) % NX * 2 + c

    class Gather:
        def __init__(self, buf, offset, rows):
            self.buf, self.offset, self.rows, self.half = buf, offset, rows, rows // 2
            self.ss, self.rs = sems.take(10), sems.take(10)

        def part(self, split, half):
            start = pl.multiple_of(self.offset(split), self.rows)
            if half is None:
                return self.buf.at[pl.ds(start, self.rows), :]
            return self.buf.at[pl.ds(start + half * self.half, self.half), :]

        def copy(self, k, origin, half, split, src=None):
            there = self.part(origin, half)
            if src is None:
                here = there
            elif half is None:
                here = src
            else:
                here = src.at[pl.ds(half * self.half, self.half), :]
            return remote(here, there, self.ss(k), self.rs(k), d, split)

        def send(self, k, origin, half, split, src=None):
            cp = self.copy(k, origin, half, split, src)
            cp.start()
            pending.append(cp)

        def arrived(self, k, origin, half):
            self.copy(k, origin, half, sib).wait_recv()

        def start(self, src):
            self.send(0, s, 0, on_x(1), src)
            self.send(2, s, 1, on_x(-1), src)
            self.send(1, s, 1, on_x(1), src)
            self.send(3, s, 0, on_x(-1), src)
            self.send(4, s, None, sib, src)

        def relay(self):
            self.arrived(0, on_x(-1), 0)
            self.send(5, on_x(-1), 0, on_x(1))
            self.arrived(2, on_x(1), 1)
            self.send(6, on_x(1), 1, on_x(-1))
            self.arrived(1, on_x(-1), 1)
            self.send(7, on_x(-1), None, sib)
            self.arrived(3, on_x(1), 0)
            self.send(8, on_x(1), None, sib)

        def finish(self):
            self.arrived(5, on_x(2), 0)
            self.arrived(6, on_x(2), 1)
            self.send(9, on_x(2), None, sib)
            self.arrived(4, sib, None)
            for k, dx in ((7, -1), (8, 1), (9, 2)):
                self.arrived(k, on_x(dx) + 1 - 2 * c, None)

    class Ring:
        def __init__(self, get, bufs, right, left):
            self.get, self.bufs, self.right, self.left = get, bufs, right, left
            self.ss, self.rs = sems.take(6), sems.take(6)

        def copy(self, k):
            source, landing, to = (
                (0, 2, self.right), (1, 3, self.left), (4, 8, self.right), (5, 9, self.right),
                (6, 10, self.left), (7, 11, self.left))[k]
            return remote(
                self.bufs.at[source], self.bufs.at[landing], self.ss(k), self.rs(k), *to)

        def send(self, k, value):
            self.bufs[(0, 1, 4, 5, 6, 7)[k]] = value.astype(BF)
            cp = self.copy(k)
            cp.start()
            pending.append(cp)

        def far(self):
            self.send(0, self.get(2, 0))
            self.send(1, self.get(2, 1))

        def to_right(self):
            self.send(3, self.get(1, 1))

        def to_left(self):
            self.send(4, self.get(3, 0))

        def start(self):
            self.far()
            self.to_right()
            self.to_left()

        def relay(self):
            self.copy(0).wait_recv()
            self.send(2, self.get(1, 0) + self.bufs[2].astype(F32))
            self.copy(1).wait_recv()
            self.send(5, self.get(3, 1) + self.bufs[3].astype(F32))

        def wait(self):
            for k in (3, 4, 2, 5):
                self.copy(k).wait_recv()

        def result(self, half):
            return (self.get(0, half) + self.bufs[8 + half].astype(F32)
                    + self.bufs[10 + half].astype(F32))

    class Scatter:
        def __init__(self, compute, keep, ssend, srecv, bufs):
            self.compute, self.keep, self.ssend, self.srecv = compute, keep, ssend, srecv
            self.s1, self.r1 = sems.take(4), sems.take(4)
            half = keep.shape[1] // 2
            self.ring = Ring(
                lambda k, h: keep[k, h * half:(h + 1) * half, :], bufs, (d, on_x(1)), (d, on_x(-1)))

        def to_sib(self, dx):
            return remote(self.ssend.at[dx], self.srecv.at[dx], self.s1(dx), self.r1(dx), d, sib)

        def start(self):
            for dx in (2, 1, 3, 0):
                self.ssend[dx] = self.compute((x + dx) % NX * 2 + 1 - c).astype(BF)
                cp = self.to_sib(dx)
                cp.start()
                pending.append(cp)

        def fill(self, dx):
            mine = self.compute((x + dx) % NX * 2 + c)
            self.to_sib(dx).wait_recv()
            self.keep[dx] = mine + self.srecv[dx].astype(F32)

        def middle(self):
            self.fill(2)
            self.ring.far()
            self.fill(1)
            self.ring.to_right()
            self.fill(3)
            self.ring.to_left()
            self.fill(0)

        def relay(self):
            self.ring.relay()

        def finish(self):
            self.ring.wait()
            return jnp.concatenate([self.ring.result(0), self.ring.result(1)], axis=0)

    class Swap:
        def __init__(self, src, dst):
            self.src, self.dst = src, dst
            self.ss, self.rs = sems.take(NJ), sems.take(NJ)

        def start(self):
            for j in range(NJ):
                peer = t_mine + S * j
                land = pl.multiple_of((d % S) * SLAB + (d // S) * GH, GH)
                cp = remote(
                    self.src.at[pl.ds(j * GH, GH), :], self.dst.at[pl.ds(land, GH), :],
                    self.ss(j), self.rs(d // S), peer, s)
                pl.when(peer != d)(cp.start)

                @pl.when(peer == d)
                def _():
                    self.dst[pl.ds(land, GH), :] = self.src[pl.ds(j * GH, GH), :]

        def finish(self):
            for j in range(NJ):
                peer = t_mine + S * j
                land = pl.multiple_of(t_mine * SLAB + j * GH, GH)
                cp = remote(
                    self.src.at[pl.ds(j * GH, GH), :], self.dst.at[pl.ds(land, GH), :],
                    self.ss(j), self.rs(j), peer, s)

                @pl.when(peer != d)
                def _():
                    cp.wait_recv()
                    cp.wait_send()

    gather_nodes = Gather(tbl, lambda q: q * N, N)
    gather_nodes.start(nodes_in)

    def permuted(values):
        ghost = values - PN
        part = ghost // GH
        place = PN + (part % S) * SLAB + (part // S) * GH + ghost % GH
        return jnp.where(values >= PN, place, values)

    def column(row):
        size = row.shape[1]
        hit = lax.broadcasted_iota(jnp.int32, (size, size), 0) == lax.broadcasted_iota(
            jnp.int32, (size, size), 1)
        return jnp.sum(jnp.where(hit, row.astype(F32), 0.0), axis=1, keepdims=True).astype(jnp.int32)

    def hot(mask):
        return jnp.where(mask, 1.0, 0.0).astype(BF)

    send_r = permuted(snd_row[...])
    recv_r = rcv_row[...]
    send_c = column(send_r)
    recv_c = column(recv_r)

    def build_t(r0):
        ids = lax.broadcasted_iota(jnp.int32, (256, E), 0) + r0
        pst[pl.ds(r0, 256), :] = hot(ids == send_r)

    rows_loop(PN + S * SLAB, 256, build_t)

    def build_rt(r0):
        ids = lax.broadcasted_iota(jnp.int32, (256, E), 0) + r0
        prt[pl.ds(r0, 256), :] = hot(ids == recv_r)

    rows_loop(PN, 256, build_rt)
    for c0 in range(0, PN + S * SLAB, 256):
        ids = lax.broadcasted_iota(jnp.int32, (E, 256), 1) + c0
        ps[:, c0:c0 + 256] = hot(ids == send_c)
        if c0 < PN:
            pr[:, c0:c0 + 256] = hot(ids == recv_c)

    lists = snd_lists[0]
    slot = lax.broadcasted_iota(jnp.int32, (S * SLAB, DOM), 0)
    part = slot // SLAB + (slot // GH) % NJ * S
    rows = hot(lax.broadcasted_iota(jnp.int32, (S * SLAB, DOM), 1) == part)
    high = dot(rows, (lists // 32).astype(F32).astype(BF))
    low = dot(rows, (lists % 32).astype(F32).astype(BF))
    slot = lax.broadcasted_iota(jnp.int32, (S * SLAB, GH), 0)
    here = lax.broadcasted_iota(jnp.int32, (S * SLAB, GH), 1) == slot % GH
    lists_c = jnp.sum(
        jnp.where(here, high * 32.0 + low, 0.0), axis=1, keepdims=True).astype(jnp.int32)

    loads[0].wait()
    loads[1].wait()

    def edge_part(r0):
        pre[pl.ds(r0, 256), :] = dot(edges[pl.ds(r0, 256), :], ein[0])

    rows_loop(E, 256, edge_part)

    gather_nodes.relay()
    gather_nodes.finish()

    hit = jnp.zeros((SLAB, 1), jnp.int32)
    for t in range(S):
        hit = jnp.where(t_mine == t, lists_c[t * SLAB:(t + 1) * SLAB, :], hit)
    pick = hot(lax.broadcasted_iota(jnp.int32, (SLAB, PN), 1) == hit)
    gsend[...] = dot(pick, tbl[:PN, :]).astype(BF)
    ghosts = tbl.at[pl.ds(PN, S * SLAB), :]
    swap_ghost = Swap(gsend, ghosts)
    swap_ghost.start()

    def gather_recv(r0):
        rows = pl.ds(r0, 256)
        got = dot(pr[rows, :], tbl[:PN, :]).astype(BF)
        recv[rows, :] = got
        pre[rows, :] = pre[rows, :] + dot(got, ein[2])

    rows_loop(E, 256, gather_recv)
    swap_ghost.finish()
    gather_ghost = Gather(ghosts, lambda q: ((q - d + DOM) % S) * SLAB, SLAB)
    gather_ghost.start(ghosts.at[pl.ds(pl.multiple_of(t_mine * SLAB, SLAB), SLAB), :])

    def gather_sent(r0):
        rows = pl.ds(r0, 256)
        sent_acc[rows, :] = dot(ps[rows, :PN], tbl[:PN, :])

    rows_loop(E, 256, gather_sent)
    gather_ghost.relay()
    gather_ghost.finish()

    loads[2].wait()
    edge_gain = egain[...]

    def edge_forward(r0):
        rows = pl.ds(r0, 256)
        got = (sent_acc[rows, :] + dot(ps[rows, PN:], tbl[PN:, :])).astype(BF)
        sent[rows, :] = got
        act = pre[rows, :] + dot(got, ein[1])
        pre[rows, :] = act
        hidden = swish(act).astype(BF)
        hid[rows, :] = hidden
        message = dot(hidden, eout[...])
        msg[rows, :] = message
        edges_out[rows, :] = (edges[rows, :].astype(F32) + normalize(message, edge_gain)).astype(BF)

    rows_loop(E, 256, edge_forward)

    def agg_block(q):
        return dot(prt[pl.ds(pl.multiple_of(q * N, N), N), :], edges_out[...])

    reduce_agg = Scatter(agg_block, agg_keep, aggs_send, aggs_recv, agg_bufs)
    reduce_agg.start()
    reduce_agg.middle()
    loads[3].wait()
    loads[4].wait()
    loads[5].wait()
    reduce_agg.relay()
    npre[...] = dot(nodes_in[...], nin[0])
    agg[...] = reduce_agg.finish().astype(BF)

    node_gain = ngain[...]
    act = npre[...] + dot(agg[...], nin[1])
    hidden = swish(act).astype(BF)
    nhid[...] = hidden
    message = dot(hidden, nout[...])
    nodes_out[...] = (nodes_in[...].astype(F32) + normalize(message, node_gain)).astype(BF)
    upstream = ncot[...].astype(F32)
    grad_message = normalize_back(message, node_gain, upstream).astype(BF)
    dnmsg[...] = grad_message
    grad_pre = (dot_nt(grad_message, nout[...]) * swish_slope(act)).astype(BF)
    dnpre[...] = grad_pre
    dagg_own[...] = dot_nt(grad_pre, nin[1]).astype(BF)
    dagg[pl.ds(pl.multiple_of(s * N, N), N), :] = dagg_own[...]

    gather_dagg = Gather(dagg, lambda q: q * N, N)
    gather_dagg.start(dagg_own)
    gdirect[...] = upstream + dot_nt(grad_pre, nin[0])

    mine_cols = pl.ds(pl.multiple_of(c * HALF, HALF), HALF)
    sib_cols = pl.ds(pl.multiple_of((1 - c) * HALF, HALF), HALF)

    class Weights:
        def __init__(self, base, pairs, ssend, srecv, own, ybufs, ysum, xbufs, zsend, zrecv):
            self.base, self.pairs, self.count = base, pairs, len(pairs)
            self.ssend, self.srecv, self.own, self.ysum = ssend, srecv, own, ysum
            self.zsend, self.zrecv = zsend, zrecv
            self.s0, self.r0 = sems.take(self.count), sems.take(self.count)
            self.sz, self.rz = sems.take(NZ - 1), sems.take(NZ - 1)

            def y_term(k, half):
                rows = pl.ds(pl.multiple_of((y + k) % NY * 128 + half * 64, 64), 64)
                return own[:, rows, :] + srecv[:, rows, :].astype(F32)

            def x_term(k, half):
                which = jnp.minimum((x + k) % NX, self.count - 1)
                return ysum[which, half * 64:(half + 1) * 64, :]

            self.y = Ring(
                y_term, ybufs, ((y + 1) % NY * NZ + z, s), ((y + NY - 1) % NY * NZ + z, s))
            self.x = Ring(x_term, xbufs, (d, on_x(1)), (d, on_x(-1)))

        def sib_copy(self, i):
            return remote(self.ssend.at[i], self.srecv.at[i], self.s0(i), self.r0(i), d, sib)

        def z_copy(self, k):
            return remote(
                self.zsend.at[k], self.zrecv.at[k - 1], self.sz(k - 1), self.rz(k - 1),
                y * NZ + (z + k) % NZ, s)

        def products(self, i):
            left, right = self.pairs[i]
            self.ssend[i] = dot_tn(left[...], right[:, sib_cols]).astype(BF)
            cp = self.sib_copy(i)
            cp.start()
            pending.append(cp)
            self.own[i] = dot_tn(left[...], right[:, mine_cols])

        def to_y(self):
            for i in range(self.count):
                self.sib_copy(i).wait_recv()
            self.y.start()

        def to_x(self):
            self.y.wait()
            for half in range(2):
                self.ysum[:, half * 64:(half + 1) * 64, :] = self.y.result(half)
            self.x.start()

        def to_z(self, total):
            self.x.wait()
            for half in range(2):
                total[half * 64:(half + 1) * 64, :] = self.x.result(half)
            for k in (4, 3, 5, 2, 6, 1, 7, 0):
                rows = pl.ds(pl.multiple_of((z + k) % NZ * 16, 16), 16)
                self.zsend[k] = total[rows, :].astype(BF)
                if k:
                    cp = self.z_copy(k)
                    cp.start()
                    pending.append(cp)

        def finish(self, out):
            for k in range(1, NZ):
                self.z_copy(k).wait_recv()
            total = self.zsend[0].astype(F32)
            for k in range(NZ - 1):
                total = total + self.zrecv[k].astype(F32)
            out[...] = total

    node_weights = Weights(
        4, ((nodes_in, dnpre), (agg, dnpre), (nhid, dnmsg)),
        fn_ssend, fn_srecv, fn_own, fn_ybufs, fn_ysum, fn_xbufs, fn_zsend, fn_zrecv)
    edge_weights = Weights(
        0, ((edges, dpre), (sent, dpre), (recv, dpre), (hid, dmsg)),
        fe_ssend, fe_srecv, fe_own, fe_ybufs, fe_ysum, fe_xbufs, fe_zsend, fe_zrecv)

    gather_dagg.relay()
    for i in range(3):
        node_weights.products(i)
    gather_dagg.finish()
    node_weights.to_y()

    def edge_backward(r0):
        rows = pl.ds(r0, 256)
        up = ecot[rows, :].astype(F32) + dot(pr[rows, :], dagg[...])
        gedge[rows, :] = up
        grad_msg = normalize_back(msg[rows, :], edge_gain, up).astype(BF)
        dmsg[rows, :] = grad_msg
        grad = (dot_nt(grad_msg, eout[...]) * swish_slope(pre[rows, :])).astype(BF)
        dpre[rows, :] = grad
        dsent[rows, :] = dot_nt(grad, ein[1]).astype(BF)

    rows_loop(E, 256, edge_backward)

    def ghost_block(q):
        place = PN + ((q - d + DOM) % S) * SLAB
        return dot(pst[pl.ds(pl.multiple_of(place, SLAB), SLAB), :], dsent[...])

    for i in (3, 0, 1, 2):
        edge_weights.products(i)
    node_weights.y.relay()
    reduce_ghost = Scatter(ghost_block, gg_keep, gg_ssend, gg_srecv, gg_bufs)
    reduce_ghost.start()
    edge_weights.to_y()
    reduce_ghost.middle()
    node_weights.to_x()

    def recv_grad(r0):
        rows = pl.ds(r0, 256)
        drecv[rows, :] = dot_nt(dpre[rows, :], ein[2]).astype(BF)

    rows_loop(E, 256, recv_grad)
    reduce_ghost.relay()

    def own_block(q):
        rows = pl.ds(pl.multiple_of(q * N, N), N)
        return dot(pst[rows, :], dsent[...]) + dot(prt[rows, :], drecv[...])

    reduce_own = Scatter(own_block, own_keep, own_ssend, own_srecv, own_bufs)
    reduce_own.start()
    edge_weights.y.relay()
    a2_send[...] = reduce_ghost.finish().astype(BF)
    swap_back = Swap(a2_send, retg)
    swap_back.start()
    reduce_own.middle()
    node_weights.x.relay()
    swap_back.finish()
    gather_back = Gather(retg, lambda q: ((q - d + DOM) % S) * SLAB, SLAB)
    gather_back.start(retg.at[pl.ds(pl.multiple_of(t_mine * SLAB, SLAB), SLAB), :])
    reduce_own.relay()
    edge_weights.to_x()
    gather_back.relay()
    node_weights.to_z(fz_total)

    def edge_grad(r0):
        rows = pl.ds(r0, 256)
        egrad[rows, :] = (gedge[rows, :] + dot_nt(dpre[rows, :], ein[0])).astype(BF)

    rows_loop(E, 256, edge_grad)
    edge_weights.x.relay()
    gather_back.finish()
    place = hot(lax.broadcasted_iota(jnp.int32, (S * SLAB, N), 1) + s * N == lists_c)
    direct = gdirect[...] + dot_tn(place, retg[...])
    edge_weights.to_z(fz_total)
    ngrad[...] = (direct + reduce_own.finish()).astype(BF)

    s_fin, r_fin = sems.take(6), sems.take(4)

    def fin_copy(group, i, slot, half):
        to = jnp.minimum(owner(group, i)[0], DOM * S - 1)
        return remote(
            fin.at[group], rows_in.at[slot, half], s_fin(3 * group + i), r_fin(2 * slot + half),
            to // S, to % S)

    def hand_out(group):
        for i in range(3):
            to, at, valid = owner(group, i)
            for slot in range(2):
                for half in range(2):
                    here = valid & (at == slot) & (c == half)
                    pl.when(here & (to != lin))(fin_copy(group, i, slot, half).start)

                    @pl.when(here & (to == lin))
                    def _():
                        rows_in[slot, half] = fin[group]

    node_weights.finish(fin.at[1])
    hand_out(1)
    edge_weights.finish(fin.at[0])
    hand_out(0)
    for slot in range(2):
        for half in range(2):
            pl.when(from_other(slot, half))(fin_copy(0, 0, slot, half).wait_recv)
    shift = first_row % 16
    for choice in range(0, 16, 2):
        @pl.when(shift == choice)
        def _():
            split = min(16 - choice, OUT_ROWS)
            for half in range(2):
                cols = slice(half * HALF, (half + 1) * HALF)
                wout[:split, cols] = rows_in[0, half, choice:choice + split, :]
                if split < OUT_ROWS:
                    wout[split:, cols] = rows_in[1, half, :OUT_ROWS - split, :]

    for cp in pending:
        cp.wait_send()
    for group in range(2):
        for i in range(3):
            to, _, valid = owner(group, i)
            pl.when(valid & (to != lin))(fin_copy(group, i, 0, 0).wait_send)


def scratch():
    def bf(*shape):
        return pltpu.VMEM(shape, BF)

    def f32(*shape):
        return pltpu.VMEM(shape, F32)

    T = PN + S * SLAB

    def scatter(rows):
        return [f32(NX, rows, D), bf(NX, rows, D), bf(NX, rows, D), bf(12, rows // 2, D)]

    def weights(count):
        return [
            bf(count, D, HALF), bf(count, D, HALF), f32(count, D, HALF),
            bf(12, count, 64, HALF), f32(count, 128, HALF), bf(12, 64, HALF),
            bf(NZ, 16, HALF), bf(NZ - 1, 16, HALF),
        ]

    return [
        bf(E, D), bf(3, D, D), bf(D, D), bf(2, D, D), bf(D, D), bf(E, D),
        bf(E, T), bf(E, PN), bf(T, E), bf(PN, E), bf(T, D), f32(E, D), bf(E, D), bf(E, D),
        f32(E, D), f32(E, D), bf(E, D),
        bf(SLAB, D), *scatter(N),
        bf(N, D), f32(N, D), bf(N, D), f32(N, D), bf(N, D), bf(N, D), bf(N, D), bf(PN, D),
        f32(E, D), bf(E, D), bf(E, D), bf(E, D), bf(E, D),
        *scatter(SLAB), bf(SLAB, D), bf(S * SLAB, D), *scatter(N),
        *weights(3), *weights(4),
        f32(128, HALF), f32(2, 16, HALF), f32(2, 2, 16, HALF),
        pltpu.SemaphoreType.DMA((N_SEM,)),
    ]


def hand_over(a0, a1, a2, a3, w_in, b0, b1, b2, b3, w_out):
    for src, dst in ((a0, b0), (a1, b1), (a2, b2), (a3, b3)):
        dst[...] = src[...]
    for i in range(OUT_ROWS):
        w_out[:, i * D:(i + 1) * D] = w_in[i:i + 1, :]


def body(
    node_state, edge_state, senders, receivers, send_rows, edge_in, edge_out, edge_gain,
    node_in, node_out, node_gain, node_cot, edge_cot,
):
    vmem = pl.BlockSpec(memory_space=pltpu.VMEM)
    hbm = pl.BlockSpec(memory_space=pl.ANY)
    states = (
        jax.ShapeDtypeStruct((N, D), BF),
        jax.ShapeDtypeStruct((E, D), BF),
        jax.ShapeDtypeStruct((N, D), BF),
        jax.ShapeDtypeStruct((E, D), BF),
    )
    results = pl.pallas_call(
        kernel,
        out_shape=states + (jax.ShapeDtypeStruct((OUT_ROWS, D), F32),),
        in_specs=[vmem] * 7 + [hbm] * 6,
        out_specs=[vmem] * 5,
        scratch_shapes=scratch(),
        compiler_params=pltpu.CompilerParams(
            collective_id=0, has_side_effects=True, vmem_limit_bytes=60 * 1024 * 1024),
    )(
        node_state, senders.reshape(1, E), receivers.reshape(1, E), send_rows,
        edge_gain, node_gain, node_cot,
        edge_state, edge_in[0], edge_out[0], node_in[0], node_out[0], edge_cot,
    )
    return pl.pallas_call(
        hand_over,
        out_shape=states + (jax.ShapeDtypeStruct((1, OUT_ROWS * D), F32),),
        in_specs=[vmem] * 5,
        out_specs=[vmem] * 5,
    )(*results)


def solution(mesh):
    both = P(("dom", "esplit"), None)
    in_specs = (
        both, both, P(("dom", "esplit")), P(("dom", "esplit")), P("dom", None, None),
        P(), P(), P(), P(), P(), P(), both, both,
    )
    out_specs = (both, both, both, both, P(None, ("dom", "esplit")))
    return jax.shard_map(body, mesh=mesh, in_specs=in_specs, out_specs=out_specs, check_vma=False)
```

```python
import functools

import jax
import jax.numpy as jnp
from jax import lax
from jax.experimental import pallas as pl
from jax.experimental.pallas import tpu as pltpu
from jax.sharding import PartitionSpec as P

EPSILON = 1e-05
BF = jnp.bfloat16
F32 = jnp.float32
MESH = pl.DeviceIdType.MESH

NZ = 8
NY = 4
NX = 4
DOM = NY * NZ
S = NX * 2
D = 512
N = 128
PN = N * S
E = 512
GH = 16
SLAB = DOM // S * GH
NJ = DOM // S
HALF = D // 2
NMAT = 7
OUT_ROWS = 14


def dot(a, b):
    return lax.dot_general(a, b, (((1,), (0,)), ((), ())), preferred_element_type=F32)


def dot_nt(a, b):
    return lax.dot_general(a, b, (((1,), (1,)), ((), ())), preferred_element_type=F32)


def dot_tn(a, b):
    return lax.dot_general(a, b, (((0,), (0,)), ((), ())), preferred_element_type=F32)


def normalize(values, gain):
    average = jnp.mean(values, axis=-1, keepdims=True)
    centered = values - average
    inv_scale = lax.rsqrt(jnp.mean(centered * centered, axis=-1, keepdims=True) + EPSILON)
    return gain * centered * inv_scale


def normalize_back(values, gain, upstream):
    average = jnp.mean(values, axis=-1, keepdims=True)
    centered = values - average
    inv_scale = lax.rsqrt(jnp.mean(centered * centered, axis=-1, keepdims=True) + EPSILON)
    scaled = centered * inv_scale
    grad_scaled = upstream * gain
    first = jnp.mean(grad_scaled, axis=-1, keepdims=True)
    second = jnp.mean(grad_scaled * scaled, axis=-1, keepdims=True)
    return inv_scale * (grad_scaled - first - scaled * second)


def swish(values):
    return values * jax.nn.sigmoid(values)


def swish_slope(values):
    sigma = jax.nn.sigmoid(values)
    return sigma * (1.0 + values * (1.0 - sigma))


def rows_loop(total, step, fn):
    def one(i, carry):
        fn(pl.multiple_of(i * step, step))
        return carry

    lax.fori_loop(0, total // step, one, 0)


class Sems:
    def __init__(self, ref):
        self.ref = ref
        self.used = 0

    def take(self, count):
        base = self.used
        self.used += count
        return lambda i: self.ref.at[base + i]


N_SEM = 280


def kernel(
    nodes_in, snd_row, rcv_row, snd_lists, egain, ngain, ncot,
    edges_hbm, ein_hbm, eout_hbm, nin_hbm, nout_hbm, ecot_hbm,
    nodes_out, edges_out, ngrad, egrad, wout,
    edges, ein, eout, nin, nout, ecot,
    ps, pr, pst, prt, tbl, sent_acc, sent, recv, pre, msg, hid,
    gsend, aggs_send, aggs_recv, aggx_send, aggx_recv, agg_own,
    agg, npre, nhid, gdirect, dnpre, dnmsg, dagg_own, dagg,
    gedge, dmsg, dpre, dsent, drecv,
    gg_ssend, gg_srecv, gg_xsend, gg_xrecv, gg_own, a2_send, retg,
    own_ssend, own_srecv, own_xsend, own_xrecv, own_own,
    fn_ssend, fn_srecv, fn_own, fn_ysend, fn_yrecv, fn_ysum, fn_xsend, fn_xrecv, fn_xsum, fn_zsend, fn_zrecv,
    fe_ssend, fe_srecv, fe_own, fe_ysend, fe_yrecv, fe_ysum, fe_xsend, fe_xrecv, fe_xsum, fe_zsend, fe_zrecv,
    fo_ssend, fo_srecv, fo_own, fo_zsend, fo_zrecv, fo_zsum, fo_ysend, fo_yrecv, fo_xsend, fo_xrecv,
    fin, rows_in,
    sem_ref,
):
    d = lax.axis_index("dom")
    s = lax.axis_index("esplit")
    y = d // NZ
    z = d % NZ
    x = s // 2
    c = s % 2
    lin = d * S + s
    sib = s + 1 - 2 * c
    t_mine = (s - d + DOM) % S
    sems = Sems(sem_ref)
    pending = []

    def remote(src, dst, send_sem, recv_sem, dom, split):
        return pltpu.make_async_remote_copy(
            src_ref=src, dst_ref=dst, send_sem=send_sem, recv_sem=recv_sem,
            device_id=(dom, split), device_id_type=MESH,
        )

    bar = pltpu.get_barrier_semaphore()

    def greet(dom, split):
        pl.semaphore_signal(bar, inc=1, device_id=(dom, split), device_id_type=MESH)

    for k in range(1, S):
        greet(d, (s + k) % S)
    for k in range(1, NY):
        greet((y + k) % NY * NZ + z, s)
    for k in range(1, NZ):
        greet(y * NZ + (z + k) % NZ, s)
    for j in range(NJ):
        pl.when(t_mine + S * j != d)(functools.partial(greet, t_mine + S * j, s))
    first_row = OUT_ROWS * lin
    b_first = first_row // 16
    b_last = (first_row + OUT_ROWS - 1) // 16

    def holder(b, half):
        r = b % DOM
        return jnp.where(b // DOM == 3, r % NY * NZ + r // NY, r), (b // DOM) % NX * 2 + half

    def from_other(slot, half):
        dom, split = holder(b_first + slot, half)
        here = dom * S + split != lin
        return here if slot == 0 else here & (b_last != b_first)

    for slot in range(2):
        for half in range(2):
            dom, split = holder(b_first + slot, half)
            pl.when(from_other(slot, half))(functools.partial(greet, dom, split))

    lsem = sems.take(6)
    loads = [
        pltpu.make_async_copy(a, b, lsem(i))
        for i, (a, b) in enumerate(
            ((edges_hbm, edges), (ein_hbm, ein), (eout_hbm, eout), (nin_hbm, nin),
             (nout_hbm, nout), (ecot_hbm, ecot)))
    ]
    for load in loads:
        load.start()

    tbl[pl.ds(pl.multiple_of(s * N, N), N), :] = nodes_in[...]

    def owner(group, i):
        b = DOM * (x + NX * group) + (d if group else jnp.where(x == 3, z * NY + y, d))
        to = (16 * b) // OUT_ROWS + i
        valid = to <= (16 * b + 15) // OUT_ROWS
        if group:
            valid = valid & (x < NMAT - NX)
        return to, b - (OUT_ROWS * to) // 16, valid

    arrivals = (S - 1) + (NY - 1) + (NZ - 1)
    for j in range(NJ):
        arrivals = arrivals + jnp.where(t_mine + S * j != d, 1, 0)
    for group in range(2):
        for i in range(3):
            to, _, valid = owner(group, i)
            arrivals = arrivals + jnp.where(valid & (to != lin), 1, 0)
    pl.semaphore_wait(bar, arrivals)

    def on_x(dx):
        return (x + dx + NX) % NX * 2 + c

    class Gather:
        def __init__(self, buf, offset, rows):
            self.buf, self.offset, self.rows = buf, offset, rows
            self.ss, self.rs = sems.take(7), sems.take(7)

        def copy(self, k, origin, split, src=None):
            there = self.buf.at[pl.ds(pl.multiple_of(self.offset(origin), self.rows), self.rows), :]
            here = there if src is None else src
            return remote(here, there, self.ss(k), self.rs(k), d, split)

        def send(self, k, origin, split, src=None):
            cp = self.copy(k, origin, split, src)
            cp.start()
            pending.append(cp)

        def start(self, src):
            for dx in (2, 1, 3):
                self.send(dx - 1, s, on_x(dx), src)
            self.send(3, s, sib, src)

        def forward(self, dx):
            origin = on_x(-dx)
            self.copy(dx - 1, origin, sib).wait_recv()
            self.send(3 + dx, origin, sib)

        def relay(self):
            self.forward(1)
            self.forward(3)

        def finish(self):
            self.forward(2)
            self.copy(3, sib, sib).wait_recv()
            for dx in (1, 3, 2):
                self.copy(3 + dx, on_x(-dx) + 1 - 2 * c, sib).wait_recv()

    class Scatter:
        def __init__(self, compute, own, ssend, srecv, xsend, xrecv):
            self.compute, self.own = compute, own
            self.ssend, self.srecv, self.xsend, self.xrecv = ssend, srecv, xsend, xrecv
            self.s1, self.r1 = sems.take(4), sems.take(4)
            self.s2, self.r2 = sems.take(3), sems.take(3)

        def to_sib(self, dx):
            return remote(self.ssend.at[dx], self.srecv.at[dx], self.s1(dx), self.r1(dx), d, sib)

        def to_chip(self, dx):
            return remote(
                self.xsend.at[dx - 1], self.xrecv.at[dx - 1], self.s2(dx - 1), self.r2(dx - 1),
                d, on_x(dx))

        def start(self):
            for dx in (2, 1, 3, 0):
                self.ssend[dx] = self.compute((x + dx) % NX * 2 + 1 - c).astype(BF)
                cp = self.to_sib(dx)
                cp.start()
                pending.append(cp)

        def middle(self):
            for dx in (2, 1, 3):
                mine = self.compute(on_x(dx))
                self.to_sib(dx).wait_recv()
                self.xsend[dx - 1] = (mine + self.srecv[dx].astype(F32)).astype(BF)
                cp = self.to_chip(dx)
                cp.start()
                pending.append(cp)
            mine = self.compute(s)
            self.to_sib(0).wait_recv()
            self.own[...] = mine + self.srecv[0].astype(F32)

        def finish(self):
            total = self.own[...]
            for dx in (1, 3, 2):
                self.to_chip(dx).wait_recv()
                total = total + self.xrecv[dx - 1].astype(F32)
            return total

    class Swap:
        def __init__(self, src, dst):
            self.src, self.dst = src, dst
            self.ss, self.rs = sems.take(NJ), sems.take(NJ)

        def start(self):
            for j in range(NJ):
                peer = t_mine + S * j
                land = pl.multiple_of((d % S) * SLAB + (d // S) * GH, GH)
                cp = remote(
                    self.src.at[pl.ds(j * GH, GH), :], self.dst.at[pl.ds(land, GH), :],
                    self.ss(j), self.rs(d // S), peer, s)
                pl.when(peer != d)(cp.start)

                @pl.when(peer == d)
                def _():
                    self.dst[pl.ds(land, GH), :] = self.src[pl.ds(j * GH, GH), :]

        def finish(self):
            for j in range(NJ):
                peer = t_mine + S * j
                land = pl.multiple_of(t_mine * SLAB + j * GH, GH)
                cp = remote(
                    self.src.at[pl.ds(j * GH, GH), :], self.dst.at[pl.ds(land, GH), :],
                    self.ss(j), self.rs(j), peer, s)

                @pl.when(peer != d)
                def _():
                    cp.wait_recv()
                    cp.wait_send()

    gather_nodes = Gather(tbl, lambda q: q * N, N)
    gather_nodes.start(nodes_in)

    def permuted(values):
        ghost = values - PN
        part = ghost // GH
        place = PN + (part % S) * SLAB + (part // S) * GH + ghost % GH
        return jnp.where(values >= PN, place, values)

    def column(row):
        size = row.shape[1]
        hit = lax.broadcasted_iota(jnp.int32, (size, size), 0) == lax.broadcasted_iota(
            jnp.int32, (size, size), 1)
        return jnp.sum(jnp.where(hit, row.astype(F32), 0.0), axis=1, keepdims=True).astype(jnp.int32)

    def hot(mask):
        return jnp.where(mask, 1.0, 0.0).astype(BF)

    send_r = permuted(snd_row[...])
    recv_r = rcv_row[...]
    send_c = column(send_r)
    recv_c = column(recv_r)

    def build_t(r0):
        ids = lax.broadcasted_iota(jnp.int32, (256, E), 0) + r0
        pst[pl.ds(r0, 256), :] = hot(ids == send_r)

    rows_loop(PN + S * SLAB, 256, build_t)

    def build_rt(r0):
        ids = lax.broadcasted_iota(jnp.int32, (256, E), 0) + r0
        prt[pl.ds(r0, 256), :] = hot(ids == recv_r)

    rows_loop(PN, 256, build_rt)
    for c0 in range(0, PN + S * SLAB, 256):
        ids = lax.broadcasted_iota(jnp.int32, (E, 256), 1) + c0
        ps[:, c0:c0 + 256] = hot(ids == send_c)
        if c0 < PN:
            pr[:, c0:c0 + 256] = hot(ids == recv_c)

    lists = snd_lists[0]
    slot = lax.broadcasted_iota(jnp.int32, (S * SLAB, DOM), 0)
    part = slot // SLAB + (slot // GH) % NJ * S
    rows = hot(lax.broadcasted_iota(jnp.int32, (S * SLAB, DOM), 1) == part)
    high = dot_nt(rows, (lists // 32).astype(F32).astype(BF))
    low = dot_nt(rows, (lists % 32).astype(F32).astype(BF))
    slot = lax.broadcasted_iota(jnp.int32, (S * SLAB, GH), 0)
    here = lax.broadcasted_iota(jnp.int32, (S * SLAB, GH), 1) == slot % GH
    lists_c = jnp.sum(
        jnp.where(here, high * 32.0 + low, 0.0), axis=1, keepdims=True).astype(jnp.int32)

    loads[0].wait()
    loads[1].wait()

    def edge_part(r0):
        pre[pl.ds(r0, 256), :] = dot(edges[pl.ds(r0, 256), :], ein[0])

    rows_loop(E, 256, edge_part)

    gather_nodes.relay()
    gather_nodes.finish()

    hit = jnp.zeros((SLAB, 1), jnp.int32)
    for t in range(S):
        hit = jnp.where(t_mine == t, lists_c[t * SLAB:(t + 1) * SLAB, :], hit)
    pick = hot(lax.broadcasted_iota(jnp.int32, (SLAB, PN), 1) == hit)
    gsend[...] = dot(pick, tbl[:PN, :]).astype(BF)
    ghosts = tbl.at[pl.ds(PN, S * SLAB), :]
    swap_ghost = Swap(gsend, ghosts)
    swap_ghost.start()

    def gather_recv(r0):
        rows = pl.ds(r0, 256)
        got = dot(pr[rows, :], tbl[:PN, :]).astype(BF)
        recv[rows, :] = got
        pre[rows, :] = pre[rows, :] + dot(got, ein[2])

    rows_loop(E, 256, gather_recv)
    swap_ghost.finish()
    gather_ghost = Gather(ghosts, lambda q: ((q - d + DOM) % S) * SLAB, SLAB)
    gather_ghost.start(ghosts.at[pl.ds(pl.multiple_of(t_mine * SLAB, SLAB), SLAB), :])

    def gather_sent(r0):
        rows = pl.ds(r0, 256)
        sent_acc[rows, :] = dot(ps[rows, :PN], tbl[:PN, :])

    rows_loop(E, 256, gather_sent)
    gather_ghost.relay()
    gather_ghost.finish()

    loads[2].wait()
    edge_gain = egain[...]

    def edge_forward(r0):
        rows = pl.ds(r0, 256)
        got = (sent_acc[rows, :] + dot(ps[rows, PN:], tbl[PN:, :])).astype(BF)
        sent[rows, :] = got
        act = pre[rows, :] + dot(got, ein[1])
        pre[rows, :] = act
        hidden = swish(act).astype(BF)
        hid[rows, :] = hidden
        message = dot(hidden, eout[...])
        msg[rows, :] = message
        edges_out[rows, :] = (edges[rows, :].astype(F32) + normalize(message, edge_gain)).astype(BF)

    rows_loop(E, 256, edge_forward)

    def agg_block(q):
        return dot(prt[pl.ds(pl.multiple_of(q * N, N), N), :], edges_out[...])

    reduce_agg = Scatter(agg_block, agg_own, aggs_send, aggs_recv, aggx_send, aggx_recv)
    reduce_agg.start()
    reduce_agg.middle()
    loads[3].wait()
    loads[4].wait()
    loads[5].wait()
    npre[...] = dot(nodes_in[...], nin[0])
    agg[...] = reduce_agg.finish().astype(BF)

    node_gain = ngain[...]
    act = npre[...] + dot(agg[...], nin[1])
    hidden = swish(act).astype(BF)
    nhid[...] = hidden
    message = dot(hidden, nout[...])
    nodes_out[...] = (nodes_in[...].astype(F32) + normalize(message, node_gain)).astype(BF)
    upstream = ncot[...].astype(F32)
    grad_message = normalize_back(message, node_gain, upstream).astype(BF)
    dnmsg[...] = grad_message
    grad_pre = (dot_nt(grad_message, nout[...]) * swish_slope(act)).astype(BF)
    dnpre[...] = grad_pre
    dagg_own[...] = dot_nt(grad_pre, nin[1]).astype(BF)
    dagg[pl.ds(pl.multiple_of(s * N, N), N), :] = dagg_own[...]

    gather_dagg = Gather(dagg, lambda q: q * N, N)
    gather_dagg.start(dagg_own)
    gdirect[...] = upstream + dot_nt(grad_pre, nin[0])

    mine_cols = pl.ds(pl.multiple_of(c * HALF, HALF), HALF)
    sib_cols = pl.ds(pl.multiple_of((1 - c) * HALF, HALF), HALF)

    class Products:
        def __init__(self, pairs, ssend, srecv, own):
            self.pairs, self.ssend, self.srecv, self.own = pairs, ssend, srecv, own
            self.s0, self.r0 = sems.take(len(pairs)), sems.take(len(pairs))

        def sib_copy(self, i):
            return remote(self.ssend.at[i], self.srecv.at[i], self.s0(i), self.r0(i), d, sib)

        def products(self, i):
            left, right = self.pairs[i]
            self.ssend[i] = dot_tn(left[...], right[:, sib_cols]).astype(BF)
            cp = self.sib_copy(i)
            cp.start()
            pending.append(cp)
            self.own[i] = dot_tn(left[...], right[:, mine_cols])

        def chip_sum(self, i, rows):
            return self.own[i, rows, :] + self.srecv[i, rows, :].astype(F32)

    class Peers:
        def __init__(self, count, send, recv, to):
            self.count, self.sbuf, self.rbuf, self.to = count, send, recv, to
            self.ss, self.rs = sems.take(count - 1), sems.take(count - 1)

        def copy(self, k):
            return remote(
                self.sbuf.at[k - 1], self.rbuf.at[k - 1], self.ss(k - 1), self.rs(k - 1),
                *self.to(k))

        def send(self, k, value):
            self.sbuf[k - 1] = value.astype(BF)
            cp = self.copy(k)
            cp.start()
            pending.append(cp)

        def total(self, mine):
            for k in range(1, self.count):
                self.copy(k).wait_recv()
                mine = mine + self.rbuf[k - 1].astype(F32)
            return mine

    def on_y(k):
        return (y + k) % NY * NZ + z, s

    def on_z(k):
        return y * NZ + (z + k) % NZ, s

    Z_ORDER = (4, 3, 5, 2, 6, 1, 7)

    class Weights(Products):
        def __init__(self, pairs, ssend, srecv, own, ysend, yrecv, ysum, xsend, xrecv, xsum, zsend, zrecv):
            super().__init__(pairs, ssend, srecv, own)
            self.y = [Peers(NY, ysend.at[i], yrecv.at[i], on_y) for i in range(3)]
            self.ysum, self.xsend, self.xrecv, self.xsum = ysum, xsend, xrecv, xsum
            self.sx, self.rx = sems.take(NX - 1), sems.take(NX - 1)
            self.z = Peers(NZ, zsend, zrecv, on_z)

        def to_y(self, i):
            self.sib_copy(i).wait_recv()
            for k in (2, 1, 3):
                rows = pl.ds(pl.multiple_of((y + k) % NY * 128, 128), 128)
                self.y[i].send(k, self.chip_sum(i, rows))

        def x_copy(self, k):
            return remote(
                self.xsend.at[k - 1], self.xrecv.at[k - 1], self.sx(k - 1), self.rx(k - 1),
                d, on_x(k))

        def to_x(self):
            rows = pl.ds(pl.multiple_of(y * 128, 128), 128)
            for i in range(3):
                self.ysum[i] = self.y[i].total(self.chip_sum(i, rows))
            for k in (2, 1, 3):
                @pl.when((x + k) % NX < 3)
                def _():
                    self.xsend[k - 1] = self.ysum[(x + k) % NX].astype(BF)
                    self.x_copy(k).start()

        def to_z(self):
            self.xsum[...] = self.ysum[jnp.minimum(x, 2)]

            @pl.when(x < 3)
            def _():
                total = self.xsum[...]
                for k in (1, 3, 2):
                    self.x_copy(k).wait_recv()
                    total = total + self.xrecv[k - 1].astype(F32)
                self.xsum[...] = total
            for k in Z_ORDER:
                rows = pl.ds(pl.multiple_of((z + k) % NZ * 16, 16), 16)
                self.z.send(k, self.xsum[rows, :])

        def finish(self):
            return self.z.total(self.xsum[pl.ds(pl.multiple_of(z * 16, 16), 16), :])

        def drain(self):
            for k in (2, 1, 3):
                pl.when((x + k) % NX < 3)(self.x_copy(k).wait_send)

    class LastWeights(Products):
        def __init__(self, pairs, ssend, srecv, own, zsend, zrecv, zsum, ysend, yrecv, xsend, xrecv):
            super().__init__(pairs, ssend, srecv, own)
            self.zsum, self.xsend, self.xrecv = zsum, xsend, xrecv
            self.z = Peers(NZ, zsend, zrecv, on_z)
            self.y = Peers(NY, ysend, yrecv, on_y)
            self.sx, self.rx = sems.take(1), sems.take(3)

        def to_z(self):
            self.sib_copy(0).wait_recv()
            for k in Z_ORDER:
                rows = pl.ds(pl.multiple_of((z + k) % NZ * 64, 64), 64)
                self.z.send(k, self.chip_sum(0, rows))

        def to_y(self):
            rows = pl.ds(pl.multiple_of(z * 64, 64), 64)
            self.zsum[...] = self.z.total(self.chip_sum(0, rows))
            for k in (2, 1, 3):
                rows = pl.ds(pl.multiple_of((y + k) % NY * 16, 16), 16)
                self.y.send(k, self.zsum[rows, :])

        def x_copy(self, k):
            return remote(self.xsend, self.xrecv.at[k], self.sx(0), self.rx(k), d, 6 + c)

        def to_x(self):
            total = self.y.total(self.zsum[pl.ds(pl.multiple_of(y * 16, 16), 16), :])
            fin[0] = total
            self.xsend[...] = total.astype(BF)
            for k in range(3):
                pl.when(x == k)(self.x_copy(k).start)

        def finish(self):
            total = fin[0]
            for k in range(3):
                self.x_copy(k).wait_recv()
                total = total + self.xrecv[k].astype(F32)
            return total

        def drain(self):
            pl.when(x < 3)(self.x_copy(0).wait_send)

    node_weights = Weights(
        ((nodes_in, dnpre), (agg, dnpre), (nhid, dnmsg)),
        fn_ssend, fn_srecv, fn_own, fn_ysend, fn_yrecv, fn_ysum, fn_xsend, fn_xrecv, fn_xsum,
        fn_zsend, fn_zrecv)
    edge_weights = Weights(
        ((edges, dpre), (sent, dpre), (recv, dpre)),
        fe_ssend, fe_srecv, fe_own, fe_ysend, fe_yrecv, fe_ysum, fe_xsend, fe_xrecv, fe_xsum,
        fe_zsend, fe_zrecv)
    out_weights = LastWeights(
        ((hid, dmsg),),
        fo_ssend, fo_srecv, fo_own, fo_zsend, fo_zrecv, fo_zsum, fo_ysend, fo_yrecv, fo_xsend,
        fo_xrecv)

    for i in range(3):
        node_weights.products(i)
    for i in range(3):
        node_weights.to_y(i)
    gather_dagg.relay()
    gather_dagg.finish()

    def edge_backward(r0):
        rows = pl.ds(r0, 256)
        up = ecot[rows, :].astype(F32) + dot(pr[rows, :], dagg[...])
        gedge[rows, :] = up
        grad_msg = normalize_back(msg[rows, :], edge_gain, up).astype(BF)
        dmsg[rows, :] = grad_msg
        grad = (dot_nt(grad_msg, eout[...]) * swish_slope(pre[rows, :])).astype(BF)
        dpre[rows, :] = grad

    rows_loop(E, 256, edge_backward)

    def ghost_block(q):
        place = PN + ((q - d + DOM) % S) * SLAB
        return dot(pst[pl.ds(pl.multiple_of(place, SLAB), SLAB), :], dsent[...])

    out_weights.products(0)
    edge_weights.products(0)
    out_weights.to_z()
    edge_weights.products(1)
    edge_weights.to_y(0)
    edge_weights.products(2)
    edge_weights.to_y(1)

    def send_grad(r0):
        rows = pl.ds(r0, 256)
        dsent[rows, :] = dot_nt(dpre[rows, :], ein[1]).astype(BF)

    rows_loop(E, 256, send_grad)
    reduce_ghost = Scatter(ghost_block, gg_own, gg_ssend, gg_srecv, gg_xsend, gg_xrecv)
    reduce_ghost.start()
    edge_weights.to_y(2)
    reduce_ghost.middle()

    def recv_grad(r0):
        rows = pl.ds(r0, 256)
        drecv[rows, :] = dot_nt(dpre[rows, :], ein[2]).astype(BF)

    rows_loop(E, 256, recv_grad)

    def own_block(q):
        rows = pl.ds(pl.multiple_of(q * N, N), N)
        return dot(pst[rows, :], dsent[...]) + dot(prt[rows, :], drecv[...])

    reduce_own = Scatter(own_block, own_own, own_ssend, own_srecv, own_xsend, own_xrecv)
    reduce_own.start()
    node_weights.to_x()
    a2_send[...] = reduce_ghost.finish().astype(BF)
    swap_back = Swap(a2_send, retg)
    swap_back.start()
    reduce_own.middle()

    def edge_grad(r0):
        rows = pl.ds(r0, 256)
        egrad[rows, :] = (gedge[rows, :] + dot_nt(dpre[rows, :], ein[0])).astype(BF)

    rows_loop(E, 256, edge_grad)
    place = hot(lax.broadcasted_iota(jnp.int32, (S * SLAB, N), 1) + s * N == lists_c)
    swap_back.finish()
    gather_back = Gather(retg, lambda q: ((q - d + DOM) % S) * SLAB, SLAB)
    gather_back.start(retg.at[pl.ds(pl.multiple_of(t_mine * SLAB, SLAB), SLAB), :])
    out_weights.to_y()
    edge_weights.to_x()
    node_weights.to_z()
    gather_back.relay()
    out_weights.to_x()
    gather_back.finish()
    edge_weights.to_z()
    direct = gdirect[...] + dot_tn(place, retg[...])
    ngrad[...] = (direct + reduce_own.finish()).astype(BF)

    s_fin, r_fin = sems.take(6), sems.take(4)

    def fin_copy(group, i, slot, half):
        to = jnp.minimum(owner(group, i)[0], DOM * S - 1)
        return remote(
            fin.at[group], rows_in.at[slot, half], s_fin(3 * group + i), r_fin(2 * slot + half),
            to // S, to % S)

    def hand_out(group):
        for i in range(3):
            to, at, valid = owner(group, i)
            for slot in range(2):
                for half in range(2):
                    here = valid & (at == slot) & (c == half)
                    pl.when(here & (to != lin))(fin_copy(group, i, slot, half).start)

                    @pl.when(here & (to == lin))
                    def _():
                        rows_in[slot, half] = fin[group]

    fin[1] = node_weights.finish()
    hand_out(1)
    edge_block = edge_weights.finish()

    @pl.when(x < 3)
    def _():
        fin[0] = edge_block

    @pl.when(x == 3)
    def _():
        fin[0] = out_weights.finish()

    hand_out(0)
    for slot in range(2):
        for half in range(2):
            pl.when(from_other(slot, half))(fin_copy(0, 0, slot, half).wait_recv)
    shift = first_row % 16
    for choice in range(0, 16, 2):
        @pl.when(shift == choice)
        def _():
            split = min(16 - choice, OUT_ROWS)
            for half in range(2):
                cols = slice(half * HALF, (half + 1) * HALF)
                wout[:split, cols] = rows_in[0, half, choice:choice + split, :]
                if split < OUT_ROWS:
                    wout[split:, cols] = rows_in[1, half, :OUT_ROWS - split, :]

    for cp in pending:
        cp.wait_send()
    node_weights.drain()
    edge_weights.drain()
    out_weights.drain()
    for group in range(2):
        for i in range(3):
            to, _, valid = owner(group, i)
            pl.when(valid & (to != lin))(fin_copy(group, i, 0, 0).wait_send)


def scratch():
    def bf(*shape):
        return pltpu.VMEM(shape, BF)

    def f32(*shape):
        return pltpu.VMEM(shape, F32)

    T = PN + S * SLAB

    def scatter(rows):
        return [bf(NX, rows, D), bf(NX, rows, D), bf(NX - 1, rows, D), bf(NX - 1, rows, D), f32(rows, D)]

    def products(count):
        return [bf(count, D, HALF), bf(count, D, HALF), f32(count, D, HALF)]

    def weights():
        return [
            *products(3), bf(3, NY - 1, 128, HALF), bf(3, NY - 1, 128, HALF), f32(3, 128, HALF),
            bf(NX - 1, 128, HALF), bf(NX - 1, 128, HALF), f32(128, HALF),
            bf(NZ - 1, 16, HALF), bf(NZ - 1, 16, HALF),
        ]

    return [
        bf(E, D), bf(3, D, D), bf(D, D), bf(2, D, D), bf(D, D), bf(E, D),
        bf(E, T), bf(E, PN), bf(T, E), bf(PN, E), bf(T, D), f32(E, D), bf(E, D), bf(E, D),
        f32(E, D), f32(E, D), bf(E, D),
        bf(SLAB, D), *scatter(N),
        bf(N, D), f32(N, D), bf(N, D), f32(N, D), bf(N, D), bf(N, D), bf(N, D), bf(PN, D),
        f32(E, D), bf(E, D), bf(E, D), bf(E, D), bf(E, D),
        *scatter(SLAB), bf(SLAB, D), bf(S * SLAB, D), *scatter(N),
        *weights(), *weights(),
        *products(1), bf(NZ - 1, 64, HALF), bf(NZ - 1, 64, HALF), f32(64, HALF),
        bf(NY - 1, 16, HALF), bf(NY - 1, 16, HALF), bf(16, HALF), bf(NX - 1, 16, HALF),
        f32(2, 16, HALF), f32(2, 2, 16, HALF),
        pltpu.SemaphoreType.DMA((N_SEM,)),
    ]


def hand_over(a0, a1, a2, a3, w_in, b0, b1, b2, b3, w_out):
    for src, dst in ((a0, b0), (a1, b1), (a2, b2), (a3, b3)):
        dst[...] = src[...]
    for i in range(OUT_ROWS):
        w_out[:, i * D:(i + 1) * D] = w_in[i:i + 1, :]


def body(
    node_state, edge_state, senders, receivers, send_rows, edge_in, edge_out, edge_gain,
    node_in, node_out, node_gain, node_cot, edge_cot,
):
    vmem = pl.BlockSpec(memory_space=pltpu.VMEM)
    hbm = pl.BlockSpec(memory_space=pl.ANY)
    states = (
        jax.ShapeDtypeStruct((N, D), BF),
        jax.ShapeDtypeStruct((E, D), BF),
        jax.ShapeDtypeStruct((N, D), BF),
        jax.ShapeDtypeStruct((E, D), BF),
    )
    results = pl.pallas_call(
        kernel,
        out_shape=states + (jax.ShapeDtypeStruct((OUT_ROWS, D), F32),),
        in_specs=[vmem] * 7 + [hbm] * 6,
        out_specs=[vmem] * 5,
        scratch_shapes=scratch(),
        compiler_params=pltpu.CompilerParams(
            collective_id=0, has_side_effects=True, vmem_limit_bytes=60 * 1024 * 1024),
    )(
        node_state, senders.reshape(1, E), receivers.reshape(1, E),
        send_rows.transpose(0, 2, 1),
        edge_gain, node_gain, node_cot,
        edge_state, edge_in[0], edge_out[0], node_in[0], node_out[0], edge_cot,
    )
    return pl.pallas_call(
        hand_over,
        out_shape=states + (jax.ShapeDtypeStruct((1, OUT_ROWS * D), F32),),
        in_specs=[vmem] * 5,
        out_specs=[vmem] * 5,
    )(*results)


def solution(mesh):
    both = P(("dom", "esplit"), None)
    in_specs = (
        both, both, P(("dom", "esplit")), P(("dom", "esplit")), P("dom", None, None),
        P(), P(), P(), P(), P(), P(), both, both,
    )
    out_specs = (both, both, both, both, P(None, ("dom", "esplit")))
    return jax.shard_map(body, mesh=mesh, in_specs=in_specs, out_specs=out_specs, check_vma=False)
```

```python
import functools

import jax
import jax.numpy as jnp
from jax import lax
from jax.experimental import pallas as pl
from jax.experimental.pallas import tpu as pltpu
from jax.sharding import PartitionSpec as P

EPSILON = 1e-05
BF = jnp.bfloat16
F32 = jnp.float32
MESH = pl.DeviceIdType.MESH

NZ = 8
NY = 4
NX = 4
DOM = NY * NZ
S = NX * 2
D = 512
N = 128
PN = N * S
E = 512
GH = 16
SLAB = DOM // S * GH
NJ = DOM // S
HALF = D // 2
NMAT = 7
OUT_ROWS = 14


def dot(a, b):
    return lax.dot_general(a, b, (((1,), (0,)), ((), ())), preferred_element_type=F32)


def dot_nt(a, b):
    return lax.dot_general(a, b, (((1,), (1,)), ((), ())), preferred_element_type=F32)


def dot_tn(a, b):
    return lax.dot_general(a, b, (((0,), (0,)), ((), ())), preferred_element_type=F32)


def normalize(values, gain):
    average = jnp.mean(values, axis=-1, keepdims=True)
    centered = values - average
    inv_scale = lax.rsqrt(jnp.mean(centered * centered, axis=-1, keepdims=True) + EPSILON)
    return gain * centered * inv_scale


def normalize_back(values, gain, upstream):
    average = jnp.mean(values, axis=-1, keepdims=True)
    centered = values - average
    inv_scale = lax.rsqrt(jnp.mean(centered * centered, axis=-1, keepdims=True) + EPSILON)
    scaled = centered * inv_scale
    grad_scaled = upstream * gain
    first = jnp.mean(grad_scaled, axis=-1, keepdims=True)
    second = jnp.mean(grad_scaled * scaled, axis=-1, keepdims=True)
    return inv_scale * (grad_scaled - first - scaled * second)


def swish(values):
    return values * jax.nn.sigmoid(values)


def swish_slope(values):
    sigma = jax.nn.sigmoid(values)
    return sigma * (1.0 + values * (1.0 - sigma))


def rows_loop(total, step, fn):
    def one(i, carry):
        fn(pl.multiple_of(i * step, step))
        return carry

    lax.fori_loop(0, total // step, one, 0)


class Sems:
    def __init__(self, ref):
        self.ref = ref
        self.used = 0

    def take(self, count):
        base = self.used
        self.used += count
        return lambda i: self.ref.at[base + i]


N_SEM = 340


def kernel(
    nodes_in, snd_row, rcv_row, snd_lists, egain, ngain, ncot,
    edges_hbm, ein_hbm, eout_hbm, nin_hbm, nout_hbm, ecot_hbm,
    nodes_out, edges_out, ngrad, egrad, wout,
    nodes_out_v, edges_out_v, egrad_v, edges, ein, eout, nin, nout, ecot,
    ps, pr, pst, prt, tbl, sent_acc, sent, recv, pre, msg, hid,
    gsend, aggs_send, aggs_recv, aggx_send, aggx_recv, agg_own,
    agg, npre, nmsg, nhid, gdirect, dnpre, dnmsg, dagg_own, dagg,
    gedge, dmsg, dpre, dsent, drecv,
    gg_ssend, gg_srecv, gg_xsend, gg_xrecv, gg_own, a2_send, retg,
    own_ssend, own_srecv, own_xsend, own_xrecv, own_own,
    fn_ssend, fn_srecv, fn_own, fn_ysend, fn_yrecv, fn_ysum, fn_zsend, fn_zrecv, fn_zsum, fn_xsend, fn_xrecv,
    fe_ssend, fe_srecv, fe_own, fe_ysend, fe_yrecv, fe_ysum, fe_zsend, fe_zrecv, fe_zsum, fe_xsend, fe_xrecv,
    fo_ssend, fo_srecv, fo_own, fo_zsend, fo_zrecv, fo_zsum, fo_ysend, fo_yrecv, fo_ysum, fo_xsend, fo_xrecv,
    fin, rows_in,
    sem_ref,
):
    d = lax.axis_index("dom")
    s = lax.axis_index("esplit")
    y = d // NZ
    z = d % NZ
    x = s // 2
    c = s % 2
    lin = d * S + s
    sib = s + 1 - 2 * c
    t_mine = (s - d + DOM) % S
    sems = Sems(sem_ref)
    pending = []

    def remote(src, dst, send_sem, recv_sem, dom, split):
        return pltpu.make_async_remote_copy(
            src_ref=src, dst_ref=dst, send_sem=send_sem, recv_sem=recv_sem,
            device_id=(dom, split), device_id_type=MESH,
        )

    bar = pltpu.get_barrier_semaphore()

    def greet(dom, split):
        pl.semaphore_signal(bar, inc=1, device_id=(dom, split), device_id_type=MESH)

    for k in range(1, S):
        greet(d, (s + k) % S)
    for k in range(1, NY):
        greet((y + k) % NY * NZ + z, s)
    for k in range(1, NZ):
        greet(y * NZ + (z + k) % NZ, s)
    for j in range(NJ):
        pl.when(t_mine + S * j != d)(functools.partial(greet, t_mine + S * j, s))
    first_row = OUT_ROWS * lin
    b_first = first_row // 16
    b_last = (first_row + OUT_ROWS - 1) // 16

    def holder(b, half):
        r = b % DOM
        return jnp.where(b // DOM == 3, r % NY * NZ + r // NY, r), (b // DOM) % NX * 2 + half

    def from_other(slot, half):
        dom, split = holder(b_first + slot, half)
        here = dom * S + split != lin
        return here if slot == 0 else here & (b_last != b_first)

    for slot in range(2):
        for half in range(2):
            dom, split = holder(b_first + slot, half)
            pl.when(from_other(slot, half))(functools.partial(greet, dom, split))

    lsem = sems.take(6)
    loads = [
        pltpu.make_async_copy(a, b, lsem(i))
        for i, (a, b) in enumerate(
            ((edges_hbm, edges), (ein_hbm, ein), (eout_hbm, eout), (nin_hbm, nin),
             (nout_hbm, nout), (ecot_hbm, ecot)))
    ]
    ssem = sems.take(3)
    stores = [
        pltpu.make_async_copy(a, b, ssem(i))
        for i, (a, b) in enumerate(
            ((edges_out_v, edges_out), (nodes_out_v, nodes_out), (egrad_v, egrad)))
    ]
    for load in loads:
        load.start()

    tbl[pl.ds(pl.multiple_of(s * N, N), N), :] = nodes_in[...]

    def owner(group, i):
        b = DOM * (x + NX * group) + (d if group else jnp.where(x == 3, z * NY + y, d))
        to = (16 * b) // OUT_ROWS + i
        valid = to <= (16 * b + 15) // OUT_ROWS
        if group:
            valid = valid & (x < NMAT - NX)
        return to, b - (OUT_ROWS * to) // 16, valid

    arrivals = (S - 1) + (NY - 1) + (NZ - 1)
    for j in range(NJ):
        arrivals = arrivals + jnp.where(t_mine + S * j != d, 1, 0)
    for group in range(2):
        for i in range(3):
            to, _, valid = owner(group, i)
            arrivals = arrivals + jnp.where(valid & (to != lin), 1, 0)
    pl.semaphore_wait(bar, arrivals)

    def on_x(dx):
        return (x + dx + NX) % NX * 2 + c

    class Gather:
        def __init__(self, buf, offset, rows):
            self.buf, self.offset, self.rows = buf, offset, rows
            self.ss, self.rs = sems.take(7), sems.take(7)

        def copy(self, k, origin, split, src=None):
            there = self.buf.at[pl.ds(pl.multiple_of(self.offset(origin), self.rows), self.rows), :]
            here = there if src is None else src
            return remote(here, there, self.ss(k), self.rs(k), d, split)

        def send(self, k, origin, split, src=None):
            cp = self.copy(k, origin, split, src)
            cp.start()
            pending.append(cp)

        def start(self, src):
            for dx in (2, 1, 3):
                self.send(dx - 1, s, on_x(dx), src)
            self.send(3, s, sib, src)

        def forward(self, dx):
            origin = on_x(-dx)
            self.copy(dx - 1, origin, sib).wait_recv()
            self.send(3 + dx, origin, sib)

        def relay(self):
            self.forward(1)
            self.forward(3)

        def finish(self):
            self.forward(2)
            self.copy(3, sib, sib).wait_recv()
            for dx in (1, 3, 2):
                self.copy(3 + dx, on_x(-dx) + 1 - 2 * c, sib).wait_recv()

    class Scatter:
        def __init__(self, compute, own, ssend, srecv, xsend, xrecv):
            self.compute, self.own = compute, own
            self.ssend, self.srecv, self.xsend, self.xrecv = ssend, srecv, xsend, xrecv
            self.s1, self.r1 = sems.take(4), sems.take(4)
            self.s2, self.r2 = sems.take(3), sems.take(3)

        def to_sib(self, dx):
            return remote(self.ssend.at[dx], self.srecv.at[dx], self.s1(dx), self.r1(dx), d, sib)

        def to_chip(self, dx):
            return remote(
                self.xsend.at[dx - 1], self.xrecv.at[dx - 1], self.s2(dx - 1), self.r2(dx - 1),
                d, on_x(dx))

        def start(self):
            for dx in (2, 1, 3, 0):
                self.ssend[dx] = self.compute((x + dx) % NX * 2 + 1 - c).astype(BF)
                cp = self.to_sib(dx)
                cp.start()
                pending.append(cp)

        def middle(self):
            for dx in (2, 1, 3):
                mine = self.compute(on_x(dx))
                self.to_sib(dx).wait_recv()
                self.xsend[dx - 1] = (mine + self.srecv[dx].astype(F32)).astype(BF)
                cp = self.to_chip(dx)
                cp.start()
                pending.append(cp)
            mine = self.compute(s)
            self.to_sib(0).wait_recv()
            self.own[...] = mine + self.srecv[0].astype(F32)

        def finish(self):
            total = self.own[...]
            for dx in (1, 3, 2):
                self.to_chip(dx).wait_recv()
                total = total + self.xrecv[dx - 1].astype(F32)
            return total

    class Swap:
        def __init__(self, src, dst):
            self.src, self.dst = src, dst
            self.ss, self.rs = sems.take(NJ), sems.take(NJ)

        def start(self):
            for j in range(NJ):
                peer = t_mine + S * j
                land = pl.multiple_of((d % S) * SLAB + (d // S) * GH, GH)
                cp = remote(
                    self.src.at[pl.ds(j * GH, GH), :], self.dst.at[pl.ds(land, GH), :],
                    self.ss(j), self.rs(d // S), peer, s)
                pl.when(peer != d)(cp.start)

                @pl.when(peer == d)
                def _():
                    self.dst[pl.ds(land, GH), :] = self.src[pl.ds(j * GH, GH), :]

        def finish(self):
            for j in range(NJ):
                peer = t_mine + S * j
                land = pl.multiple_of(t_mine * SLAB + j * GH, GH)
                cp = remote(
                    self.src.at[pl.ds(j * GH, GH), :], self.dst.at[pl.ds(land, GH), :],
                    self.ss(j), self.rs(j), peer, s)

                @pl.when(peer != d)
                def _():
                    cp.wait_recv()
                    cp.wait_send()

    gather_nodes = Gather(tbl, lambda q: q * N, N)
    gather_nodes.start(nodes_in)

    def permuted(values):
        ghost = values - PN
        part = ghost // GH
        place = PN + (part % S) * SLAB + (part // S) * GH + ghost % GH
        return jnp.where(values >= PN, place, values)

    def column(row):
        size = row.shape[1]
        hit = lax.broadcasted_iota(jnp.int32, (size, size), 0) == lax.broadcasted_iota(
            jnp.int32, (size, size), 1)
        return jnp.sum(jnp.where(hit, row.astype(F32), 0.0), axis=1, keepdims=True).astype(jnp.int32)

    def hot(mask):
        return jnp.where(mask, 1.0, 0.0).astype(BF)

    send_r = permuted(snd_row[...])
    recv_r = rcv_row[...]
    send_c = column(send_r)
    recv_c = column(recv_r)

    def build_t(r0):
        ids = lax.broadcasted_iota(jnp.int32, (256, E), 0) + r0
        pst[pl.ds(r0, 256), :] = hot(ids == send_r)

    rows_loop(PN + S * SLAB, 256, build_t)

    def build_rt(r0):
        ids = lax.broadcasted_iota(jnp.int32, (256, E), 0) + r0
        prt[pl.ds(r0, 256), :] = hot(ids == recv_r)

    rows_loop(PN, 256, build_rt)
    for c0 in range(0, PN + S * SLAB, 256):
        ids = lax.broadcasted_iota(jnp.int32, (E, 256), 1) + c0
        ps[:, c0:c0 + 256] = hot(ids == send_c)
        if c0 < PN:
            pr[:, c0:c0 + 256] = hot(ids == recv_c)

    lists = snd_lists[0]
    slot = lax.broadcasted_iota(jnp.int32, (S * SLAB, DOM), 0)
    part = slot // SLAB + (slot // GH) % NJ * S
    rows = hot(lax.broadcasted_iota(jnp.int32, (S * SLAB, DOM), 1) == part)
    high = dot_nt(rows, (lists // 32).astype(F32).astype(BF))
    low = dot_nt(rows, (lists % 32).astype(F32).astype(BF))
    slot = lax.broadcasted_iota(jnp.int32, (S * SLAB, GH), 0)
    here = lax.broadcasted_iota(jnp.int32, (S * SLAB, GH), 1) == slot % GH
    lists_c = jnp.sum(
        jnp.where(here, high * 32.0 + low, 0.0), axis=1, keepdims=True).astype(jnp.int32)

    loads[0].wait()
    loads[1].wait()

    def edge_part(r0):
        pre[pl.ds(r0, 256), :] = dot(edges[pl.ds(r0, 256), :], ein[0])

    rows_loop(E, 256, edge_part)

    gather_nodes.relay()
    gather_nodes.finish()

    hit = jnp.zeros((SLAB, 1), jnp.int32)
    for t in range(S):
        hit = jnp.where(t_mine == t, lists_c[t * SLAB:(t + 1) * SLAB, :], hit)
    pick = hot(lax.broadcasted_iota(jnp.int32, (SLAB, PN), 1) == hit)
    gsend[...] = dot(pick, tbl[:PN, :]).astype(BF)
    ghosts = tbl.at[pl.ds(PN, S * SLAB), :]
    swap_ghost = Swap(gsend, ghosts)
    swap_ghost.start()

    def gather_recv(r0):
        rows = pl.ds(r0, 256)
        got = dot(pr[rows, :], tbl[:PN, :]).astype(BF)
        recv[rows, :] = got
        pre[rows, :] = pre[rows, :] + dot(got, ein[2])

    rows_loop(E, 256, gather_recv)
    swap_ghost.finish()
    gather_ghost = Gather(ghosts, lambda q: ((q - d + DOM) % S) * SLAB, SLAB)
    gather_ghost.start(ghosts.at[pl.ds(pl.multiple_of(t_mine * SLAB, SLAB), SLAB), :])

    def gather_sent(r0):
        rows = pl.ds(r0, 256)
        sent_acc[rows, :] = dot(ps[rows, :PN], tbl[:PN, :])

    rows_loop(E, 256, gather_sent)
    gather_ghost.relay()
    gather_ghost.finish()

    loads[2].wait()
    edge_gain = egain[...]

    def edge_forward(r0):
        rows = pl.ds(r0, 256)
        got = (sent_acc[rows, :] + dot(ps[rows, PN:], tbl[PN:, :])).astype(BF)
        sent[rows, :] = got
        act = pre[rows, :] + dot(got, ein[1])
        pre[rows, :] = act
        hidden = swish(act).astype(BF)
        hid[rows, :] = hidden
        message = dot(hidden, eout[...])
        msg[rows, :] = message
        edges_out_v[rows, :] = (edges[rows, :].astype(F32) + normalize(message, edge_gain)).astype(BF)

    rows_loop(E, 256, edge_forward)

    NH = N // 2

    def agg_block(half):
        def block(q):
            return dot(prt[pl.ds(pl.multiple_of(q * N + half * NH, NH), NH), :], edges_out_v[...])

        return block

    reduce_agg = [
        Scatter(agg_block(h), agg_own.at[h], aggs_send.at[h], aggs_recv.at[h], aggx_send.at[h],
                aggx_recv.at[h])
        for h in range(2)
    ]
    gather_dagg = [
        Gather(dagg, functools.partial(lambda h, q: q * N + h * NH, h), NH) for h in range(2)
    ]
    for h in range(2):
        reduce_agg[h].start()
    for h in range(2):
        reduce_agg[h].middle()
    stores[0].start()
    loads[3].wait()
    loads[4].wait()
    loads[5].wait()
    npre[...] = dot(nodes_in[...], nin[0])
    node_gain = ngain[...]

    for h in range(2):
        rows = slice(h * NH, (h + 1) * NH)
        sums = reduce_agg[h].finish().astype(BF)
        agg[rows, :] = sums
        act = npre[rows, :] + dot(sums, nin[1])
        npre[rows, :] = act
        hidden = swish(act).astype(BF)
        nhid[rows, :] = hidden
        message = dot(hidden, nout[...])
        nmsg[rows, :] = message
        upstream = ncot[rows, :].astype(F32)
        grad_message = normalize_back(message, node_gain, upstream).astype(BF)
        dnmsg[rows, :] = grad_message
        grad_pre = (dot_nt(grad_message, nout[...]) * swish_slope(act)).astype(BF)
        dnpre[rows, :] = grad_pre
        dagg_own[rows, :] = dot_nt(grad_pre, nin[1]).astype(BF)
        dagg[pl.ds(pl.multiple_of(s * N + h * NH, NH), NH), :] = dagg_own[rows, :]
        gather_dagg[h].start(dagg_own.at[rows, :])
    gdirect[...] = ncot[...].astype(F32) + dot_nt(dnpre[...], nin[0])
    nodes_out_v[...] = (
        nodes_in[...].astype(F32) + normalize(nmsg[...], node_gain)).astype(BF)
    stores[1].start()

    mine_cols = pl.ds(pl.multiple_of(c * HALF, HALF), HALF)
    sib_cols = pl.ds(pl.multiple_of((1 - c) * HALF, HALF), HALF)

    class Products:
        def __init__(self, pairs, ssend, srecv, own):
            self.pairs, self.ssend, self.srecv, self.own = pairs, ssend, srecv, own
            self.s0, self.r0 = sems.take(len(pairs)), sems.take(len(pairs))

        def sib_copy(self, i):
            return remote(self.ssend.at[i], self.srecv.at[i], self.s0(i), self.r0(i), d, sib)

        def products(self, i):
            left, right = self.pairs[i]
            self.ssend[i] = dot_tn(left[...], right[:, sib_cols]).astype(BF)
            cp = self.sib_copy(i)
            cp.start()
            pending.append(cp)
            self.own[i] = dot_tn(left[...], right[:, mine_cols])

        def chip_sum(self, i, rows):
            return self.own[i, rows, :] + self.srecv[i, rows, :].astype(F32)

    class Peers:
        def __init__(self, count, send, recv, to):
            self.count, self.sbuf, self.rbuf, self.to = count, send, recv, to
            self.ss, self.rs = sems.take(count - 1), sems.take(count - 1)

        def copy(self, k):
            return remote(
                self.sbuf.at[k - 1], self.rbuf.at[k - 1], self.ss(k - 1), self.rs(k - 1),
                *self.to(k))

        def send(self, k, value):
            self.sbuf[k - 1] = value.astype(BF)
            cp = self.copy(k)
            cp.start()
            pending.append(cp)

        def total(self, mine):
            for k in range(1, self.count):
                self.copy(k).wait_recv()
                mine = mine + self.rbuf[k - 1].astype(F32)
            return mine

    def on_y(k):
        return (y + k) % NY * NZ + z, s

    def on_z(k):
        return y * NZ + (z + k) % NZ, s

    Z_ORDER = (4, 3, 5, 2, 6, 1, 7)

    class Weights(Products):
        def __init__(self, pairs, ssend, srecv, own, ysend, yrecv, ysum, zsend, zrecv, zsum, xsend, xrecv):
            super().__init__(pairs, ssend, srecv, own)
            self.y = [Peers(NY, ysend.at[i], yrecv.at[i], on_y) for i in range(3)]
            self.z = [Peers(NZ, zsend.at[i], zrecv.at[i], on_z) for i in range(3)]
            self.ysum, self.zsum, self.xsend, self.xrecv = ysum, zsum, xsend, xrecv
            self.sx, self.rx = sems.take(NX - 1), sems.take(NX - 1)

        def to_y(self, i):
            self.sib_copy(i).wait_recv()
            for k in (2, 1, 3):
                rows = pl.ds(pl.multiple_of((y + k) % NY * 128, 128), 128)
                self.y[i].send(k, self.chip_sum(i, rows))

        def to_z(self, i):
            rows = pl.ds(pl.multiple_of(y * 128, 128), 128)
            self.ysum[i] = self.y[i].total(self.chip_sum(i, rows))
            for k in Z_ORDER:
                rows = pl.ds(pl.multiple_of((z + k) % NZ * 16, 16), 16)
                self.z[i].send(k, self.ysum[i, rows, :])

        def x_copy(self, k):
            return remote(
                self.xsend.at[k - 1], self.xrecv.at[k - 1], self.sx(k - 1), self.rx(k - 1),
                d, on_x(k))

        def to_x(self):
            rows = pl.ds(pl.multiple_of(z * 16, 16), 16)
            for i in range(3):
                self.zsum[i] = self.z[i].total(self.ysum[i, rows, :])
            for k in (2, 1, 3):
                @pl.when((x + k) % NX < 3)
                def _():
                    self.xsend[k - 1] = self.zsum[(x + k) % NX].astype(BF)
                    self.x_copy(k).start()

        def finish(self):
            total = self.zsum[jnp.minimum(x, 2)]
            for k in (1, 3, 2):
                self.x_copy(k).wait_recv()
                total = total + self.xrecv[k - 1].astype(F32)
            return total

        def drain(self):
            for k in (2, 1, 3):
                pl.when((x + k) % NX < 3)(self.x_copy(k).wait_send)

    class LastWeights(Products):
        def __init__(self, pairs, ssend, srecv, own, zsend, zrecv, zsum, ysend, yrecv, ysum, xsend, xrecv):
            super().__init__(pairs, ssend, srecv, own)
            self.zsum, self.ysum, self.xsend, self.xrecv = zsum, ysum, xsend, xrecv
            self.z = Peers(NZ, zsend, zrecv, on_z)
            self.y = Peers(NY, ysend, yrecv, on_y)
            self.sx, self.rx = sems.take(1), sems.take(3)

        def to_z(self):
            self.sib_copy(0).wait_recv()
            for k in Z_ORDER:
                rows = pl.ds(pl.multiple_of((z + k) % NZ * 64, 64), 64)
                self.z.send(k, self.chip_sum(0, rows))

        def to_y(self):
            rows = pl.ds(pl.multiple_of(z * 64, 64), 64)
            self.zsum[...] = self.z.total(self.chip_sum(0, rows))
            for k in (2, 1, 3):
                rows = pl.ds(pl.multiple_of((y + k) % NY * 16, 16), 16)
                self.y.send(k, self.zsum[rows, :])

        def x_copy(self, k):
            return remote(self.xsend, self.xrecv.at[k], self.sx(0), self.rx(k), d, 6 + c)

        def to_x(self):
            total = self.y.total(self.zsum[pl.ds(pl.multiple_of(y * 16, 16), 16), :])
            self.ysum[...] = total
            self.xsend[...] = total.astype(BF)
            for k in range(3):
                pl.when(x == k)(self.x_copy(k).start)

        def finish(self):
            total = self.ysum[...]
            for k in range(3):
                self.x_copy(k).wait_recv()
                total = total + self.xrecv[k].astype(F32)
            return total

        def drain(self):
            pl.when(x < 3)(self.x_copy(0).wait_send)

    node_weights = Weights(
        ((nodes_in, dnpre), (agg, dnpre), (nhid, dnmsg)),
        fn_ssend, fn_srecv, fn_own, fn_ysend, fn_yrecv, fn_ysum, fn_zsend, fn_zrecv, fn_zsum,
        fn_xsend, fn_xrecv)
    edge_weights = Weights(
        ((edges, dpre), (sent, dpre), (recv, dpre)),
        fe_ssend, fe_srecv, fe_own, fe_ysend, fe_yrecv, fe_ysum, fe_zsend, fe_zrecv, fe_zsum,
        fe_xsend, fe_xrecv)
    out_weights = LastWeights(
        ((hid, dmsg),),
        fo_ssend, fo_srecv, fo_own, fo_zsend, fo_zrecv, fo_zsum, fo_ysend, fo_yrecv, fo_ysum,
        fo_xsend, fo_xrecv)

    for i in range(3):
        node_weights.products(i)
    for i in range(3):
        node_weights.to_y(i)
    for h in range(2):
        gather_dagg[h].relay()
    for h in range(2):
        gather_dagg[h].finish()

    def edge_backward(r0):
        rows = pl.ds(r0, 256)
        up = ecot[rows, :].astype(F32) + dot(pr[rows, :], dagg[...])
        gedge[rows, :] = up
        grad_msg = normalize_back(msg[rows, :], edge_gain, up).astype(BF)
        dmsg[rows, :] = grad_msg
        grad = (dot_nt(grad_msg, eout[...]) * swish_slope(pre[rows, :])).astype(BF)
        dpre[rows, :] = grad

    rows_loop(E, 256, edge_backward)

    def ghost_block(q):
        place = PN + ((q - d + DOM) % S) * SLAB
        return dot(pst[pl.ds(pl.multiple_of(place, SLAB), SLAB), :], dsent[...])

    out_weights.products(0)
    edge_weights.products(0)

    def send_grad(r0):
        rows = pl.ds(r0, 256)
        dsent[rows, :] = dot_nt(dpre[rows, :], ein[1]).astype(BF)

    rows_loop(E, 256, send_grad)
    out_weights.to_z()
    edge_weights.to_y(0)
    reduce_ghost = Scatter(ghost_block, gg_own, gg_ssend, gg_srecv, gg_xsend, gg_xrecv)
    reduce_ghost.start()
    edge_weights.products(1)
    reduce_ghost.middle()
    edge_weights.to_y(1)
    edge_weights.products(2)

    def recv_grad(r0):
        rows = pl.ds(r0, 256)
        drecv[rows, :] = dot_nt(dpre[rows, :], ein[2]).astype(BF)

    rows_loop(E, 256, recv_grad)
    edge_weights.to_y(2)

    def own_block(q):
        rows = pl.ds(pl.multiple_of(q * N, N), N)
        return dot(pst[rows, :], dsent[...]) + dot(prt[rows, :], drecv[...])

    reduce_own = Scatter(own_block, own_own, own_ssend, own_srecv, own_xsend, own_xrecv)
    reduce_own.start()
    for i in range(3):
        node_weights.to_z(i)
    a2_send[...] = reduce_ghost.finish().astype(BF)
    swap_back = Swap(a2_send, retg)
    swap_back.start()
    reduce_own.middle()

    def edge_grad(r0):
        rows = pl.ds(r0, 256)
        egrad_v[rows, :] = (gedge[rows, :] + dot_nt(dpre[rows, :], ein[0])).astype(BF)

    rows_loop(E, 256, edge_grad)
    stores[2].start()
    place = hot(lax.broadcasted_iota(jnp.int32, (S * SLAB, N), 1) + s * N == lists_c)
    swap_back.finish()
    gather_back = Gather(retg, lambda q: ((q - d + DOM) % S) * SLAB, SLAB)
    gather_back.start(retg.at[pl.ds(pl.multiple_of(t_mine * SLAB, SLAB), SLAB), :])
    edge_weights.to_z(0)
    out_weights.to_y()
    node_weights.to_x()
    edge_weights.to_z(1)
    gather_back.relay()
    edge_weights.to_z(2)
    out_weights.to_x()
    gather_back.finish()
    direct = gdirect[...] + dot_tn(place, retg[...])
    edge_weights.to_x()
    ngrad[...] = (direct + reduce_own.finish()).astype(BF)

    s_fin, r_fin = sems.take(6), sems.take(4)

    def fin_copy(group, i, slot, half):
        to = jnp.minimum(owner(group, i)[0], DOM * S - 1)
        return remote(
            fin.at[group], rows_in.at[slot, half], s_fin(3 * group + i), r_fin(2 * slot + half),
            to // S, to % S)

    def hand_out(group):
        for i in range(3):
            to, at, valid = owner(group, i)
            for slot in range(2):
                for half in range(2):
                    here = valid & (at == slot) & (c == half)
                    pl.when(here & (to != lin))(fin_copy(group, i, slot, half).start)

                    @pl.when(here & (to == lin))
                    def _():
                        rows_in[slot, half] = fin[group]

    @pl.when(x < 3)
    def _():
        fin[1] = node_weights.finish()

    hand_out(1)

    @pl.when(x < 3)
    def _():
        fin[0] = edge_weights.finish()

    @pl.when(x == 3)
    def _():
        fin[0] = out_weights.finish()

    hand_out(0)
    for slot in range(2):
        for half in range(2):
            pl.when(from_other(slot, half))(fin_copy(0, 0, slot, half).wait_recv)
    shift = first_row % 16
    for choice in range(0, 16, 2):
        @pl.when(shift == choice)
        def _():
            split = min(16 - choice, OUT_ROWS)
            for half in range(2):
                cols = slice(half * HALF, (half + 1) * HALF)
                wout[:split, cols] = rows_in[0, half, choice:choice + split, :]
                if split < OUT_ROWS:
                    wout[split:, cols] = rows_in[1, half, :OUT_ROWS - split, :]

    for store in stores:
        store.wait()
    for cp in pending:
        cp.wait_send()
    node_weights.drain()
    edge_weights.drain()
    out_weights.drain()
    for group in range(2):
        for i in range(3):
            to, _, valid = owner(group, i)
            pl.when(valid & (to != lin))(fin_copy(group, i, 0, 0).wait_send)


def scratch():
    def bf(*shape):
        return pltpu.VMEM(shape, BF)

    def f32(*shape):
        return pltpu.VMEM(shape, F32)

    T = PN + S * SLAB

    def scatter(rows, *lead):
        return [
            bf(*lead, NX, rows, D), bf(*lead, NX, rows, D), bf(*lead, NX - 1, rows, D),
            bf(*lead, NX - 1, rows, D), f32(*lead, rows, D),
        ]

    def products(count):
        return [bf(count, D, HALF), bf(count, D, HALF), f32(count, D, HALF)]

    def weights():
        return [
            *products(3), bf(3, NY - 1, 128, HALF), bf(3, NY - 1, 128, HALF), f32(3, 128, HALF),
            bf(3, NZ - 1, 16, HALF), bf(3, NZ - 1, 16, HALF), f32(3, 16, HALF),
            bf(NX - 1, 16, HALF), bf(NX - 1, 16, HALF),
        ]

    return [
        bf(N, D), bf(E, D), bf(E, D),
        bf(E, D), bf(3, D, D), bf(D, D), bf(2, D, D), bf(D, D), bf(E, D),
        bf(E, T), bf(E, PN), bf(T, E), bf(PN, E), bf(T, D), f32(E, D), bf(E, D), bf(E, D),
        f32(E, D), f32(E, D), bf(E, D),
        bf(SLAB, D), *scatter(N // 2, 2),
        bf(N, D), f32(N, D), f32(N, D), bf(N, D), f32(N, D), bf(N, D), bf(N, D), bf(N, D), bf(PN, D),
        f32(E, D), bf(E, D), bf(E, D), bf(E, D), bf(E, D),
        *scatter(SLAB), bf(SLAB, D), bf(S * SLAB, D), *scatter(N),
        *weights(), *weights(),
        *products(1), bf(NZ - 1, 64, HALF), bf(NZ - 1, 64, HALF), f32(64, HALF),
        bf(NY - 1, 16, HALF), bf(NY - 1, 16, HALF), f32(16, HALF), bf(16, HALF), bf(NX - 1, 16, HALF),
        f32(2, 16, HALF), f32(2, 2, 16, HALF),
        pltpu.SemaphoreType.DMA((N_SEM,)),
    ]


def hand_over(a0, a1, a2, a3, w_in, b0, b1, b2, b3, w_out):
    for src, dst in ((a0, b0), (a1, b1), (a2, b2), (a3, b3)):
        dst[...] = src[...]
    for i in range(OUT_ROWS):
        w_out[:, i * D:(i + 1) * D] = w_in[i:i + 1, :]


def body(
    node_state, edge_state, senders, receivers, send_rows, edge_in, edge_out, edge_gain,
    node_in, node_out, node_gain, node_cot, edge_cot,
):
    vmem = pl.BlockSpec(memory_space=pltpu.VMEM)
    hbm = pl.BlockSpec(memory_space=pl.ANY)
    states = (
        jax.ShapeDtypeStruct((N, D), BF),
        jax.ShapeDtypeStruct((E, D), BF),
        jax.ShapeDtypeStruct((N, D), BF),
        jax.ShapeDtypeStruct((E, D), BF),
    )
    results = pl.pallas_call(
        kernel,
        out_shape=states + (jax.ShapeDtypeStruct((OUT_ROWS, D), F32),),
        in_specs=[vmem] * 7 + [hbm] * 6,
        out_specs=[hbm, hbm, vmem, hbm, vmem],
        scratch_shapes=scratch(),
        compiler_params=pltpu.CompilerParams(
            collective_id=0, has_side_effects=True, vmem_limit_bytes=60 * 1024 * 1024),
    )(
        node_state, senders.reshape(1, E), receivers.reshape(1, E),
        send_rows.transpose(0, 2, 1),
        edge_gain, node_gain, node_cot,
        edge_state, edge_in[0], edge_out[0], node_in[0], node_out[0], edge_cot,
    )
    return pl.pallas_call(
        hand_over,
        out_shape=states + (jax.ShapeDtypeStruct((1, OUT_ROWS * D), F32),),
        in_specs=[vmem] * 5,
        out_specs=[vmem] * 5,
    )(*results)


def solution(mesh):
    both = P(("dom", "esplit"), None)
    in_specs = (
        both, both, P(("dom", "esplit")), P(("dom", "esplit")), P("dom", None, None),
        P(), P(), P(), P(), P(), P(), both, both,
    )
    out_specs = (both, both, both, both, P(None, ("dom", "esplit")))
    return jax.shard_map(body, mesh=mesh, in_specs=in_specs, out_specs=out_specs, check_vma=False)
```

```python
import functools

import jax
import jax.numpy as jnp
from jax import lax
from jax.experimental import pallas as pl
from jax.experimental.pallas import tpu as pltpu
from jax.sharding import PartitionSpec as P

EPSILON = 1e-05
BF = jnp.bfloat16
F32 = jnp.float32
MESH = pl.DeviceIdType.MESH

NZ = 8
NY = 4
NX = 4
DOM = NY * NZ
S = NX * 2
D = 512
N = 128
PN = N * S
E = 512
GH = 16
SLAB = DOM // S * GH
NJ = DOM // S
HALF = D // 2
NMAT = 7
OUT_ROWS = 14
BLOCK = 512


def dot(a, b):
    return lax.dot_general(a, b, (((1,), (0,)), ((), ())), preferred_element_type=F32)


def dot_nt(a, b):
    return lax.dot_general(a, b, (((1,), (1,)), ((), ())), preferred_element_type=F32)


def dot_tn(a, b):
    return lax.dot_general(a, b, (((0,), (0,)), ((), ())), preferred_element_type=F32)


def normalize(values, gain):
    average = jnp.mean(values, axis=-1, keepdims=True)
    centered = values - average
    inv_scale = lax.rsqrt(jnp.mean(centered * centered, axis=-1, keepdims=True) + EPSILON)
    return gain * centered * inv_scale


def normalize_back(values, gain, upstream):
    average = jnp.mean(values, axis=-1, keepdims=True)
    centered = values - average
    inv_scale = lax.rsqrt(jnp.mean(centered * centered, axis=-1, keepdims=True) + EPSILON)
    scaled = centered * inv_scale
    grad_scaled = upstream * gain
    first = jnp.mean(grad_scaled, axis=-1, keepdims=True)
    second = jnp.mean(grad_scaled * scaled, axis=-1, keepdims=True)
    return inv_scale * (grad_scaled - first - scaled * second)


def swish(values):
    return values * jax.nn.sigmoid(values)


def swish_slope(values):
    sigma = jax.nn.sigmoid(values)
    return sigma * (1.0 + values * (1.0 - sigma))


def rows_loop(total, step, fn):
    def one(i, carry):
        fn(pl.multiple_of(i * step, step))
        return carry

    lax.fori_loop(0, total // step, one, 0)


class Sems:
    def __init__(self, ref):
        self.ref = ref
        self.used = 0

    def take(self, count):
        base = self.used
        self.used += count
        return lambda i: self.ref.at[base + i]


N_SEM = 340


def kernel(
    snd_row, rcv_row, snd_lists, egain, ngain,
    nodes_hbm, ncot_hbm, edges_hbm, ein_hbm, eout_hbm, nin_hbm, nout_hbm, ecot_hbm,
    nodes_out, edges_out, ngrad, egrad, wout,
    nodes_in, ncot, nodes_out_v, edges_out_v, egrad_v, edges, ein, eout, nin, nout, ecot,
    ps, pr, pst, prt, tbl, sent_acc, sent, recv, pre, msg, hid,
    gsend, aggs_send, aggs_recv, aggx_send, aggx_recv, agg_own,
    agg, npre, nmsg, nhid, gdirect, dnpre, dnmsg, dagg_own, dagg,
    gedge, dmsg, dpre, dsent, drecv,
    gg_ssend, gg_srecv, gg_xsend, gg_xrecv, gg_own, a2_send, retg,
    own_ssend, own_srecv, own_xsend, own_xrecv, own_own,
    fn_ssend, fn_srecv, fn_own, fn_ysend, fn_yrecv, fn_ysum, fn_zsend, fn_zrecv, fn_zsum, fn_xsend, fn_xrecv,
    fe_ssend, fe_srecv, fe_own, fe_ysend, fe_yrecv, fe_ysum, fe_zsend, fe_zrecv, fe_zsum, fe_xsend, fe_xrecv,
    fo_ssend, fo_srecv, fo_own, fo_zsend, fo_zrecv, fo_zsum, fo_ysend, fo_yrecv, fo_ysum, fo_xsend, fo_xrecv,
    fin, rows_in,
    sem_ref,
):
    d = lax.axis_index("dom")
    s = lax.axis_index("esplit")
    y = d // NZ
    z = d % NZ
    x = s // 2
    c = s % 2
    lin = d * S + s
    sib = s + 1 - 2 * c
    t_mine = (s - d + DOM) % S
    sems = Sems(sem_ref)
    pending = []

    def remote(src, dst, send_sem, recv_sem, dom, split):
        return pltpu.make_async_remote_copy(
            src_ref=src, dst_ref=dst, send_sem=send_sem, recv_sem=recv_sem,
            device_id=(dom, split), device_id_type=MESH,
        )

    bar = pltpu.get_barrier_semaphore()

    def greet(dom, split):
        pl.semaphore_signal(bar, inc=1, device_id=(dom, split), device_id_type=MESH)

    for k in range(1, S):
        greet(d, (s + k) % S)
    for k in range(1, NY):
        greet((y + k) % NY * NZ + z, s)
    for k in range(1, NZ):
        greet(y * NZ + (z + k) % NZ, s)
    for j in range(NJ):
        pl.when(t_mine + S * j != d)(functools.partial(greet, t_mine + S * j, s))
    first_row = OUT_ROWS * lin
    b_first = first_row // 16
    b_last = (first_row + OUT_ROWS - 1) // 16

    def holder(b, half):
        r = b % DOM
        return jnp.where(b // DOM == 3, r % NY * NZ + r // NY, r), (b // DOM) % NX * 2 + half

    def from_other(slot, half):
        dom, split = holder(b_first + slot, half)
        here = dom * S + split != lin
        return here if slot == 0 else here & (b_last != b_first)

    for slot in range(2):
        for half in range(2):
            dom, split = holder(b_first + slot, half)
            pl.when(from_other(slot, half))(functools.partial(greet, dom, split))

    lsem = sems.take(9)
    loads = [
        pltpu.make_async_copy(a, b, lsem(i))
        for i, (a, b) in enumerate(
            ((edges_hbm, edges), (ein_hbm, ein), (eout_hbm, eout), (nin_hbm, nin),
             (nout_hbm, nout), (ecot_hbm, ecot), (nodes_hbm, nodes_in), (ncot_hbm, ncot),
             (nodes_hbm, tbl.at[pl.ds(pl.multiple_of(s * N, N), N), :])))
    ]
    ssem = sems.take(3)
    stores = [
        pltpu.make_async_copy(a, b, ssem(i))
        for i, (a, b) in enumerate(
            ((edges_out_v, edges_out), (nodes_out_v, nodes_out), (egrad_v, egrad)))
    ]
    for load in loads:
        load.start()

    def owner(group, i):
        b = DOM * (x + NX * group) + (d if group else jnp.where(x == 3, z * NY + y, d))
        to = (16 * b) // OUT_ROWS + i
        valid = to <= (16 * b + 15) // OUT_ROWS
        if group:
            valid = valid & (x < NMAT - NX)
        return to, b - (OUT_ROWS * to) // 16, valid

    arrivals = (S - 1) + (NY - 1) + (NZ - 1)
    for j in range(NJ):
        arrivals = arrivals + jnp.where(t_mine + S * j != d, 1, 0)
    for group in range(2):
        for i in range(3):
            to, _, valid = owner(group, i)
            arrivals = arrivals + jnp.where(valid & (to != lin), 1, 0)
    pl.semaphore_wait(bar, arrivals)

    def on_x(dx):
        return (x + dx + NX) % NX * 2 + c

    class Gather:
        def __init__(self, buf, offset, rows):
            self.buf, self.offset, self.rows = buf, offset, rows
            self.ss, self.rs = sems.take(7), sems.take(7)

        def copy(self, k, origin, split, src=None):
            there = self.buf.at[pl.ds(pl.multiple_of(self.offset(origin), self.rows), self.rows), :]
            here = there if src is None else src
            return remote(here, there, self.ss(k), self.rs(k), d, split)

        def send(self, k, origin, split, src=None):
            cp = self.copy(k, origin, split, src)
            cp.start()
            pending.append(cp)

        def start(self, src):
            for dx in (2, 1, 3):
                self.send(dx - 1, s, on_x(dx), src)
            self.send(3, s, sib, src)

        def forward(self, dx):
            origin = on_x(-dx)
            self.copy(dx - 1, origin, sib).wait_recv()
            self.send(3 + dx, origin, sib)

        def relay(self):
            self.forward(1)
            self.forward(3)

        def finish(self):
            self.forward(2)
            self.copy(3, sib, sib).wait_recv()
            for dx in (1, 3, 2):
                self.copy(3 + dx, on_x(-dx) + 1 - 2 * c, sib).wait_recv()

    class Scatter:
        def __init__(self, compute, own, ssend, srecv, xsend, xrecv):
            self.compute, self.own = compute, own
            self.ssend, self.srecv, self.xsend, self.xrecv = ssend, srecv, xsend, xrecv
            self.s1, self.r1 = sems.take(4), sems.take(4)
            self.s2, self.r2 = sems.take(3), sems.take(3)

        def to_sib(self, dx):
            return remote(self.ssend.at[dx], self.srecv.at[dx], self.s1(dx), self.r1(dx), d, sib)

        def to_chip(self, dx):
            return remote(
                self.xsend.at[dx - 1], self.xrecv.at[dx - 1], self.s2(dx - 1), self.r2(dx - 1),
                d, on_x(dx))

        def start(self):
            for dx in (2, 1, 3, 0):
                self.ssend[dx] = self.compute((x + dx) % NX * 2 + 1 - c).astype(BF)
                cp = self.to_sib(dx)
                cp.start()
                pending.append(cp)

        def middle(self):
            for dx in (2, 1, 3):
                mine = self.compute(on_x(dx))
                self.to_sib(dx).wait_recv()
                self.xsend[dx - 1] = (mine + self.srecv[dx].astype(F32)).astype(BF)
                cp = self.to_chip(dx)
                cp.start()
                pending.append(cp)
            mine = self.compute(s)
            self.to_sib(0).wait_recv()
            self.own[...] = mine + self.srecv[0].astype(F32)

        def finish(self):
            total = self.own[...]
            for dx in (1, 3, 2):
                self.to_chip(dx).wait_recv()
                total = total + self.xrecv[dx - 1].astype(F32)
            return total

    class Swap:
        def __init__(self, src, dst):
            self.src, self.dst = src, dst
            self.ss, self.rs = sems.take(NJ), sems.take(NJ)

        def start(self):
            for j in range(NJ):
                peer = t_mine + S * j
                land = pl.multiple_of((d % S) * SLAB + (d // S) * GH, GH)
                cp = remote(
                    self.src.at[pl.ds(j * GH, GH), :], self.dst.at[pl.ds(land, GH), :],
                    self.ss(j), self.rs(d // S), peer, s)
                pl.when(peer != d)(cp.start)

                @pl.when(peer == d)
                def _():
                    self.dst[pl.ds(land, GH), :] = self.src[pl.ds(j * GH, GH), :]

        def finish(self):
            for j in range(NJ):
                peer = t_mine + S * j
                land = pl.multiple_of(t_mine * SLAB + j * GH, GH)
                cp = remote(
                    self.src.at[pl.ds(j * GH, GH), :], self.dst.at[pl.ds(land, GH), :],
                    self.ss(j), self.rs(j), peer, s)

                @pl.when(peer != d)
                def _():
                    cp.wait_recv()
                    cp.wait_send()

    gather_nodes = Gather(tbl, lambda q: q * N, N)
    gather_nodes.start(nodes_hbm)

    def permuted(values):
        ghost = values - PN
        part = ghost // GH
        place = PN + (part % S) * SLAB + (part // S) * GH + ghost % GH
        return jnp.where(values >= PN, place, values)

    def column(row):
        size = row.shape[1]
        hit = lax.broadcasted_iota(jnp.int32, (size, size), 0) == lax.broadcasted_iota(
            jnp.int32, (size, size), 1)
        return jnp.sum(jnp.where(hit, row.astype(F32), 0.0), axis=1, keepdims=True).astype(jnp.int32)

    def hot(mask):
        return jnp.where(mask, 1.0, 0.0).astype(BF)

    send_r = permuted(snd_row[...])
    recv_r = rcv_row[...]
    send_c = column(send_r)
    recv_c = column(recv_r)

    def build_t(r0):
        ids = lax.broadcasted_iota(jnp.int32, (256, E), 0) + r0
        pst[pl.ds(r0, 256), :] = hot(ids == send_r)

    rows_loop(PN + S * SLAB, 256, build_t)

    def build_rt(r0):
        ids = lax.broadcasted_iota(jnp.int32, (256, E), 0) + r0
        prt[pl.ds(r0, 256), :] = hot(ids == recv_r)

    rows_loop(PN, 256, build_rt)
    for c0 in range(0, PN + S * SLAB, 256):
        ids = lax.broadcasted_iota(jnp.int32, (E, 256), 1) + c0
        ps[:, c0:c0 + 256] = hot(ids == send_c)
        if c0 < PN:
            pr[:, c0:c0 + 256] = hot(ids == recv_c)

    lists = snd_lists[0]
    slot = lax.broadcasted_iota(jnp.int32, (S * SLAB, DOM), 0)
    part = slot // SLAB + (slot // GH) % NJ * S
    rows = hot(lax.broadcasted_iota(jnp.int32, (S * SLAB, DOM), 1) == part)
    high = dot_nt(rows, (lists // 32).astype(F32).astype(BF))
    low = dot_nt(rows, (lists % 32).astype(F32).astype(BF))
    slot = lax.broadcasted_iota(jnp.int32, (S * SLAB, GH), 0)
    here = lax.broadcasted_iota(jnp.int32, (S * SLAB, GH), 1) == slot % GH
    lists_c = jnp.sum(
        jnp.where(here, high * 32.0 + low, 0.0), axis=1, keepdims=True).astype(jnp.int32)

    loads[0].wait()
    loads[1].wait()

    def edge_part(r0):
        rows = pl.ds(r0, BLOCK)
        pre[rows, :] = dot(edges[rows, :], ein[0])

    rows_loop(E, BLOCK, edge_part)

    loads[8].wait()
    gather_nodes.relay()
    gather_nodes.finish()

    hit = jnp.zeros((SLAB, 1), jnp.int32)
    for t in range(S):
        hit = jnp.where(t_mine == t, lists_c[t * SLAB:(t + 1) * SLAB, :], hit)
    pick = hot(lax.broadcasted_iota(jnp.int32, (SLAB, PN), 1) == hit)
    gsend[...] = dot(pick, tbl[:PN, :]).astype(BF)
    ghosts = tbl.at[pl.ds(PN, S * SLAB), :]
    swap_ghost = Swap(gsend, ghosts)
    swap_ghost.start()

    def gather_recv(r0):
        rows = pl.ds(r0, BLOCK)
        got = dot(pr[rows, :], tbl[:PN, :]).astype(BF)
        recv[rows, :] = got
        pre[rows, :] = pre[rows, :] + dot(got, ein[2])

    rows_loop(E, BLOCK, gather_recv)
    swap_ghost.finish()
    gather_ghost = Gather(ghosts, lambda q: ((q - d + DOM) % S) * SLAB, SLAB)
    gather_ghost.start(ghosts.at[pl.ds(pl.multiple_of(t_mine * SLAB, SLAB), SLAB), :])

    def gather_sent(r0):
        rows = pl.ds(r0, BLOCK)
        sent_acc[rows, :] = dot(ps[rows, :PN], tbl[:PN, :])

    rows_loop(E, BLOCK, gather_sent)
    gather_ghost.relay()
    gather_ghost.finish()

    loads[2].wait()
    edge_gain = egain[...]

    def edge_forward(r0):
        rows = pl.ds(r0, BLOCK)
        got = (sent_acc[rows, :] + dot(ps[rows, PN:], tbl[PN:, :])).astype(BF)
        sent[rows, :] = got
        act = pre[rows, :] + dot(got, ein[1])
        pre[rows, :] = act
        hidden = swish(act).astype(BF)
        hid[rows, :] = hidden
        message = dot(hidden, eout[...])
        msg[rows, :] = message
        edges_out_v[rows, :] = (edges[rows, :].astype(F32) + normalize(message, edge_gain)).astype(BF)

    rows_loop(E, BLOCK, edge_forward)

    NH = N // 2

    def agg_block(half):
        def block(q):
            return dot(prt[pl.ds(pl.multiple_of(q * N + half * NH, NH), NH), :], edges_out_v[...])

        return block

    reduce_agg = [
        Scatter(agg_block(h), agg_own.at[h], aggs_send.at[h], aggs_recv.at[h], aggx_send.at[h],
                aggx_recv.at[h])
        for h in range(2)
    ]
    gather_dagg = [
        Gather(dagg, functools.partial(lambda h, q: q * N + h * NH, h), NH) for h in range(2)
    ]
    for h in range(2):
        reduce_agg[h].start()
    for h in range(2):
        reduce_agg[h].middle()
    stores[0].start()
    loads[3].wait()
    loads[4].wait()
    loads[5].wait()
    loads[6].wait()
    loads[7].wait()
    npre[...] = dot(nodes_in[...], nin[0])
    node_gain = ngain[...]

    for h in range(2):
        rows = slice(h * NH, (h + 1) * NH)
        sums = reduce_agg[h].finish().astype(BF)
        agg[rows, :] = sums
        act = npre[rows, :] + dot(sums, nin[1])
        npre[rows, :] = act
        hidden = swish(act).astype(BF)
        nhid[rows, :] = hidden
        message = dot(hidden, nout[...])
        nmsg[rows, :] = message
        upstream = ncot[rows, :].astype(F32)
        grad_message = normalize_back(message, node_gain, upstream).astype(BF)
        dnmsg[rows, :] = grad_message
        grad_pre = (dot_nt(grad_message, nout[...]) * swish_slope(act)).astype(BF)
        dnpre[rows, :] = grad_pre
        dagg_own[rows, :] = dot_nt(grad_pre, nin[1]).astype(BF)
        dagg[pl.ds(pl.multiple_of(s * N + h * NH, NH), NH), :] = dagg_own[rows, :]
        gather_dagg[h].start(dagg_own.at[rows, :])
    gdirect[...] = ncot[...].astype(F32) + dot_nt(dnpre[...], nin[0])
    nodes_out_v[...] = (
        nodes_in[...].astype(F32) + normalize(nmsg[...], node_gain)).astype(BF)
    stores[1].start()

    mine_cols = pl.ds(pl.multiple_of(c * HALF, HALF), HALF)
    sib_cols = pl.ds(pl.multiple_of((1 - c) * HALF, HALF), HALF)

    class Products:
        def __init__(self, pairs, ssend, srecv, own):
            self.pairs, self.ssend, self.srecv, self.own = pairs, ssend, srecv, own
            self.s0, self.r0 = sems.take(len(pairs)), sems.take(len(pairs))

        def sib_copy(self, i):
            return remote(self.ssend.at[i], self.srecv.at[i], self.s0(i), self.r0(i), d, sib)

        def products(self, i):
            left, right = self.pairs[i]
            columns = jnp.concatenate([right[:, sib_cols], right[:, mine_cols]], axis=1)
            grad = dot_tn(left[...], columns)
            self.ssend[i] = grad[:, :HALF].astype(BF)
            cp = self.sib_copy(i)
            cp.start()
            pending.append(cp)
            self.own[i] = grad[:, HALF:]

        def chip_sum(self, i, rows):
            return self.own[i, rows, :] + self.srecv[i, rows, :].astype(F32)

    class Peers:
        def __init__(self, count, send, recv, to):
            self.count, self.sbuf, self.rbuf, self.to = count, send, recv, to
            self.ss, self.rs = sems.take(count - 1), sems.take(count - 1)

        def copy(self, k):
            return remote(
                self.sbuf.at[k - 1], self.rbuf.at[k - 1], self.ss(k - 1), self.rs(k - 1),
                *self.to(k))

        def send(self, k, value):
            self.sbuf[k - 1] = value.astype(BF)
            cp = self.copy(k)
            cp.start()
            pending.append(cp)

        def total(self, mine):
            for k in range(1, self.count):
                self.copy(k).wait_recv()
                mine = mine + self.rbuf[k - 1].astype(F32)
            return mine

    def on_y(k):
        return (y + k) % NY * NZ + z, s

    def on_z(k):
        return y * NZ + (z + k) % NZ, s

    Z_ORDER = (4, 3, 5, 2, 6, 1, 7)

    class Weights(Products):
        def __init__(self, pairs, ssend, srecv, own, ysend, yrecv, ysum, zsend, zrecv, zsum, xsend, xrecv):
            super().__init__(pairs, ssend, srecv, own)
            self.y = [Peers(NY, ysend.at[i], yrecv.at[i], on_y) for i in range(3)]
            self.z = [Peers(NZ, zsend.at[i], zrecv.at[i], on_z) for i in range(3)]
            self.ysum, self.zsum, self.xsend, self.xrecv = ysum, zsum, xsend, xrecv
            self.sx, self.rx = sems.take(NX - 1), sems.take(NX - 1)

        def to_y(self, i):
            self.sib_copy(i).wait_recv()
            for k in (2, 1, 3):
                rows = pl.ds(pl.multiple_of((y + k) % NY * 128, 128), 128)
                self.y[i].send(k, self.chip_sum(i, rows))

        def to_z(self, i):
            rows = pl.ds(pl.multiple_of(y * 128, 128), 128)
            self.ysum[i] = self.y[i].total(self.chip_sum(i, rows))
            for k in Z_ORDER:
                rows = pl.ds(pl.multiple_of((z + k) % NZ * 16, 16), 16)
                self.z[i].send(k, self.ysum[i, rows, :])

        def x_copy(self, k):
            return remote(
                self.xsend.at[k - 1], self.xrecv.at[k - 1], self.sx(k - 1), self.rx(k - 1),
                d, on_x(k))

        def to_x(self):
            rows = pl.ds(pl.multiple_of(z * 16, 16), 16)
            for i in range(3):
                self.zsum[i] = self.z[i].total(self.ysum[i, rows, :])
            for k in (2, 1, 3):
                @pl.when((x + k) % NX < 3)
                def _():
                    self.xsend[k - 1] = self.zsum[(x + k) % NX].astype(BF)
                    self.x_copy(k).start()

        def finish(self):
            total = self.zsum[jnp.minimum(x, 2)]
            for k in (1, 3, 2):
                self.x_copy(k).wait_recv()
                total = total + self.xrecv[k - 1].astype(F32)
            return total

        def drain(self):
            for k in (2, 1, 3):
                pl.when((x + k) % NX < 3)(self.x_copy(k).wait_send)

    class LastWeights(Products):
        def __init__(self, pairs, ssend, srecv, own, zsend, zrecv, zsum, ysend, yrecv, ysum, xsend, xrecv):
            super().__init__(pairs, ssend, srecv, own)
            self.zsum, self.ysum, self.xsend, self.xrecv = zsum, ysum, xsend, xrecv
            self.z = Peers(NZ, zsend, zrecv, on_z)
            self.y = Peers(NY, ysend, yrecv, on_y)
            self.sx, self.rx = sems.take(1), sems.take(3)

        def to_z(self):
            self.sib_copy(0).wait_recv()
            for k in Z_ORDER:
                rows = pl.ds(pl.multiple_of((z + k) % NZ * 64, 64), 64)
                self.z.send(k, self.chip_sum(0, rows))

        def to_y(self):
            rows = pl.ds(pl.multiple_of(z * 64, 64), 64)
            self.zsum[...] = self.z.total(self.chip_sum(0, rows))
            for k in (2, 1, 3):
                rows = pl.ds(pl.multiple_of((y + k) % NY * 16, 16), 16)
                self.y.send(k, self.zsum[rows, :])

        def x_copy(self, k):
            return remote(self.xsend, self.xrecv.at[k], self.sx(0), self.rx(k), d, 6 + c)

        def to_x(self):
            total = self.y.total(self.zsum[pl.ds(pl.multiple_of(y * 16, 16), 16), :])
            self.ysum[...] = total
            self.xsend[...] = total.astype(BF)
            for k in range(3):
                pl.when(x == k)(self.x_copy(k).start)

        def finish(self):
            total = self.ysum[...]
            for k in range(3):
                self.x_copy(k).wait_recv()
                total = total + self.xrecv[k].astype(F32)
            return total

        def drain(self):
            pl.when(x < 3)(self.x_copy(0).wait_send)

    node_weights = Weights(
        ((nodes_in, dnpre), (agg, dnpre), (nhid, dnmsg)),
        fn_ssend, fn_srecv, fn_own, fn_ysend, fn_yrecv, fn_ysum, fn_zsend, fn_zrecv, fn_zsum,
        fn_xsend, fn_xrecv)
    edge_weights = Weights(
        ((edges, dpre), (sent, dpre), (recv, dpre)),
        fe_ssend, fe_srecv, fe_own, fe_ysend, fe_yrecv, fe_ysum, fe_zsend, fe_zrecv, fe_zsum,
        fe_xsend, fe_xrecv)
    out_weights = LastWeights(
        ((hid, dmsg),),
        fo_ssend, fo_srecv, fo_own, fo_zsend, fo_zrecv, fo_zsum, fo_ysend, fo_yrecv, fo_ysum,
        fo_xsend, fo_xrecv)

    for i in range(3):
        node_weights.products(i)
    for i in range(3):
        node_weights.to_y(i)
    for h in range(2):
        gather_dagg[h].relay()
    for h in range(2):
        gather_dagg[h].finish()

    def edge_backward(r0):
        rows = pl.ds(r0, BLOCK)
        up = ecot[rows, :].astype(F32) + dot(pr[rows, :], dagg[...])
        gedge[rows, :] = up
        grad_msg = normalize_back(msg[rows, :], edge_gain, up).astype(BF)
        dmsg[rows, :] = grad_msg
        grad = (dot_nt(grad_msg, eout[...]) * swish_slope(pre[rows, :])).astype(BF)
        dpre[rows, :] = grad

    rows_loop(E, BLOCK, edge_backward)

    def ghost_block(q):
        place = PN + ((q - d + DOM) % S) * SLAB
        return dot(pst[pl.ds(pl.multiple_of(place, SLAB), SLAB), :], dsent[...])

    out_weights.products(0)
    edge_weights.products(0)

    def send_grad(r0):
        rows = pl.ds(r0, BLOCK)
        dsent[rows, :] = dot_nt(dpre[rows, :], ein[1]).astype(BF)

    rows_loop(E, BLOCK, send_grad)
    out_weights.to_z()
    edge_weights.to_y(0)
    reduce_ghost = Scatter(ghost_block, gg_own, gg_ssend, gg_srecv, gg_xsend, gg_xrecv)
    reduce_ghost.start()
    edge_weights.products(1)
    reduce_ghost.middle()
    edge_weights.to_y(1)
    edge_weights.products(2)

    def recv_grad(r0):
        rows = pl.ds(r0, BLOCK)
        drecv[rows, :] = dot_nt(dpre[rows, :], ein[2]).astype(BF)

    rows_loop(E, BLOCK, recv_grad)
    edge_weights.to_y(2)

    def own_block(q):
        rows = pl.ds(pl.multiple_of(q * N, N), N)
        return dot(pst[rows, :], dsent[...]) + dot(prt[rows, :], drecv[...])

    reduce_own = Scatter(own_block, own_own, own_ssend, own_srecv, own_xsend, own_xrecv)
    reduce_own.start()
    for i in range(3):
        node_weights.to_z(i)
    a2_send[...] = reduce_ghost.finish().astype(BF)
    swap_back = Swap(a2_send, retg)
    swap_back.start()
    reduce_own.middle()

    def edge_grad(r0):
        rows = pl.ds(r0, BLOCK)
        egrad_v[rows, :] = (gedge[rows, :] + dot_nt(dpre[rows, :], ein[0])).astype(BF)

    rows_loop(E, BLOCK, edge_grad)
    stores[2].start()
    place = hot(lax.broadcasted_iota(jnp.int32, (S * SLAB, N), 1) + s * N == lists_c)
    swap_back.finish()
    gather_back = Gather(retg, lambda q: ((q - d + DOM) % S) * SLAB, SLAB)
    gather_back.start(retg.at[pl.ds(pl.multiple_of(t_mine * SLAB, SLAB), SLAB), :])
    edge_weights.to_z(0)
    out_weights.to_y()
    node_weights.to_x()
    edge_weights.to_z(1)
    edge_weights.to_z(2)
    gather_back.relay()
    out_weights.to_x()
    edge_weights.to_x()
    gather_back.finish()
    direct = gdirect[...] + dot_tn(place, retg[...])
    ngrad[...] = (direct + reduce_own.finish()).astype(BF)

    s_fin, r_fin = sems.take(6), sems.take(4)

    def fin_copy(group, i, slot, half):
        to = jnp.minimum(owner(group, i)[0], DOM * S - 1)
        return remote(
            fin.at[group], rows_in.at[slot, half], s_fin(3 * group + i), r_fin(2 * slot + half),
            to // S, to % S)

    def hand_out(group):
        for i in range(3):
            to, at, valid = owner(group, i)
            for slot in range(2):
                for half in range(2):
                    here = valid & (at == slot) & (c == half)
                    pl.when(here & (to != lin))(fin_copy(group, i, slot, half).start)

                    @pl.when(here & (to == lin))
                    def _():
                        rows_in[slot, half] = fin[group]

    @pl.when(x < 3)
    def _():
        fin[1] = node_weights.finish()

    hand_out(1)

    @pl.when(x < 3)
    def _():
        fin[0] = edge_weights.finish()

    @pl.when(x == 3)
    def _():
        fin[0] = out_weights.finish()

    hand_out(0)
    for slot in range(2):
        for half in range(2):
            pl.when(from_other(slot, half))(fin_copy(0, 0, slot, half).wait_recv)
    shift = first_row % 16
    for choice in range(0, 16, 2):
        @pl.when(shift == choice)
        def _():
            split = min(16 - choice, OUT_ROWS)
            for half in range(2):
                cols = slice(half * HALF, (half + 1) * HALF)
                wout[:split, cols] = rows_in[0, half, choice:choice + split, :]
                if split < OUT_ROWS:
                    wout[split:, cols] = rows_in[1, half, :OUT_ROWS - split, :]

    for store in stores:
        store.wait()
    for cp in pending:
        cp.wait_send()
    node_weights.drain()
    edge_weights.drain()
    out_weights.drain()
    for group in range(2):
        for i in range(3):
            to, _, valid = owner(group, i)
            pl.when(valid & (to != lin))(fin_copy(group, i, 0, 0).wait_send)


def scratch():
    def bf(*shape):
        return pltpu.VMEM(shape, BF)

    def f32(*shape):
        return pltpu.VMEM(shape, F32)

    T = PN + S * SLAB

    def scatter(rows, *lead):
        return [
            bf(*lead, NX, rows, D), bf(*lead, NX, rows, D), bf(*lead, NX - 1, rows, D),
            bf(*lead, NX - 1, rows, D), f32(*lead, rows, D),
        ]

    def products(count):
        return [bf(count, D, HALF), bf(count, D, HALF), f32(count, D, HALF)]

    def weights():
        return [
            *products(3), bf(3, NY - 1, 128, HALF), bf(3, NY - 1, 128, HALF), f32(3, 128, HALF),
            bf(3, NZ - 1, 16, HALF), bf(3, NZ - 1, 16, HALF), f32(3, 16, HALF),
            bf(NX - 1, 16, HALF), bf(NX - 1, 16, HALF),
        ]

    return [
        bf(N, D), bf(N, D), bf(N, D), bf(E, D), bf(E, D),
        bf(E, D), bf(3, D, D), bf(D, D), bf(2, D, D), bf(D, D), bf(E, D),
        bf(E, T), bf(E, PN), bf(T, E), bf(PN, E), bf(T, D), f32(E, D), bf(E, D), bf(E, D),
        f32(E, D), f32(E, D), bf(E, D),
        bf(SLAB, D), *scatter(N // 2, 2),
        bf(N, D), f32(N, D), f32(N, D), bf(N, D), f32(N, D), bf(N, D), bf(N, D), bf(N, D), bf(PN, D),
        f32(E, D), bf(E, D), bf(E, D), bf(E, D), bf(E, D),
        *scatter(SLAB), bf(SLAB, D), bf(S * SLAB, D), *scatter(N),
        *weights(), *weights(),
        *products(1), bf(NZ - 1, 64, HALF), bf(NZ - 1, 64, HALF), f32(64, HALF),
        bf(NY - 1, 16, HALF), bf(NY - 1, 16, HALF), f32(16, HALF), bf(16, HALF), bf(NX - 1, 16, HALF),
        f32(2, 16, HALF), f32(2, 2, 16, HALF),
        pltpu.SemaphoreType.DMA((N_SEM,)),
    ]


def hand_over(a0, a1, a2, a3, w_in, b0, b1, b2, b3, w_out):
    for src, dst in ((a0, b0), (a1, b1), (a2, b2), (a3, b3)):
        dst[...] = src[...]
    for i in range(OUT_ROWS):
        w_out[:, i * D:(i + 1) * D] = w_in[i:i + 1, :]


def body(
    node_state, edge_state, senders, receivers, send_rows, edge_in, edge_out, edge_gain,
    node_in, node_out, node_gain, node_cot, edge_cot,
):
    vmem = pl.BlockSpec(memory_space=pltpu.VMEM)
    hbm = pl.BlockSpec(memory_space=pl.ANY)
    states = (
        jax.ShapeDtypeStruct((N, D), BF),
        jax.ShapeDtypeStruct((E, D), BF),
        jax.ShapeDtypeStruct((N, D), BF),
        jax.ShapeDtypeStruct((E, D), BF),
    )
    results = pl.pallas_call(
        kernel,
        out_shape=states + (jax.ShapeDtypeStruct((OUT_ROWS, D), F32),),
        in_specs=[vmem] * 5 + [hbm] * 8,
        out_specs=[hbm, hbm, vmem, hbm, vmem],
        scratch_shapes=scratch(),
        compiler_params=pltpu.CompilerParams(
            collective_id=0, has_side_effects=True, vmem_limit_bytes=60 * 1024 * 1024),
    )(
        senders.reshape(1, E), receivers.reshape(1, E), send_rows.transpose(0, 2, 1),
        edge_gain, node_gain,
        node_state, node_cot, edge_state, edge_in[0], edge_out[0], node_in[0], node_out[0], edge_cot,
    )
    return pl.pallas_call(
        hand_over,
        out_shape=states + (jax.ShapeDtypeStruct((1, OUT_ROWS * D), F32),),
        in_specs=[vmem] * 5,
        out_specs=[vmem] * 5,
    )(*results)


def solution(mesh):
    both = P(("dom", "esplit"), None)
    in_specs = (
        both, both, P(("dom", "esplit")), P(("dom", "esplit")), P("dom", None, None),
        P(), P(), P(), P(), P(), P(), both, both,
    )
    out_specs = (both, both, both, both, P(None, ("dom", "esplit")))
    return jax.shard_map(body, mesh=mesh, in_specs=in_specs, out_specs=out_specs, check_vma=False)
```

```python
import functools

import jax
import jax.numpy as jnp
from jax import lax
from jax.experimental import pallas as pl
from jax.experimental.pallas import tpu as pltpu
from jax.sharding import PartitionSpec as P

EPSILON = 1e-05
BF = jnp.bfloat16
F32 = jnp.float32
MESH = pl.DeviceIdType.MESH

NZ = 8
NY = 4
NX = 4
DOM = NY * NZ
S = NX * 2
D = 512
N = 128
PN = N * S
E = 512
GH = 16
SLAB = DOM // S * GH
NJ = DOM // S
HALF = D // 2
NMAT = 7
OUT_ROWS = 14
BLOCK = 512


def dot(a, b):
    return lax.dot_general(a, b, (((1,), (0,)), ((), ())), preferred_element_type=F32)


def dot_nt(a, b):
    return lax.dot_general(a, b, (((1,), (1,)), ((), ())), preferred_element_type=F32)


def dot_tn(a, b):
    return lax.dot_general(a, b, (((0,), (0,)), ((), ())), preferred_element_type=F32)


def normalize(values, gain):
    average = jnp.mean(values, axis=-1, keepdims=True)
    centered = values - average
    inv_scale = lax.rsqrt(jnp.mean(centered * centered, axis=-1, keepdims=True) + EPSILON)
    return gain * centered * inv_scale


def normalize_back(values, gain, upstream):
    average = jnp.mean(values, axis=-1, keepdims=True)
    centered = values - average
    inv_scale = lax.rsqrt(jnp.mean(centered * centered, axis=-1, keepdims=True) + EPSILON)
    scaled = centered * inv_scale
    grad_scaled = upstream * gain
    first = jnp.mean(grad_scaled, axis=-1, keepdims=True)
    second = jnp.mean(grad_scaled * scaled, axis=-1, keepdims=True)
    return inv_scale * (grad_scaled - first - scaled * second)


def swish(values):
    return values * jax.nn.sigmoid(values)


def swish_slope(values):
    sigma = jax.nn.sigmoid(values)
    return sigma * (1.0 + values * (1.0 - sigma))


def rows_loop(total, step, fn):
    def one(i, carry):
        fn(pl.multiple_of(i * step, step))
        return carry

    lax.fori_loop(0, total // step, one, 0)


class Sems:
    def __init__(self, ref):
        self.ref = ref
        self.used = 0

    def take(self, count):
        base = self.used
        self.used += count
        return lambda i: self.ref.at[base + i]


N_SEM = 340


def kernel(
    snd_row, rcv_row, snd_lists, egain, ngain,
    nodes_hbm, ncot_hbm, edges_hbm, ein_hbm, eout_hbm, nin_hbm, nout_hbm, ecot_hbm,
    nodes_out, edges_out, ngrad, egrad, wout,
    nodes_in, ncot, nodes_out_v, edges_out_v, egrad_v, edges, ein, eout, nin, nout, ecot,
    ps, pr, pst, prt, tbl, sent_acc, sent, recv, pre, msg, hid,
    gsend, aggs_send, aggs_recv, aggx_send, aggx_recv, agg_own,
    agg, npre, nmsg, nhid, gdirect, dnpre, dnmsg, dagg_own, dagg,
    gedge, dmsg, dpre, dsent, drecv,
    gg_ssend, gg_srecv, gg_xsend, gg_xrecv, gg_own, a2_send, retg,
    own_ssend, own_srecv, own_xsend, own_xrecv, own_own,
    fn_ssend, fn_srecv, fn_own, fn_ysend, fn_yrecv, fn_ysum, fn_zsend, fn_zrecv, fn_zsum, fn_xsend, fn_xrecv,
    fe_ssend, fe_srecv, fe_own, fe_ysend, fe_yrecv, fe_ysum, fe_zsend, fe_zrecv, fe_zsum, fe_xsend, fe_xrecv,
    fo_ssend, fo_srecv, fo_own, fo_zsend, fo_zrecv, fo_zsum, fo_ysend, fo_yrecv, fo_ysum, fo_xsend, fo_xrecv,
    fin, rows_in,
    sem_ref,
):
    d = lax.axis_index("dom")
    s = lax.axis_index("esplit")
    y = d // NZ
    z = d % NZ
    x = s // 2
    c = s % 2
    lin = d * S + s
    sib = s + 1 - 2 * c
    t_mine = (s - d + DOM) % S
    sems = Sems(sem_ref)
    pending = []

    def remote(src, dst, send_sem, recv_sem, dom, split):
        return pltpu.make_async_remote_copy(
            src_ref=src, dst_ref=dst, send_sem=send_sem, recv_sem=recv_sem,
            device_id=(dom, split), device_id_type=MESH,
        )

    bar = pltpu.get_barrier_semaphore()

    def greet(dom, split):
        pl.semaphore_signal(bar, inc=1, device_id=(dom, split), device_id_type=MESH)

    for k in range(1, S):
        greet(d, (s + k) % S)
    for k in range(1, NY):
        greet((y + k) % NY * NZ + z, s)
    for k in range(1, NZ):
        greet(y * NZ + (z + k) % NZ, s)
    for j in range(NJ):
        pl.when(t_mine + S * j != d)(functools.partial(greet, t_mine + S * j, s))
    first_row = OUT_ROWS * lin
    b_first = first_row // 16
    b_last = (first_row + OUT_ROWS - 1) // 16

    def holder(b, half):
        r = b % DOM
        return jnp.where(b // DOM == 3, r % NY * NZ + r // NY, r), (b // DOM) % NX * 2 + half

    def from_other(slot, half):
        dom, split = holder(b_first + slot, half)
        here = dom * S + split != lin
        return here if slot == 0 else here & (b_last != b_first)

    for slot in range(2):
        for half in range(2):
            dom, split = holder(b_first + slot, half)
            pl.when(from_other(slot, half))(functools.partial(greet, dom, split))

    lsem = sems.take(9)
    loads = [
        pltpu.make_async_copy(a, b, lsem(i))
        for i, (a, b) in enumerate(
            ((edges_hbm, edges), (ein_hbm, ein), (eout_hbm, eout), (nin_hbm, nin),
             (nout_hbm, nout), (ecot_hbm, ecot), (nodes_hbm, nodes_in), (ncot_hbm, ncot),
             (nodes_hbm, tbl.at[pl.ds(pl.multiple_of(s * N, N), N), :])))
    ]
    ssem = sems.take(3)
    stores = [
        pltpu.make_async_copy(a, b, ssem(i))
        for i, (a, b) in enumerate(
            ((edges_out_v, edges_out), (nodes_out_v, nodes_out), (egrad_v, egrad)))
    ]

    def owner(group, i):
        b = DOM * (x + NX * group) + (d if group else jnp.where(x == 3, z * NY + y, d))
        to = (16 * b) // OUT_ROWS + i
        valid = to <= (16 * b + 15) // OUT_ROWS
        if group:
            valid = valid & (x < NMAT - NX)
        return to, b - (OUT_ROWS * to) // 16, valid

    arrivals = (S - 1) + (NY - 1) + (NZ - 1)
    for j in range(NJ):
        arrivals = arrivals + jnp.where(t_mine + S * j != d, 1, 0)
    for group in range(2):
        for i in range(3):
            to, _, valid = owner(group, i)
            arrivals = arrivals + jnp.where(valid & (to != lin), 1, 0)
    pl.semaphore_wait(bar, arrivals)

    def on_x(dx):
        return (x + dx + NX) % NX * 2 + c

    class Gather:
        def __init__(self, buf, offset, rows):
            self.buf, self.offset, self.rows = buf, offset, rows
            self.ss, self.rs = sems.take(7), sems.take(7)

        def copy(self, k, origin, split, src=None):
            there = self.buf.at[pl.ds(pl.multiple_of(self.offset(origin), self.rows), self.rows), :]
            here = there if src is None else src
            return remote(here, there, self.ss(k), self.rs(k), d, split)

        def send(self, k, origin, split, src=None):
            cp = self.copy(k, origin, split, src)
            cp.start()
            pending.append(cp)

        def start(self, src):
            for dx in (2, 1, 3):
                self.send(dx - 1, s, on_x(dx), src)
            self.send(3, s, sib, src)

        def forward(self, dx):
            origin = on_x(-dx)
            self.copy(dx - 1, origin, sib).wait_recv()
            self.send(3 + dx, origin, sib)

        def relay(self):
            self.forward(1)
            self.forward(3)

        def near(self):
            self.copy(3, sib, sib).wait_recv()
            for dx in (1, 3):
                self.copy(3 + dx, on_x(-dx) + 1 - 2 * c, sib).wait_recv()

        def far(self):
            self.copy(5, on_x(2) + 1 - 2 * c, sib).wait_recv()

        def finish(self):
            self.forward(2)
            self.near()
            self.far()

    class Scatter:
        def __init__(self, compute, own, ssend, srecv, xsend, xrecv):
            self.compute, self.own = compute, own
            self.ssend, self.srecv, self.xsend, self.xrecv = ssend, srecv, xsend, xrecv
            self.s1, self.r1 = sems.take(4), sems.take(4)
            self.s2, self.r2 = sems.take(3), sems.take(3)

        def to_sib(self, dx):
            return remote(self.ssend.at[dx], self.srecv.at[dx], self.s1(dx), self.r1(dx), d, sib)

        def to_chip(self, dx):
            return remote(
                self.xsend.at[dx - 1], self.xrecv.at[dx - 1], self.s2(dx - 1), self.r2(dx - 1),
                d, on_x(dx))

        def start(self):
            for dx in (2, 1, 3, 0):
                self.ssend[dx] = self.compute((x + dx) % NX * 2 + 1 - c).astype(BF)
                cp = self.to_sib(dx)
                cp.start()
                pending.append(cp)

        def middle(self):
            for dx in (2, 1, 3):
                mine = self.compute(on_x(dx))
                self.to_sib(dx).wait_recv()
                self.xsend[dx - 1] = (mine + self.srecv[dx].astype(F32)).astype(BF)
                cp = self.to_chip(dx)
                cp.start()
                pending.append(cp)
            mine = self.compute(s)
            self.to_sib(0).wait_recv()
            self.own[...] = mine + self.srecv[0].astype(F32)

        def finish(self):
            total = self.own[...]
            for dx in (1, 3, 2):
                self.to_chip(dx).wait_recv()
                total = total + self.xrecv[dx - 1].astype(F32)
            return total

    class Swap:
        def __init__(self, src, dst):
            self.src, self.dst = src, dst
            self.ss, self.rs = sems.take(NJ), sems.take(NJ)

        def start(self):
            for j in range(NJ):
                peer = t_mine + S * j
                land = pl.multiple_of((d % S) * SLAB + (d // S) * GH, GH)
                cp = remote(
                    self.src.at[pl.ds(j * GH, GH), :], self.dst.at[pl.ds(land, GH), :],
                    self.ss(j), self.rs(d // S), peer, s)
                pl.when(peer != d)(cp.start)

                @pl.when(peer == d)
                def _():
                    self.dst[pl.ds(land, GH), :] = self.src[pl.ds(j * GH, GH), :]

        def finish(self):
            for j in range(NJ):
                peer = t_mine + S * j
                land = pl.multiple_of(t_mine * SLAB + j * GH, GH)
                cp = remote(
                    self.src.at[pl.ds(j * GH, GH), :], self.dst.at[pl.ds(land, GH), :],
                    self.ss(j), self.rs(j), peer, s)

                @pl.when(peer != d)
                def _():
                    cp.wait_recv()
                    cp.wait_send()

    gather_nodes = Gather(tbl, lambda q: q * N, N)
    gather_nodes.start(nodes_hbm)
    for i in (8, 0, 1):
        loads[i].start()

    def permuted(values):
        ghost = values - PN
        part = ghost // GH
        place = PN + (part % S) * SLAB + (part // S) * GH + ghost % GH
        return jnp.where(values >= PN, place, values)

    def column(row):
        size = row.shape[1]
        hit = lax.broadcasted_iota(jnp.int32, (size, size), 0) == lax.broadcasted_iota(
            jnp.int32, (size, size), 1)
        return jnp.sum(jnp.where(hit, row.astype(F32), 0.0), axis=1, keepdims=True).astype(jnp.int32)

    def hot(mask):
        return jnp.where(mask, 1.0, 0.0).astype(BF)

    send_r = permuted(snd_row[...])
    recv_r = rcv_row[...]
    send_c = column(send_r)
    recv_c = column(recv_r)

    def build_t(r0):
        ids = lax.broadcasted_iota(jnp.int32, (256, E), 0) + r0
        pst[pl.ds(r0, 256), :] = hot(ids == send_r)

    rows_loop(PN + S * SLAB, 256, build_t)

    def build_rt(r0):
        ids = lax.broadcasted_iota(jnp.int32, (256, E), 0) + r0
        prt[pl.ds(r0, 256), :] = hot(ids == recv_r)

    rows_loop(PN, 256, build_rt)
    for c0 in range(0, PN + S * SLAB, 256):
        ids = lax.broadcasted_iota(jnp.int32, (E, 256), 1) + c0
        ps[:, c0:c0 + 256] = hot(ids == send_c)
        if c0 < PN:
            pr[:, c0:c0 + 256] = hot(ids == recv_c)

    lists = snd_lists[0]
    slot = lax.broadcasted_iota(jnp.int32, (S * SLAB, DOM), 0)
    part = slot // SLAB + (slot // GH) % NJ * S
    rows = hot(lax.broadcasted_iota(jnp.int32, (S * SLAB, DOM), 1) == part)
    high = dot_nt(rows, (lists // 32).astype(F32).astype(BF))
    low = dot_nt(rows, (lists % 32).astype(F32).astype(BF))
    slot = lax.broadcasted_iota(jnp.int32, (S * SLAB, GH), 0)
    here = lax.broadcasted_iota(jnp.int32, (S * SLAB, GH), 1) == slot % GH
    lists_c = jnp.sum(
        jnp.where(here, high * 32.0 + low, 0.0), axis=1, keepdims=True).astype(jnp.int32)

    loads[0].wait()
    loads[1].wait()

    def edge_part(r0):
        rows = pl.ds(r0, BLOCK)
        pre[rows, :] = dot(edges[rows, :], ein[0])

    rows_loop(E, BLOCK, edge_part)

    loads[8].wait()
    gather_nodes.relay()
    gather_nodes.finish()
    for i in (2, 6, 3, 4, 7, 5):
        loads[i].start()

    hit = jnp.zeros((SLAB, 1), jnp.int32)
    for t in range(S):
        hit = jnp.where(t_mine == t, lists_c[t * SLAB:(t + 1) * SLAB, :], hit)
    pick = hot(lax.broadcasted_iota(jnp.int32, (SLAB, PN), 1) == hit)
    gsend[...] = dot(pick, tbl[:PN, :]).astype(BF)
    ghosts = tbl.at[pl.ds(PN, S * SLAB), :]
    swap_ghost = Swap(gsend, ghosts)
    swap_ghost.start()

    def gather_recv(r0):
        rows = pl.ds(r0, BLOCK)
        got = dot(pr[rows, :], tbl[:PN, :]).astype(BF)
        recv[rows, :] = got
        pre[rows, :] = pre[rows, :] + dot(got, ein[2])

    rows_loop(E, BLOCK, gather_recv)
    swap_ghost.finish()
    gather_ghost = Gather(ghosts, lambda q: ((q - d + DOM) % S) * SLAB, SLAB)
    gather_ghost.start(ghosts.at[pl.ds(pl.multiple_of(t_mine * SLAB, SLAB), SLAB), :])

    def gather_sent(r0):
        rows = pl.ds(r0, BLOCK)
        sent_acc[rows, :] = dot(ps[rows, :PN], tbl[:PN, :])

    rows_loop(E, BLOCK, gather_sent)
    gather_ghost.relay()
    gather_ghost.finish()

    loads[2].wait()
    edge_gain = egain[...]

    def edge_forward(r0):
        rows = pl.ds(r0, BLOCK)
        got = (sent_acc[rows, :] + dot(ps[rows, PN:], tbl[PN:, :])).astype(BF)
        sent[rows, :] = got
        act = pre[rows, :] + dot(got, ein[1])
        pre[rows, :] = act
        hidden = swish(act).astype(BF)
        hid[rows, :] = hidden
        message = dot(hidden, eout[...])
        msg[rows, :] = message
        edges_out_v[rows, :] = (edges[rows, :].astype(F32) + normalize(message, edge_gain)).astype(BF)

    rows_loop(E, BLOCK, edge_forward)

    NH = N // 2

    def agg_block(half):
        def block(q):
            return dot(prt[pl.ds(pl.multiple_of(q * N + half * NH, NH), NH), :], edges_out_v[...])

        return block

    reduce_agg = [
        Scatter(agg_block(h), agg_own.at[h], aggs_send.at[h], aggs_recv.at[h], aggx_send.at[h],
                aggx_recv.at[h])
        for h in range(2)
    ]
    gather_dagg = [
        Gather(dagg, functools.partial(lambda h, q: q * N + h * NH, h), NH) for h in range(2)
    ]
    for h in range(2):
        reduce_agg[h].start()
    for h in range(2):
        reduce_agg[h].middle()
    stores[0].start()
    loads[3].wait()
    loads[4].wait()
    loads[5].wait()
    loads[6].wait()
    loads[7].wait()
    npre[...] = dot(nodes_in[...], nin[0])
    node_gain = ngain[...]

    for h in range(2):
        rows = slice(h * NH, (h + 1) * NH)
        sums = reduce_agg[h].finish().astype(BF)
        agg[rows, :] = sums
        act = npre[rows, :] + dot(sums, nin[1])
        npre[rows, :] = act
        hidden = swish(act).astype(BF)
        nhid[rows, :] = hidden
        message = dot(hidden, nout[...])
        nmsg[rows, :] = message
        upstream = ncot[rows, :].astype(F32)
        grad_message = normalize_back(message, node_gain, upstream).astype(BF)
        dnmsg[rows, :] = grad_message
        grad_pre = (dot_nt(grad_message, nout[...]) * swish_slope(act)).astype(BF)
        dnpre[rows, :] = grad_pre
        dagg_own[rows, :] = dot_nt(grad_pre, nin[1]).astype(BF)
        dagg[pl.ds(pl.multiple_of(s * N + h * NH, NH), NH), :] = dagg_own[rows, :]
        gather_dagg[h].start(dagg_own.at[rows, :])
    gdirect[...] = ncot[...].astype(F32) + dot_nt(dnpre[...], nin[0])
    nodes_out_v[...] = (
        nodes_in[...].astype(F32) + normalize(nmsg[...], node_gain)).astype(BF)
    stores[1].start()

    mine_cols = pl.ds(pl.multiple_of(c * HALF, HALF), HALF)
    sib_cols = pl.ds(pl.multiple_of((1 - c) * HALF, HALF), HALF)

    class Products:
        def __init__(self, pairs, ssend, srecv, own):
            self.pairs, self.ssend, self.srecv, self.own = pairs, ssend, srecv, own
            self.s0, self.r0 = sems.take(len(pairs)), sems.take(len(pairs))

        def sib_copy(self, i):
            return remote(self.ssend.at[i], self.srecv.at[i], self.s0(i), self.r0(i), d, sib)

        def products(self, i):
            left, right = self.pairs[i]
            columns = jnp.concatenate([right[:, sib_cols], right[:, mine_cols]], axis=1)
            grad = dot_tn(left[...], columns)
            self.ssend[i] = grad[:, :HALF].astype(BF)
            cp = self.sib_copy(i)
            cp.start()
            pending.append(cp)
            self.own[i] = grad[:, HALF:]

        def chip_sum(self, i, rows):
            return self.own[i, rows, :] + self.srecv[i, rows, :].astype(F32)

    class Peers:
        def __init__(self, count, send, recv, to):
            self.count, self.sbuf, self.rbuf, self.to = count, send, recv, to
            self.ss, self.rs = sems.take(count - 1), sems.take(count - 1)

        def copy(self, k):
            return remote(
                self.sbuf.at[k - 1], self.rbuf.at[k - 1], self.ss(k - 1), self.rs(k - 1),
                *self.to(k))

        def send(self, k, value):
            self.sbuf[k - 1] = value.astype(BF)
            cp = self.copy(k)
            cp.start()
            pending.append(cp)

        def total(self, mine):
            for k in range(1, self.count):
                self.copy(k).wait_recv()
                mine = mine + self.rbuf[k - 1].astype(F32)
            return mine

    def on_y(k):
        return (y + k) % NY * NZ + z, s

    def on_z(k):
        return y * NZ + (z + k) % NZ, s

    Z_ORDER = (4, 3, 5, 2, 6, 1, 7)

    class Weights(Products):
        def __init__(self, pairs, ssend, srecv, own, ysend, yrecv, ysum, zsend, zrecv, zsum, xsend, xrecv):
            super().__init__(pairs, ssend, srecv, own)
            self.y = [Peers(NY, ysend.at[i], yrecv.at[i], on_y) for i in range(3)]
            self.z = [Peers(NZ, zsend.at[i], zrecv.at[i], on_z) for i in range(3)]
            self.ysum, self.zsum, self.xsend, self.xrecv = ysum, zsum, xsend, xrecv
            self.sx, self.rx = sems.take(NX - 1), sems.take(NX - 1)

        def to_y(self, i):
            self.sib_copy(i).wait_recv()
            for k in (2, 1, 3):
                rows = pl.ds(pl.multiple_of((y + k) % NY * 128, 128), 128)
                self.y[i].send(k, self.chip_sum(i, rows))

        def to_z(self, i):
            rows = pl.ds(pl.multiple_of(y * 128, 128), 128)
            self.ysum[i] = self.y[i].total(self.chip_sum(i, rows))
            for k in Z_ORDER:
                rows = pl.ds(pl.multiple_of((z + k) % NZ * 16, 16), 16)
                self.z[i].send(k, self.ysum[i, rows, :])

        def x_copy(self, k):
            return remote(
                self.xsend.at[k - 1], self.xrecv.at[k - 1], self.sx(k - 1), self.rx(k - 1),
                d, on_x(k))

        def to_x(self):
            rows = pl.ds(pl.multiple_of(z * 16, 16), 16)
            for i in range(3):
                self.zsum[i] = self.z[i].total(self.ysum[i, rows, :])
            for k in (2, 1, 3):
                @pl.when((x + k) % NX < 3)
                def _():
                    self.xsend[k - 1] = self.zsum[(x + k) % NX].astype(BF)
                    self.x_copy(k).start()

        def finish(self):
            total = self.zsum[jnp.minimum(x, 2)]
            for k in (1, 3, 2):
                self.x_copy(k).wait_recv()
                total = total + self.xrecv[k - 1].astype(F32)
            return total

        def drain(self):
            for k in (2, 1, 3):
                pl.when((x + k) % NX < 3)(self.x_copy(k).wait_send)

    class LastWeights(Products):
        def __init__(self, pairs, ssend, srecv, own, zsend, zrecv, zsum, ysend, yrecv, ysum, xsend, xrecv):
            super().__init__(pairs, ssend, srecv, own)
            self.zsum, self.ysum, self.xsend, self.xrecv = zsum, ysum, xsend, xrecv
            self.z = Peers(NZ, zsend, zrecv, on_z)
            self.y = Peers(NY, ysend, yrecv, on_y)
            self.sx, self.rx = sems.take(1), sems.take(3)

        def to_z(self):
            self.sib_copy(0).wait_recv()
            for k in Z_ORDER:
                rows = pl.ds(pl.multiple_of((z + k) % NZ * 64, 64), 64)
                self.z.send(k, self.chip_sum(0, rows))

        def to_y(self):
            rows = pl.ds(pl.multiple_of(z * 64, 64), 64)
            self.zsum[...] = self.z.total(self.chip_sum(0, rows))
            for k in (2, 1, 3):
                rows = pl.ds(pl.multiple_of((y + k) % NY * 16, 16), 16)
                self.y.send(k, self.zsum[rows, :])

        def x_copy(self, k):
            return remote(self.xsend, self.xrecv.at[k], self.sx(0), self.rx(k), d, 6 + c)

        def to_x(self):
            total = self.y.total(self.zsum[pl.ds(pl.multiple_of(y * 16, 16), 16), :])
            self.ysum[...] = total
            self.xsend[...] = total.astype(BF)
            for k in range(3):
                pl.when(x == k)(self.x_copy(k).start)

        def finish(self):
            total = self.ysum[...]
            for k in range(3):
                self.x_copy(k).wait_recv()
                total = total + self.xrecv[k].astype(F32)
            return total

        def drain(self):
            pl.when(x < 3)(self.x_copy(0).wait_send)

    node_weights = Weights(
        ((nodes_in, dnpre), (agg, dnpre), (nhid, dnmsg)),
        fn_ssend, fn_srecv, fn_own, fn_ysend, fn_yrecv, fn_ysum, fn_zsend, fn_zrecv, fn_zsum,
        fn_xsend, fn_xrecv)
    edge_weights = Weights(
        ((edges, dpre), (sent, dpre), (recv, dpre)),
        fe_ssend, fe_srecv, fe_own, fe_ysend, fe_yrecv, fe_ysum, fe_zsend, fe_zrecv, fe_zsum,
        fe_xsend, fe_xrecv)
    out_weights = LastWeights(
        ((hid, dmsg),),
        fo_ssend, fo_srecv, fo_own, fo_zsend, fo_zrecv, fo_zsum, fo_ysend, fo_yrecv, fo_ysum,
        fo_xsend, fo_xrecv)

    for i in range(3):
        node_weights.products(i)
    for i in range(3):
        node_weights.to_y(i)
    for h in range(2):
        gather_dagg[h].relay()
    for h in range(2):
        gather_dagg[h].forward(2)
    for h in range(2):
        gather_dagg[h].near()

    def chip_part(dx):
        rows = pl.ds(pl.multiple_of((x + dx) % NX * 2 * N, 2 * N), 2 * N)
        return dot(pr[:, rows], dagg[rows, :])

    gedge[...] = ecot[...].astype(F32) + chip_part(0)
    gedge[...] = gedge[...] + chip_part(1)
    gedge[...] = gedge[...] + chip_part(3)
    for h in range(2):
        gather_dagg[h].far()

    def edge_backward(r0):
        rows = pl.ds(r0, BLOCK)
        up = gedge[rows, :] + chip_part(2)
        gedge[rows, :] = up
        grad_msg = normalize_back(msg[rows, :], edge_gain, up).astype(BF)
        dmsg[rows, :] = grad_msg
        grad = (dot_nt(grad_msg, eout[...]) * swish_slope(pre[rows, :])).astype(BF)
        dpre[rows, :] = grad

    rows_loop(E, BLOCK, edge_backward)

    def ghost_block(q):
        place = PN + ((q - d + DOM) % S) * SLAB
        return dot(pst[pl.ds(pl.multiple_of(place, SLAB), SLAB), :], dsent[...])

    out_weights.products(0)
    edge_weights.products(0)

    def send_grad(r0):
        rows = pl.ds(r0, BLOCK)
        dsent[rows, :] = dot_nt(dpre[rows, :], ein[1]).astype(BF)

    rows_loop(E, BLOCK, send_grad)
    out_weights.to_z()
    edge_weights.to_y(0)
    reduce_ghost = Scatter(ghost_block, gg_own, gg_ssend, gg_srecv, gg_xsend, gg_xrecv)
    reduce_ghost.start()
    edge_weights.products(1)
    reduce_ghost.middle()
    edge_weights.to_y(1)
    edge_weights.products(2)

    def recv_grad(r0):
        rows = pl.ds(r0, BLOCK)
        drecv[rows, :] = dot_nt(dpre[rows, :], ein[2]).astype(BF)

    rows_loop(E, BLOCK, recv_grad)
    edge_weights.to_y(2)

    def own_block(q):
        rows = pl.ds(pl.multiple_of(q * N, N), N)
        return dot(pst[rows, :], dsent[...]) + dot(prt[rows, :], drecv[...])

    reduce_own = Scatter(own_block, own_own, own_ssend, own_srecv, own_xsend, own_xrecv)
    reduce_own.start()
    for i in range(3):
        node_weights.to_z(i)
    a2_send[...] = reduce_ghost.finish().astype(BF)
    swap_back = Swap(a2_send, retg)
    swap_back.start()
    reduce_own.middle()

    def edge_grad(r0):
        rows = pl.ds(r0, BLOCK)
        egrad_v[rows, :] = (gedge[rows, :] + dot_nt(dpre[rows, :], ein[0])).astype(BF)

    rows_loop(E, BLOCK, edge_grad)
    stores[2].start()
    place = hot(lax.broadcasted_iota(jnp.int32, (S * SLAB, N), 1) + s * N == lists_c)
    swap_back.finish()
    gather_back = Gather(retg, lambda q: ((q - d + DOM) % S) * SLAB, SLAB)
    gather_back.start(retg.at[pl.ds(pl.multiple_of(t_mine * SLAB, SLAB), SLAB), :])
    edge_weights.to_z(0)
    out_weights.to_y()
    node_weights.to_x()
    edge_weights.to_z(1)
    edge_weights.to_z(2)
    gather_back.relay()
    out_weights.to_x()
    edge_weights.to_x()
    gather_back.finish()
    direct = gdirect[...] + dot_tn(place, retg[...])
    ngrad[...] = (direct + reduce_own.finish()).astype(BF)

    s_fin, r_fin = sems.take(6), sems.take(4)

    def fin_copy(group, i, slot, half):
        to = jnp.minimum(owner(group, i)[0], DOM * S - 1)
        return remote(
            fin.at[group], rows_in.at[slot, half], s_fin(3 * group + i), r_fin(2 * slot + half),
            to // S, to % S)

    def hand_out(group):
        for i in range(3):
            to, at, valid = owner(group, i)
            for slot in range(2):
                for half in range(2):
                    here = valid & (at == slot) & (c == half)
                    pl.when(here & (to != lin))(fin_copy(group, i, slot, half).start)

                    @pl.when(here & (to == lin))
                    def _():
                        rows_in[slot, half] = fin[group]

    @pl.when(x < 3)
    def _():
        fin[1] = node_weights.finish()

    hand_out(1)

    @pl.when(x < 3)
    def _():
        fin[0] = edge_weights.finish()

    @pl.when(x == 3)
    def _():
        fin[0] = out_weights.finish()

    hand_out(0)
    for slot in range(2):
        for half in range(2):
            pl.when(from_other(slot, half))(fin_copy(0, 0, slot, half).wait_recv)
    shift = first_row % 16
    for choice in range(0, 16, 2):
        @pl.when(shift == choice)
        def _():
            split = min(16 - choice, OUT_ROWS)
            for half in range(2):
                cols = slice(half * HALF, (half + 1) * HALF)
                wout[:split, cols] = rows_in[0, half, choice:choice + split, :]
                if split < OUT_ROWS:
                    wout[split:, cols] = rows_in[1, half, :OUT_ROWS - split, :]

    for store in stores:
        store.wait()
    for cp in pending:
        cp.wait_send()
    node_weights.drain()
    edge_weights.drain()
    out_weights.drain()
    for group in range(2):
        for i in range(3):
            to, _, valid = owner(group, i)
            pl.when(valid & (to != lin))(fin_copy(group, i, 0, 0).wait_send)


def scratch():
    def bf(*shape):
        return pltpu.VMEM(shape, BF)

    def f32(*shape):
        return pltpu.VMEM(shape, F32)

    T = PN + S * SLAB

    def scatter(rows, *lead):
        return [
            bf(*lead, NX, rows, D), bf(*lead, NX, rows, D), bf(*lead, NX - 1, rows, D),
            bf(*lead, NX - 1, rows, D), f32(*lead, rows, D),
        ]

    def products(count):
        return [bf(count, D, HALF), bf(count, D, HALF), f32(count, D, HALF)]

    def weights():
        return [
            *products(3), bf(3, NY - 1, 128, HALF), bf(3, NY - 1, 128, HALF), f32(3, 128, HALF),
            bf(3, NZ - 1, 16, HALF), bf(3, NZ - 1, 16, HALF), f32(3, 16, HALF),
            bf(NX - 1, 16, HALF), bf(NX - 1, 16, HALF),
        ]

    return [
        bf(N, D), bf(N, D), bf(N, D), bf(E, D), bf(E, D),
        bf(E, D), bf(3, D, D), bf(D, D), bf(2, D, D), bf(D, D), bf(E, D),
        bf(E, T), bf(E, PN), bf(T, E), bf(PN, E), bf(T, D), f32(E, D), bf(E, D), bf(E, D),
        f32(E, D), f32(E, D), bf(E, D),
        bf(SLAB, D), *scatter(N // 2, 2),
        bf(N, D), f32(N, D), f32(N, D), bf(N, D), f32(N, D), bf(N, D), bf(N, D), bf(N, D), bf(PN, D),
        f32(E, D), bf(E, D), bf(E, D), bf(E, D), bf(E, D),
        *scatter(SLAB), bf(SLAB, D), bf(S * SLAB, D), *scatter(N),
        *weights(), *weights(),
        *products(1), bf(NZ - 1, 64, HALF), bf(NZ - 1, 64, HALF), f32(64, HALF),
        bf(NY - 1, 16, HALF), bf(NY - 1, 16, HALF), f32(16, HALF), bf(16, HALF), bf(NX - 1, 16, HALF),
        f32(2, 16, HALF), f32(2, 2, 16, HALF),
        pltpu.SemaphoreType.DMA((N_SEM,)),
    ]


def hand_over(a0, a1, a2, a3, w_in, b0, b1, b2, b3, w_out):
    for src, dst in ((a0, b0), (a1, b1), (a2, b2), (a3, b3)):
        dst[...] = src[...]
    for i in range(OUT_ROWS):
        w_out[:, i * D:(i + 1) * D] = w_in[i:i + 1, :]


def body(
    node_state, edge_state, senders, receivers, send_rows, edge_in, edge_out, edge_gain,
    node_in, node_out, node_gain, node_cot, edge_cot,
):
    vmem = pl.BlockSpec(memory_space=pltpu.VMEM)
    hbm = pl.BlockSpec(memory_space=pl.ANY)
    states = (
        jax.ShapeDtypeStruct((N, D), BF),
        jax.ShapeDtypeStruct((E, D), BF),
        jax.ShapeDtypeStruct((N, D), BF),
        jax.ShapeDtypeStruct((E, D), BF),
    )
    results = pl.pallas_call(
        kernel,
        out_shape=states + (jax.ShapeDtypeStruct((OUT_ROWS, D), F32),),
        in_specs=[vmem] * 5 + [hbm] * 8,
        out_specs=[hbm, hbm, vmem, hbm, vmem],
        scratch_shapes=scratch(),
        compiler_params=pltpu.CompilerParams(
            collective_id=0, has_side_effects=True, vmem_limit_bytes=60 * 1024 * 1024),
    )(
        senders.reshape(1, E), receivers.reshape(1, E), send_rows.transpose(0, 2, 1),
        edge_gain, node_gain,
        node_state, node_cot, edge_state, edge_in[0], edge_out[0], node_in[0], node_out[0], edge_cot,
    )
    return pl.pallas_call(
        hand_over,
        out_shape=states + (jax.ShapeDtypeStruct((1, OUT_ROWS * D), F32),),
        in_specs=[vmem] * 5,
        out_specs=[vmem] * 5,
    )(*results)


def solution(mesh):
    both = P(("dom", "esplit"), None)
    in_specs = (
        both, both, P(("dom", "esplit")), P(("dom", "esplit")), P("dom", None, None),
        P(), P(), P(), P(), P(), P(), both, both,
    )
    out_specs = (both, both, both, both, P(None, ("dom", "esplit")))
    return jax.shard_map(body, mesh=mesh, in_specs=in_specs, out_specs=out_specs, check_vma=False)
```

```python
import functools

import jax
import jax.numpy as jnp
from jax import lax
from jax.experimental import pallas as pl
from jax.experimental.pallas import tpu as pltpu
from jax.sharding import PartitionSpec as P

EPSILON = 1e-05
BF = jnp.bfloat16
F32 = jnp.float32
MESH = pl.DeviceIdType.MESH

NZ = 8
NY = 4
NX = 4
DOM = NY * NZ
S = NX * 2
D = 512
N = 128
PN = N * S
E = 512
GH = 16
SLAB = DOM // S * GH
NJ = DOM // S
HALF = D // 2
NMAT = 7
OUT_ROWS = 14
BLOCK = 512


def dot(a, b):
    return lax.dot_general(a, b, (((1,), (0,)), ((), ())), preferred_element_type=F32)


def dot_nt(a, b):
    return lax.dot_general(a, b, (((1,), (1,)), ((), ())), preferred_element_type=F32)


def dot_tn(a, b):
    return lax.dot_general(a, b, (((0,), (0,)), ((), ())), preferred_element_type=F32)


def normalize(values, gain):
    average = jnp.mean(values, axis=-1, keepdims=True)
    centered = values - average
    inv_scale = lax.rsqrt(jnp.mean(centered * centered, axis=-1, keepdims=True) + EPSILON)
    return gain * centered * inv_scale


def normalize_back(values, gain, upstream):
    average = jnp.mean(values, axis=-1, keepdims=True)
    centered = values - average
    inv_scale = lax.rsqrt(jnp.mean(centered * centered, axis=-1, keepdims=True) + EPSILON)
    scaled = centered * inv_scale
    grad_scaled = upstream * gain
    first = jnp.mean(grad_scaled, axis=-1, keepdims=True)
    second = jnp.mean(grad_scaled * scaled, axis=-1, keepdims=True)
    return inv_scale * (grad_scaled - first - scaled * second)


def swish(values):
    return values * jax.nn.sigmoid(values)


def swish_slope(values):
    sigma = jax.nn.sigmoid(values)
    return sigma * (1.0 + values * (1.0 - sigma))


def rows_loop(total, step, fn):
    def one(i, carry):
        fn(pl.multiple_of(i * step, step))
        return carry

    lax.fori_loop(0, total // step, one, 0)


class Sems:
    def __init__(self, ref):
        self.ref = ref
        self.used = 0

    def take(self, count):
        base = self.used
        self.used += count
        return lambda i: self.ref.at[base + i]


N_SEM = 340


def kernel(
    snd_row, rcv_row, snd_lists, egain, ngain,
    nodes_hbm, ncot_hbm, edges_hbm, ein_hbm, eout_hbm, nin_hbm, nout_hbm, ecot_hbm,
    nodes_out, edges_out, ngrad, egrad, wout,
    nodes_in, ncot, nodes_out_v, edges_out_v, egrad_v, edges, ein, eout, nin, nout, ecot,
    ps, pr, pst, prt, tbl, sent_acc, sent, recv, pre, msg, hid,
    gsend, aggs_send, aggs_recv, aggx_send, aggx_recv, agg_own,
    agg, npre, nmsg, nhid, gdirect, dnpre, dnmsg, dagg_own, dagg,
    gedge, dmsg, dpre, dsent, drecv,
    gg_ssend, gg_srecv, gg_xsend, gg_xrecv, gg_own, a2_send, retg,
    own_ssend, own_srecv, own_xsend, own_xrecv, own_own,
    fn_ssend, fn_srecv, fn_own, fn_ysend, fn_yrecv, fn_ysum, fn_zsend, fn_zrecv, fn_zsum, fn_xsend, fn_xrecv,
    fe_ssend, fe_srecv, fe_own, fe_ysend, fe_yrecv, fe_ysum, fe_zsend, fe_zrecv, fe_zsum, fe_xsend, fe_xrecv,
    fo_ssend, fo_srecv, fo_own, fo_zsend, fo_zrecv, fo_zsum, fo_ysend, fo_yrecv, fo_ysum, fo_xsend, fo_xrecv,
    fin, rows_in,
    sem_ref,
):
    d = lax.axis_index("dom")
    s = lax.axis_index("esplit")
    y = d // NZ
    z = d % NZ
    x = s // 2
    c = s % 2
    lin = d * S + s
    sib = s + 1 - 2 * c
    t_mine = (s - d + DOM) % S
    sems = Sems(sem_ref)
    pending = []

    def remote(src, dst, send_sem, recv_sem, dom, split):
        return pltpu.make_async_remote_copy(
            src_ref=src, dst_ref=dst, send_sem=send_sem, recv_sem=recv_sem,
            device_id=(dom, split), device_id_type=MESH,
        )

    bar = pltpu.get_barrier_semaphore()

    def greet(dom, split):
        pl.semaphore_signal(bar, inc=1, device_id=(dom, split), device_id_type=MESH)

    for k in range(1, S):
        greet(d, (s + k) % S)
    for k in range(1, NY):
        greet((y + k) % NY * NZ + z, s)
    for k in range(1, NZ):
        greet(y * NZ + (z + k) % NZ, s)
    for j in range(NJ):
        pl.when(t_mine + S * j != d)(functools.partial(greet, t_mine + S * j, s))
    first_row = OUT_ROWS * lin
    b_first = first_row // 16
    b_last = (first_row + OUT_ROWS - 1) // 16

    def holder(b, half):
        r = b % DOM
        return jnp.where(b // DOM == 3, r % NY * NZ + r // NY, r), (b // DOM) % NX * 2 + half

    def from_other(slot, half):
        dom, split = holder(b_first + slot, half)
        here = dom * S + split != lin
        return here if slot == 0 else here & (b_last != b_first)

    for slot in range(2):
        for half in range(2):
            dom, split = holder(b_first + slot, half)
            pl.when(from_other(slot, half))(functools.partial(greet, dom, split))

    lsem = sems.take(9)
    loads = [
        pltpu.make_async_copy(a, b, lsem(i))
        for i, (a, b) in enumerate(
            ((edges_hbm, edges), (ein_hbm, ein), (eout_hbm, eout), (nin_hbm, nin),
             (nout_hbm, nout), (ecot_hbm, ecot), (nodes_hbm, nodes_in), (ncot_hbm, ncot),
             (nodes_hbm, tbl.at[pl.ds(pl.multiple_of(s * N, N), N), :])))
    ]
    ssem = sems.take(3)
    stores = [
        pltpu.make_async_copy(a, b, ssem(i))
        for i, (a, b) in enumerate(
            ((edges_out_v, edges_out), (nodes_out_v, nodes_out), (egrad_v, egrad)))
    ]

    def owner(group, i):
        b = DOM * (x + NX * group) + (d if group else jnp.where(x == 3, z * NY + y, d))
        to = (16 * b) // OUT_ROWS + i
        valid = to <= (16 * b + 15) // OUT_ROWS
        if group:
            valid = valid & (x < NMAT - NX)
        return to, b - (OUT_ROWS * to) // 16, valid

    arrivals = (S - 1) + (NY - 1) + (NZ - 1)
    for j in range(NJ):
        arrivals = arrivals + jnp.where(t_mine + S * j != d, 1, 0)
    for group in range(2):
        for i in range(3):
            to, _, valid = owner(group, i)
            arrivals = arrivals + jnp.where(valid & (to != lin), 1, 0)
    pl.semaphore_wait(bar, arrivals)

    def on_x(dx):
        return (x + dx + NX) % NX * 2 + c

    class Gather:
        def __init__(self, buf, offset, rows):
            self.buf, self.offset, self.rows = buf, offset, rows
            self.ss, self.rs = sems.take(7), sems.take(7)

        def copy(self, k, origin, split, src=None):
            there = self.buf.at[pl.ds(pl.multiple_of(self.offset(origin), self.rows), self.rows), :]
            here = there if src is None else src
            return remote(here, there, self.ss(k), self.rs(k), d, split)

        def send(self, k, origin, split, src=None):
            cp = self.copy(k, origin, split, src)
            cp.start()
            pending.append(cp)

        def start(self, src):
            for dx in (2, 1, 3):
                self.send(dx - 1, s, on_x(dx), src)
            self.send(3, s, sib, src)

        def forward(self, dx):
            origin = on_x(-dx)
            self.copy(dx - 1, origin, sib).wait_recv()
            self.send(3 + dx, origin, sib)

        def relay(self):
            self.forward(1)
            self.forward(3)

        def near(self):
            self.copy(3, sib, sib).wait_recv()
            for dx in (1, 3):
                self.copy(3 + dx, on_x(-dx) + 1 - 2 * c, sib).wait_recv()

        def far(self):
            self.copy(5, on_x(2) + 1 - 2 * c, sib).wait_recv()

        def finish(self):
            self.forward(2)
            self.near()
            self.far()

    class Scatter:
        def __init__(self, compute, own, ssend, srecv, xsend, xrecv):
            self.compute, self.own = compute, own
            self.ssend, self.srecv, self.xsend, self.xrecv = ssend, srecv, xsend, xrecv
            self.s1, self.r1 = sems.take(4), sems.take(4)
            self.s2, self.r2 = sems.take(3), sems.take(3)

        def to_sib(self, dx):
            return remote(self.ssend.at[dx], self.srecv.at[dx], self.s1(dx), self.r1(dx), d, sib)

        def to_chip(self, dx):
            return remote(
                self.xsend.at[dx - 1], self.xrecv.at[dx - 1], self.s2(dx - 1), self.r2(dx - 1),
                d, on_x(dx))

        def start(self):
            for dx in (2, 1, 3, 0):
                self.ssend[dx] = self.compute((x + dx) % NX * 2 + 1 - c).astype(BF)
                cp = self.to_sib(dx)
                cp.start()
                pending.append(cp)

        def middle(self):
            for dx in (2, 1, 3):
                mine = self.compute(on_x(dx))
                self.to_sib(dx).wait_recv()
                self.xsend[dx - 1] = (mine + self.srecv[dx].astype(F32)).astype(BF)
                cp = self.to_chip(dx)
                cp.start()
                pending.append(cp)
            mine = self.compute(s)
            self.to_sib(0).wait_recv()
            self.own[...] = mine + self.srecv[0].astype(F32)

        def finish(self):
            total = self.own[...]
            for dx in (1, 3, 2):
                self.to_chip(dx).wait_recv()
                total = total + self.xrecv[dx - 1].astype(F32)
            return total

    class Swap:
        def __init__(self, src, dst):
            self.src, self.dst = src, dst
            self.ss, self.rs = sems.take(NJ), sems.take(NJ)

        def start(self):
            for j in range(NJ):
                peer = t_mine + S * j
                land = pl.multiple_of((d % S) * SLAB + (d // S) * GH, GH)
                cp = remote(
                    self.src.at[pl.ds(j * GH, GH), :], self.dst.at[pl.ds(land, GH), :],
                    self.ss(j), self.rs(d // S), peer, s)
                pl.when(peer != d)(cp.start)

                @pl.when(peer == d)
                def _():
                    self.dst[pl.ds(land, GH), :] = self.src[pl.ds(j * GH, GH), :]

        def finish(self):
            for j in range(NJ):
                peer = t_mine + S * j
                land = pl.multiple_of(t_mine * SLAB + j * GH, GH)
                cp = remote(
                    self.src.at[pl.ds(j * GH, GH), :], self.dst.at[pl.ds(land, GH), :],
                    self.ss(j), self.rs(j), peer, s)

                @pl.when(peer != d)
                def _():
                    cp.wait_recv()
                    cp.wait_send()

    gather_nodes = Gather(tbl, lambda q: q * N, N)
    gather_nodes.start(nodes_hbm)
    for i in (8, 0, 1):
        loads[i].start()

    def permuted(values):
        ghost = values - PN
        part = ghost // GH
        place = PN + (part % S) * SLAB + (part // S) * GH + ghost % GH
        return jnp.where(values >= PN, place, values)

    def column(row):
        size = row.shape[1]
        hit = lax.broadcasted_iota(jnp.int32, (size, size), 0) == lax.broadcasted_iota(
            jnp.int32, (size, size), 1)
        return jnp.sum(jnp.where(hit, row.astype(F32), 0.0), axis=1, keepdims=True).astype(jnp.int32)

    def hot(mask):
        return jnp.where(mask, 1.0, 0.0).astype(BF)

    send_r = permuted(snd_row[...])
    recv_r = rcv_row[...]
    send_c = column(send_r)
    recv_c = column(recv_r)

    def build_t(r0):
        ids = lax.broadcasted_iota(jnp.int32, (256, E), 0) + r0
        pst[pl.ds(r0, 256), :] = hot(ids == send_r)

    rows_loop(PN + S * SLAB, 256, build_t)

    def build_rt(r0):
        ids = lax.broadcasted_iota(jnp.int32, (256, E), 0) + r0
        prt[pl.ds(r0, 256), :] = hot(ids == recv_r)

    rows_loop(PN, 256, build_rt)
    for c0 in range(0, PN + S * SLAB, 256):
        ids = lax.broadcasted_iota(jnp.int32, (E, 256), 1) + c0
        ps[:, c0:c0 + 256] = hot(ids == send_c)
        if c0 < PN:
            pr[:, c0:c0 + 256] = hot(ids == recv_c)

    lists = snd_lists[0]
    slot = lax.broadcasted_iota(jnp.int32, (S * SLAB, DOM), 0)
    part = slot // SLAB + (slot // GH) % NJ * S
    rows = hot(lax.broadcasted_iota(jnp.int32, (S * SLAB, DOM), 1) == part)
    high = dot_nt(rows, (lists // 32).astype(F32).astype(BF))
    low = dot_nt(rows, (lists % 32).astype(F32).astype(BF))
    slot = lax.broadcasted_iota(jnp.int32, (S * SLAB, GH), 0)
    here = lax.broadcasted_iota(jnp.int32, (S * SLAB, GH), 1) == slot % GH
    lists_c = jnp.sum(
        jnp.where(here, high * 32.0 + low, 0.0), axis=1, keepdims=True).astype(jnp.int32)

    loads[0].wait()
    loads[1].wait()

    def edge_part(r0):
        rows = pl.ds(r0, BLOCK)
        pre[rows, :] = dot(edges[rows, :], ein[0])

    rows_loop(E, BLOCK, edge_part)

    loads[8].wait()
    gather_nodes.relay()
    gather_nodes.finish()
    for i in (2, 6, 3, 4, 7, 5):
        loads[i].start()

    hit = jnp.zeros((SLAB, 1), jnp.int32)
    for t in range(S):
        hit = jnp.where(t_mine == t, lists_c[t * SLAB:(t + 1) * SLAB, :], hit)
    pick = hot(lax.broadcasted_iota(jnp.int32, (SLAB, PN), 1) == hit)
    gsend[...] = dot(pick, tbl[:PN, :]).astype(BF)
    ghosts = tbl.at[pl.ds(PN, S * SLAB), :]
    swap_ghost = Swap(gsend, ghosts)
    swap_ghost.start()

    def gather_recv(r0):
        rows = pl.ds(r0, BLOCK)
        got = dot(pr[rows, :], tbl[:PN, :]).astype(BF)
        recv[rows, :] = got
        pre[rows, :] = pre[rows, :] + dot(got, ein[2])

    rows_loop(E, BLOCK, gather_recv)
    swap_ghost.finish()
    gather_ghost = Gather(ghosts, lambda q: ((q - d + DOM) % S) * SLAB, SLAB)
    gather_ghost.start(ghosts.at[pl.ds(pl.multiple_of(t_mine * SLAB, SLAB), SLAB), :])

    def gather_sent(r0):
        rows = pl.ds(r0, BLOCK)
        sent_acc[rows, :] = dot(ps[rows, :PN], tbl[:PN, :])

    rows_loop(E, BLOCK, gather_sent)
    gather_ghost.relay()
    gather_ghost.finish()

    loads[2].wait()
    edge_gain = egain[...]

    def edge_forward(r0):
        rows = pl.ds(r0, BLOCK)
        got = (sent_acc[rows, :] + dot(ps[rows, PN:], tbl[PN:, :])).astype(BF)
        sent[rows, :] = got
        act = pre[rows, :] + dot(got, ein[1])
        pre[rows, :] = act
        hidden = swish(act).astype(BF)
        hid[rows, :] = hidden
        message = dot(hidden, eout[...])
        msg[rows, :] = message
        edges_out_v[rows, :] = (edges[rows, :].astype(F32) + normalize(message, edge_gain)).astype(BF)

    rows_loop(E, BLOCK, edge_forward)

    NH = N // 2

    def agg_block(half):
        def block(q):
            return dot(prt[pl.ds(pl.multiple_of(q * N + half * NH, NH), NH), :], edges_out_v[...])

        return block

    reduce_agg = [
        Scatter(agg_block(h), agg_own.at[h], aggs_send.at[h], aggs_recv.at[h], aggx_send.at[h],
                aggx_recv.at[h])
        for h in range(2)
    ]
    gather_dagg = [
        Gather(dagg, functools.partial(lambda h, q: q * N + h * NH, h), NH) for h in range(2)
    ]
    for h in range(2):
        reduce_agg[h].start()
    for h in range(2):
        reduce_agg[h].middle()
    stores[0].start()
    loads[3].wait()
    loads[4].wait()
    loads[5].wait()
    loads[6].wait()
    loads[7].wait()
    npre[...] = dot(nodes_in[...], nin[0])
    node_gain = ngain[...]

    for h in range(2):
        rows = slice(h * NH, (h + 1) * NH)
        sums = reduce_agg[h].finish().astype(BF)
        agg[rows, :] = sums
        act = npre[rows, :] + dot(sums, nin[1])
        npre[rows, :] = act
        hidden = swish(act).astype(BF)
        nhid[rows, :] = hidden
        message = dot(hidden, nout[...])
        nmsg[rows, :] = message
        upstream = ncot[rows, :].astype(F32)
        grad_message = normalize_back(message, node_gain, upstream).astype(BF)
        dnmsg[rows, :] = grad_message
        grad_pre = (dot_nt(grad_message, nout[...]) * swish_slope(act)).astype(BF)
        dnpre[rows, :] = grad_pre
        dagg_own[rows, :] = dot_nt(grad_pre, nin[1]).astype(BF)
        dagg[pl.ds(pl.multiple_of(s * N + h * NH, NH), NH), :] = dagg_own[rows, :]
        gather_dagg[h].start(dagg_own.at[rows, :])
    gdirect[...] = ncot[...].astype(F32) + dot_nt(dnpre[...], nin[0])
    nodes_out_v[...] = (
        nodes_in[...].astype(F32) + normalize(nmsg[...], node_gain)).astype(BF)
    stores[1].start()

    mine_cols = pl.ds(pl.multiple_of(c * HALF, HALF), HALF)
    sib_cols = pl.ds(pl.multiple_of((1 - c) * HALF, HALF), HALF)

    class Products:
        def __init__(self, pairs, ssend, srecv, own):
            self.pairs, self.ssend, self.srecv, self.own = pairs, ssend, srecv, own
            self.s0, self.r0 = sems.take(len(pairs)), sems.take(len(pairs))

        def sib_copy(self, i):
            return remote(self.ssend.at[i], self.srecv.at[i], self.s0(i), self.r0(i), d, sib)

        def products(self, i):
            left, right = self.pairs[i]
            columns = jnp.concatenate([right[:, sib_cols], right[:, mine_cols]], axis=1)
            grad = dot_tn(left[...], columns)
            self.ssend[i] = grad[:, :HALF].astype(BF)
            cp = self.sib_copy(i)
            cp.start()
            pending.append(cp)
            self.own[i] = grad[:, HALF:]

        def chip_sum(self, i, rows):
            return self.own[i, rows, :] + self.srecv[i, rows, :].astype(F32)

    class Peers:
        def __init__(self, count, send, recv, to):
            self.count, self.sbuf, self.rbuf, self.to = count, send, recv, to
            self.ss, self.rs = sems.take(count - 1), sems.take(count - 1)

        def copy(self, k):
            return remote(
                self.sbuf.at[k - 1], self.rbuf.at[k - 1], self.ss(k - 1), self.rs(k - 1),
                *self.to(k))

        def send(self, k, value):
            self.sbuf[k - 1] = value.astype(BF)
            cp = self.copy(k)
            cp.start()
            pending.append(cp)

        def total(self, mine):
            for k in range(1, self.count):
                self.copy(k).wait_recv()
                mine = mine + self.rbuf[k - 1].astype(F32)
            return mine

    def on_y(k):
        return (y + k) % NY * NZ + z, s

    def on_z(k):
        return y * NZ + (z + k) % NZ, s

    Z_ORDER = (4, 3, 5, 2, 6, 1, 7)

    class Weights(Products):
        def __init__(self, pairs, ssend, srecv, own, ysend, yrecv, ysum, zsend, zrecv, zsum, xsend, xrecv):
            super().__init__(pairs, ssend, srecv, own)
            self.y = [Peers(NY, ysend.at[i], yrecv.at[i], on_y) for i in range(3)]
            self.z = [Peers(NZ, zsend.at[i], zrecv.at[i], on_z) for i in range(3)]
            self.ysum, self.zsum, self.xsend, self.xrecv = ysum, zsum, xsend, xrecv
            self.sx, self.rx = sems.take(NX - 1), sems.take(NX - 1)

        def to_y(self, i):
            self.sib_copy(i).wait_recv()
            for k in (2, 1, 3):
                rows = pl.ds(pl.multiple_of((y + k) % NY * 128, 128), 128)
                self.y[i].send(k, self.chip_sum(i, rows))

        def to_z(self, i):
            rows = pl.ds(pl.multiple_of(y * 128, 128), 128)
            self.ysum[i] = self.y[i].total(self.chip_sum(i, rows))
            for k in Z_ORDER:
                rows = pl.ds(pl.multiple_of((z + k) % NZ * 16, 16), 16)
                self.z[i].send(k, self.ysum[i, rows, :])

        def x_copy(self, k):
            return remote(
                self.xsend.at[k - 1], self.xrecv.at[k - 1], self.sx(k - 1), self.rx(k - 1),
                d, on_x(k))

        def to_x(self):
            rows = pl.ds(pl.multiple_of(z * 16, 16), 16)
            for i in range(3):
                self.zsum[i] = self.z[i].total(self.ysum[i, rows, :])
            for k in (2, 1, 3):
                @pl.when((x + k) % NX < 3)
                def _():
                    self.xsend[k - 1] = self.zsum[(x + k) % NX].astype(BF)
                    self.x_copy(k).start()

        def finish(self):
            total = self.zsum[jnp.minimum(x, 2)]
            for k in (1, 3, 2):
                self.x_copy(k).wait_recv()
                total = total + self.xrecv[k - 1].astype(F32)
            return total

        def drain(self):
            for k in (2, 1, 3):
                pl.when((x + k) % NX < 3)(self.x_copy(k).wait_send)

    class LastWeights(Products):
        def __init__(self, pairs, ssend, srecv, own, zsend, zrecv, zsum, ysend, yrecv, ysum, xsend, xrecv):
            super().__init__(pairs, ssend, srecv, own)
            self.zsum, self.ysum, self.xsend, self.xrecv = zsum, ysum, xsend, xrecv
            self.z = Peers(NZ, zsend, zrecv, on_z)
            self.y = Peers(NY, ysend, yrecv, on_y)
            self.sx, self.rx = sems.take(1), sems.take(3)

        def to_z(self):
            self.sib_copy(0).wait_recv()
            for k in Z_ORDER:
                rows = pl.ds(pl.multiple_of((z + k) % NZ * 64, 64), 64)
                self.z.send(k, self.chip_sum(0, rows))

        def to_y(self):
            rows = pl.ds(pl.multiple_of(z * 64, 64), 64)
            self.zsum[...] = self.z.total(self.chip_sum(0, rows))
            for k in (2, 1, 3):
                rows = pl.ds(pl.multiple_of((y + k) % NY * 16, 16), 16)
                self.y.send(k, self.zsum[rows, :])

        def x_copy(self, k):
            return remote(self.xsend, self.xrecv.at[k], self.sx(0), self.rx(k), d, 6 + c)

        def to_x(self):
            total = self.y.total(self.zsum[pl.ds(pl.multiple_of(y * 16, 16), 16), :])
            self.ysum[...] = total
            self.xsend[...] = total.astype(BF)
            for k in range(3):
                pl.when(x == k)(self.x_copy(k).start)

        def finish(self):
            total = self.ysum[...]
            for k in range(3):
                self.x_copy(k).wait_recv()
                total = total + self.xrecv[k].astype(F32)
            return total

        def drain(self):
            pl.when(x < 3)(self.x_copy(0).wait_send)

    node_weights = Weights(
        ((nodes_in, dnpre), (agg, dnpre), (nhid, dnmsg)),
        fn_ssend, fn_srecv, fn_own, fn_ysend, fn_yrecv, fn_ysum, fn_zsend, fn_zrecv, fn_zsum,
        fn_xsend, fn_xrecv)
    edge_weights = Weights(
        ((edges, dpre), (sent, dpre), (recv, dpre)),
        fe_ssend, fe_srecv, fe_own, fe_ysend, fe_yrecv, fe_ysum, fe_zsend, fe_zrecv, fe_zsum,
        fe_xsend, fe_xrecv)
    out_weights = LastWeights(
        ((hid, dmsg),),
        fo_ssend, fo_srecv, fo_own, fo_zsend, fo_zrecv, fo_zsum, fo_ysend, fo_yrecv, fo_ysum,
        fo_xsend, fo_xrecv)

    for i in range(3):
        node_weights.products(i)
    for i in range(3):
        node_weights.to_y(i)
    for h in range(2):
        gather_dagg[h].relay()
    for h in range(2):
        gather_dagg[h].forward(2)
    for h in range(2):
        gather_dagg[h].near()

    def chip_part(dx):
        rows = pl.ds(pl.multiple_of((x + dx) % NX * 2 * N, 2 * N), 2 * N)
        return dot(pr[:, rows], dagg[rows, :])

    gedge[...] = ecot[...].astype(F32) + chip_part(0)
    gedge[...] = gedge[...] + chip_part(1)
    gedge[...] = gedge[...] + chip_part(3)
    for h in range(2):
        gather_dagg[h].far()

    def edge_backward(r0):
        rows = pl.ds(r0, BLOCK)
        up = gedge[rows, :] + chip_part(2)
        gedge[rows, :] = up
        grad_msg = normalize_back(msg[rows, :], edge_gain, up).astype(BF)
        dmsg[rows, :] = grad_msg
        grad = (dot_nt(grad_msg, eout[...]) * swish_slope(pre[rows, :])).astype(BF)
        dpre[rows, :] = grad

    rows_loop(E, BLOCK, edge_backward)

    def ghost_block(q):
        place = PN + ((q - d + DOM) % S) * SLAB
        return dot(pst[pl.ds(pl.multiple_of(place, SLAB), SLAB), :], dsent[...])

    edge_weights.products(0)
    out_weights.products(0)

    def send_grad(r0):
        rows = pl.ds(r0, BLOCK)
        dsent[rows, :] = dot_nt(dpre[rows, :], ein[1]).astype(BF)

    rows_loop(E, BLOCK, send_grad)
    reduce_ghost = Scatter(ghost_block, gg_own, gg_ssend, gg_srecv, gg_xsend, gg_xrecv)
    reduce_ghost.start()
    edge_weights.to_y(0)
    edge_weights.products(1)
    out_weights.to_z()
    reduce_ghost.middle()
    edge_weights.to_y(1)
    edge_weights.products(2)

    def recv_grad(r0):
        rows = pl.ds(r0, BLOCK)
        drecv[rows, :] = dot_nt(dpre[rows, :], ein[2]).astype(BF)

    rows_loop(E, BLOCK, recv_grad)
    edge_weights.to_y(2)

    def own_block(q):
        rows = pl.ds(pl.multiple_of(q * N, N), N)
        return dot(pst[rows, :], dsent[...]) + dot(prt[rows, :], drecv[...])

    reduce_own = Scatter(own_block, own_own, own_ssend, own_srecv, own_xsend, own_xrecv)
    reduce_own.start()
    for i in range(3):
        node_weights.to_z(i)
    a2_send[...] = reduce_ghost.finish().astype(BF)
    swap_back = Swap(a2_send, retg)
    swap_back.start()
    reduce_own.middle()

    def edge_grad(r0):
        rows = pl.ds(r0, BLOCK)
        egrad_v[rows, :] = (gedge[rows, :] + dot_nt(dpre[rows, :], ein[0])).astype(BF)

    rows_loop(E, BLOCK, edge_grad)
    stores[2].start()
    place = hot(lax.broadcasted_iota(jnp.int32, (S * SLAB, N), 1) + s * N == lists_c)
    swap_back.finish()
    gather_back = Gather(retg, lambda q: ((q - d + DOM) % S) * SLAB, SLAB)
    gather_back.start(retg.at[pl.ds(pl.multiple_of(t_mine * SLAB, SLAB), SLAB), :])
    edge_weights.to_z(0)
    out_weights.to_y()
    node_weights.to_x()
    edge_weights.to_z(1)
    edge_weights.to_z(2)
    s_fin, r_fin = sems.take(6), sems.take(4)

    def fin_copy(group, i, slot, half):
        to = jnp.minimum(owner(group, i)[0], DOM * S - 1)
        return remote(
            fin.at[group], rows_in.at[slot, half], s_fin(3 * group + i), r_fin(2 * slot + half),
            to // S, to % S)

    def hand_out(group):
        for i in range(3):
            to, at, valid = owner(group, i)
            for slot in range(2):
                for half in range(2):
                    here = valid & (at == slot) & (c == half)
                    pl.when(here & (to != lin))(fin_copy(group, i, slot, half).start)

                    @pl.when(here & (to == lin))
                    def _():
                        rows_in[slot, half] = fin[group]

    out_weights.to_x()
    edge_weights.to_x()
    gather_back.relay()
    @pl.when(x < 3)
    def _():
        fin[1] = node_weights.finish()

    hand_out(1)

    gather_back.finish()
    direct = gdirect[...] + dot_tn(place, retg[...])
    ngrad[...] = (direct + reduce_own.finish()).astype(BF)

    @pl.when(x < 3)
    def _():
        fin[0] = edge_weights.finish()

    @pl.when(x == 3)
    def _():
        fin[0] = out_weights.finish()

    hand_out(0)
    for slot in range(2):
        for half in range(2):
            pl.when(from_other(slot, half))(fin_copy(0, 0, slot, half).wait_recv)
    shift = first_row % 16
    for choice in range(0, 16, 2):
        @pl.when(shift == choice)
        def _():
            split = min(16 - choice, OUT_ROWS)
            for half in range(2):
                cols = slice(half * HALF, (half + 1) * HALF)
                wout[:split, cols] = rows_in[0, half, choice:choice + split, :]
                if split < OUT_ROWS:
                    wout[split:, cols] = rows_in[1, half, :OUT_ROWS - split, :]

    for store in stores:
        store.wait()
    for cp in pending:
        cp.wait_send()
    node_weights.drain()
    edge_weights.drain()
    out_weights.drain()
    for group in range(2):
        for i in range(3):
            to, _, valid = owner(group, i)
            pl.when(valid & (to != lin))(fin_copy(group, i, 0, 0).wait_send)


def scratch():
    def bf(*shape):
        return pltpu.VMEM(shape, BF)

    def f32(*shape):
        return pltpu.VMEM(shape, F32)

    T = PN + S * SLAB

    def scatter(rows, *lead):
        return [
            bf(*lead, NX, rows, D), bf(*lead, NX, rows, D), bf(*lead, NX - 1, rows, D),
            bf(*lead, NX - 1, rows, D), f32(*lead, rows, D),
        ]

    def products(count):
        return [bf(count, D, HALF), bf(count, D, HALF), f32(count, D, HALF)]

    def weights():
        return [
            *products(3), bf(3, NY - 1, 128, HALF), bf(3, NY - 1, 128, HALF), f32(3, 128, HALF),
            bf(3, NZ - 1, 16, HALF), bf(3, NZ - 1, 16, HALF), f32(3, 16, HALF),
            bf(NX - 1, 16, HALF), bf(NX - 1, 16, HALF),
        ]

    return [
        bf(N, D), bf(N, D), bf(N, D), bf(E, D), bf(E, D),
        bf(E, D), bf(3, D, D), bf(D, D), bf(2, D, D), bf(D, D), bf(E, D),
        bf(E, T), bf(E, PN), bf(T, E), bf(PN, E), bf(T, D), f32(E, D), bf(E, D), bf(E, D),
        f32(E, D), f32(E, D), bf(E, D),
        bf(SLAB, D), *scatter(N // 2, 2),
        bf(N, D), f32(N, D), f32(N, D), bf(N, D), f32(N, D), bf(N, D), bf(N, D), bf(N, D), bf(PN, D),
        f32(E, D), bf(E, D), bf(E, D), bf(E, D), bf(E, D),
        *scatter(SLAB), bf(SLAB, D), bf(S * SLAB, D), *scatter(N),
        *weights(), *weights(),
        *products(1), bf(NZ - 1, 64, HALF), bf(NZ - 1, 64, HALF), f32(64, HALF),
        bf(NY - 1, 16, HALF), bf(NY - 1, 16, HALF), f32(16, HALF), bf(16, HALF), bf(NX - 1, 16, HALF),
        f32(2, 16, HALF), f32(2, 2, 16, HALF),
        pltpu.SemaphoreType.DMA((N_SEM,)),
    ]


def hand_over(a0, a1, a2, a3, w_in, b0, b1, b2, b3, w_out, v0, v1, v2, v3, sem_in, sem_out):
    half = E // 2
    pieces = []
    for src, mid, dst in ((a1, v1, b1), (a3, v3, b3)):
        for r0 in (0, half):
            rows = pl.ds(r0, half)
            pieces.append((src.at[rows, :], mid.at[rows, :], dst.at[rows, :]))
    pieces += [(a0, v0, b0), (a2, v2, b2)]
    loads = [
        pltpu.make_async_copy(src, mid, sem_in.at[i]) for i, (src, mid, _) in enumerate(pieces)
    ]
    stores = [
        pltpu.make_async_copy(mid, dst, sem_out.at[i]) for i, (_, mid, dst) in enumerate(pieces)
    ]
    for load in loads:
        load.start()
    for i in range(OUT_ROWS):
        w_out[:, i * D:(i + 1) * D] = w_in[i:i + 1, :]
    for load, store in zip(loads, stores):
        load.wait()
        store.start()
    for store in stores:
        store.wait()


def body(
    node_state, edge_state, senders, receivers, send_rows, edge_in, edge_out, edge_gain,
    node_in, node_out, node_gain, node_cot, edge_cot,
):
    vmem = pl.BlockSpec(memory_space=pltpu.VMEM)
    hbm = pl.BlockSpec(memory_space=pl.ANY)
    states = (
        jax.ShapeDtypeStruct((N, D), BF),
        jax.ShapeDtypeStruct((E, D), BF),
        jax.ShapeDtypeStruct((N, D), BF),
        jax.ShapeDtypeStruct((E, D), BF),
    )
    results = pl.pallas_call(
        kernel,
        out_shape=states + (jax.ShapeDtypeStruct((OUT_ROWS, D), F32),),
        in_specs=[vmem] * 5 + [hbm] * 8,
        out_specs=[hbm, hbm, vmem, hbm, vmem],
        scratch_shapes=scratch(),
        compiler_params=pltpu.CompilerParams(
            collective_id=0, has_side_effects=True, vmem_limit_bytes=60 * 1024 * 1024),
    )(
        senders.reshape(1, E), receivers.reshape(1, E), send_rows.transpose(0, 2, 1),
        edge_gain, node_gain,
        node_state, node_cot, edge_state, edge_in[0], edge_out[0], node_in[0], node_out[0], edge_cot,
    )
    return pl.pallas_call(
        hand_over,
        out_shape=states + (jax.ShapeDtypeStruct((1, OUT_ROWS * D), F32),),
        in_specs=[hbm] * 4 + [vmem],
        out_specs=[hbm] * 4 + [vmem],
        scratch_shapes=[pltpu.VMEM(leaf.shape, BF) for leaf in states]
        + [pltpu.SemaphoreType.DMA((6,)), pltpu.SemaphoreType.DMA((6,))],
    )(*results)


def solution(mesh):
    both = P(("dom", "esplit"), None)
    in_specs = (
        both, both, P(("dom", "esplit")), P(("dom", "esplit")), P("dom", None, None),
        P(), P(), P(), P(), P(), P(), both, both,
    )
    out_specs = (both, both, both, both, P(None, ("dom", "esplit")))
    return jax.shard_map(body, mesh=mesh, in_specs=in_specs, out_specs=out_specs, check_vma=False)
```

```python
import functools

import jax
import jax.numpy as jnp
from jax import lax
from jax.experimental import pallas as pl
from jax.experimental.pallas import tpu as pltpu
from jax.sharding import PartitionSpec as P

EPSILON = 1e-05
BF = jnp.bfloat16
F32 = jnp.float32
MESH = pl.DeviceIdType.MESH

NZ = 8
NY = 4
NX = 4
DOM = NY * NZ
S = NX * 2
D = 512
N = 128
PN = N * S
E = 512
GH = 16
SLAB = DOM // S * GH
NJ = DOM // S
HALF = D // 2
NMAT = 7
OUT_ROWS = 14
BLOCK = 512


def dot(a, b):
    return lax.dot_general(a, b, (((1,), (0,)), ((), ())), preferred_element_type=F32)


def dot_nt(a, b):
    return lax.dot_general(a, b, (((1,), (1,)), ((), ())), preferred_element_type=F32)


def dot_tn(a, b):
    return lax.dot_general(a, b, (((0,), (0,)), ((), ())), preferred_element_type=F32)


def normalize(values, gain):
    average = jnp.mean(values, axis=-1, keepdims=True)
    centered = values - average
    inv_scale = lax.rsqrt(jnp.mean(centered * centered, axis=-1, keepdims=True) + EPSILON)
    return gain * centered * inv_scale


def normalize_back(values, gain, upstream):
    average = jnp.mean(values, axis=-1, keepdims=True)
    centered = values - average
    inv_scale = lax.rsqrt(jnp.mean(centered * centered, axis=-1, keepdims=True) + EPSILON)
    scaled = centered * inv_scale
    grad_scaled = upstream * gain
    first = jnp.mean(grad_scaled, axis=-1, keepdims=True)
    second = jnp.mean(grad_scaled * scaled, axis=-1, keepdims=True)
    return inv_scale * (grad_scaled - first - scaled * second)


def swish(values):
    return values * jax.nn.sigmoid(values)


def swish_slope(values):
    sigma = jax.nn.sigmoid(values)
    return sigma * (1.0 + values * (1.0 - sigma))


def rows_loop(total, step, fn):
    def one(i, carry):
        fn(pl.multiple_of(i * step, step))
        return carry

    lax.fori_loop(0, total // step, one, 0)


class Sems:
    def __init__(self, ref):
        self.ref = ref
        self.used = 0

    def take(self, count):
        base = self.used
        self.used += count
        return lambda i: self.ref.at[base + i]


N_SEM = 340


def kernel(
    snd_row, rcv_row, snd_lists, egain, ngain,
    nodes_hbm, ncot_hbm, edges_hbm, ein_hbm, eout_hbm, nin_hbm, nout_hbm, ecot_hbm,
    nodes_out, edges_out, ngrad, egrad, wout,
    nodes_in, ncot, nodes_out_v, edges_out_v, egrad_v, edges, ein, eout, nin, nout, ecot,
    ps, pr, pst, prt, tbl, sent_acc, sent, recv, pre, msg, hid,
    gsend, aggs_send, aggs_recv, aggx_send, aggx_recv, agg_own,
    agg, npre, nmsg, nhid, gdirect, dnpre, dnmsg, dagg_own, dagg,
    gedge, dmsg, dpre, dsent, drecv,
    gg_ssend, gg_srecv, gg_xsend, gg_xrecv, gg_own, a2_send, retg,
    own_ssend, own_srecv, own_xsend, own_xrecv, own_own,
    fn_ssend, fn_srecv, fn_own, fn_ysend, fn_yrecv, fn_ysum, fn_zsend, fn_zrecv, fn_zsum, fn_xsend, fn_xrecv,
    fe_ssend, fe_srecv, fe_own, fe_ysend, fe_yrecv, fe_ysum, fe_zsend, fe_zrecv, fe_zsum, fe_xsend, fe_xrecv,
    fo_ssend, fo_srecv, fo_own, fo_zsend, fo_zrecv, fo_zsum, fo_ysend, fo_yrecv, fo_ysum, fo_xsend, fo_xrecv,
    fin, rows_in,
    sem_ref,
):
    d = lax.axis_index("dom")
    s = lax.axis_index("esplit")
    y = d // NZ
    z = d % NZ
    x = s // 2
    c = s % 2
    lin = d * S + s
    sib = s + 1 - 2 * c
    t_mine = (s - d + DOM) % S
    sems = Sems(sem_ref)
    pending = []

    def remote(src, dst, send_sem, recv_sem, dom, split):
        return pltpu.make_async_remote_copy(
            src_ref=src, dst_ref=dst, send_sem=send_sem, recv_sem=recv_sem,
            device_id=(dom, split), device_id_type=MESH,
        )

    bar = pltpu.get_barrier_semaphore()

    def greet(dom, split):
        pl.semaphore_signal(bar, inc=1, device_id=(dom, split), device_id_type=MESH)

    for k in range(1, S):
        greet(d, (s + k) % S)
    for k in range(1, NY):
        greet((y + k) % NY * NZ + z, s)
    for k in range(1, NZ):
        greet(y * NZ + (z + k) % NZ, s)
    for j in range(NJ):
        pl.when(t_mine + S * j != d)(functools.partial(greet, t_mine + S * j, s))
    first_row = OUT_ROWS * lin
    b_first = first_row // 16
    b_last = (first_row + OUT_ROWS - 1) // 16

    def holder(b, half):
        r = b % DOM
        return jnp.where(b // DOM == 3, r % NY * NZ + r // NY, r), (b // DOM) % NX * 2 + half

    def from_other(slot, half):
        dom, split = holder(b_first + slot, half)
        here = dom * S + split != lin
        return here if slot == 0 else here & (b_last != b_first)

    for slot in range(2):
        for half in range(2):
            dom, split = holder(b_first + slot, half)
            pl.when(from_other(slot, half))(functools.partial(greet, dom, split))

    lsem = sems.take(9)
    loads = [
        pltpu.make_async_copy(a, b, lsem(i))
        for i, (a, b) in enumerate(
            ((edges_hbm, edges), (ein_hbm, ein), (eout_hbm, eout), (nin_hbm, nin),
             (nout_hbm, nout), (ecot_hbm, ecot), (nodes_hbm, nodes_in), (ncot_hbm, ncot),
             (nodes_hbm, tbl.at[pl.ds(pl.multiple_of(s * N, N), N), :])))
    ]
    ssem = sems.take(3)
    stores = [
        pltpu.make_async_copy(a, b, ssem(i))
        for i, (a, b) in enumerate(
            ((edges_out_v, edges_out), (nodes_out_v, nodes_out), (egrad_v, egrad)))
    ]

    def owner(group, i):
        b = DOM * (x + NX * group) + (d if group else jnp.where(x == 3, z * NY + y, d))
        to = (16 * b) // OUT_ROWS + i
        valid = to <= (16 * b + 15) // OUT_ROWS
        if group:
            valid = valid & (x < NMAT - NX)
        return to, b - (OUT_ROWS * to) // 16, valid

    arrivals = (S - 1) + (NY - 1) + (NZ - 1)
    for j in range(NJ):
        arrivals = arrivals + jnp.where(t_mine + S * j != d, 1, 0)
    for group in range(2):
        for i in range(3):
            to, _, valid = owner(group, i)
            arrivals = arrivals + jnp.where(valid & (to != lin), 1, 0)
    pl.semaphore_wait(bar, arrivals)

    def on_x(dx):
        return (x + dx + NX) % NX * 2 + c

    class Gather:
        def __init__(self, buf, offset, rows):
            self.buf, self.offset, self.rows = buf, offset, rows
            self.ss, self.rs = sems.take(7), sems.take(7)

        def copy(self, k, origin, split, src=None):
            there = self.buf.at[pl.ds(pl.multiple_of(self.offset(origin), self.rows), self.rows), :]
            here = there if src is None else src
            return remote(here, there, self.ss(k), self.rs(k), d, split)

        def send(self, k, origin, split, src=None):
            cp = self.copy(k, origin, split, src)
            cp.start()
            pending.append(cp)

        def start(self, src):
            for dx in (2, 1, 3):
                self.send(dx - 1, s, on_x(dx), src)
            self.send(3, s, sib, src)

        def forward(self, dx):
            origin = on_x(-dx)
            self.copy(dx - 1, origin, sib).wait_recv()
            self.send(3 + dx, origin, sib)

        def relay(self):
            self.forward(1)
            self.forward(3)

        def near(self):
            self.copy(3, sib, sib).wait_recv()
            for dx in (1, 3):
                self.copy(3 + dx, on_x(-dx) + 1 - 2 * c, sib).wait_recv()

        def far(self):
            self.copy(5, on_x(2) + 1 - 2 * c, sib).wait_recv()

        def finish(self):
            self.forward(2)
            self.near()
            self.far()

    def target(near, dx):
        return (x + dx) % NX * 2 + (c if near else 1 - c)

    class Scatter:
        def __init__(self, compute, own, ssend, srecv, xsend, xrecv):
            self.compute, self.own = compute, own
            self.ssend, self.srecv, self.xsend, self.xrecv = ssend, srecv, xsend, xrecv
            self.s1, self.r1 = sems.take(4), sems.take(4)
            self.s2, self.r2 = sems.take(3), sems.take(3)

        def to_sib(self, dx):
            return remote(self.ssend.at[dx], self.srecv.at[dx], self.s1(dx), self.r1(dx), d, sib)

        def to_chip(self, dx):
            return remote(
                self.xsend.at[dx - 1], self.xrecv.at[dx - 1], self.s2(dx - 1), self.r2(dx - 1),
                d, on_x(dx))

        def start(self):
            for dx in (2, 1, 3, 0):
                self.ssend[dx] = self.compute(0, dx).astype(BF)
                cp = self.to_sib(dx)
                cp.start()
                pending.append(cp)

        def middle(self):
            for dx in (2, 1, 3):
                mine = self.compute(1, dx)
                self.to_sib(dx).wait_recv()
                self.xsend[dx - 1] = (mine + self.srecv[dx].astype(F32)).astype(BF)
                cp = self.to_chip(dx)
                cp.start()
                pending.append(cp)
            mine = self.compute(1, 0)
            self.to_sib(0).wait_recv()
            self.own[...] = mine + self.srecv[0].astype(F32)

        def finish(self):
            total = self.own[...]
            for dx in (1, 3, 2):
                self.to_chip(dx).wait_recv()
                total = total + self.xrecv[dx - 1].astype(F32)
            return total

    class Swap:
        def __init__(self, src, dst):
            self.src, self.dst = src, dst
            self.ss, self.rs = sems.take(NJ), sems.take(NJ)

        def start(self):
            for j in range(NJ):
                peer = t_mine + S * j
                land = pl.multiple_of((d % S) * SLAB + (d // S) * GH, GH)
                cp = remote(
                    self.src.at[pl.ds(j * GH, GH), :], self.dst.at[pl.ds(land, GH), :],
                    self.ss(j), self.rs(d // S), peer, s)
                pl.when(peer != d)(cp.start)

                @pl.when(peer == d)
                def _():
                    self.dst[pl.ds(land, GH), :] = self.src[pl.ds(j * GH, GH), :]

        def finish(self):
            for j in range(NJ):
                peer = t_mine + S * j
                land = pl.multiple_of(t_mine * SLAB + j * GH, GH)
                cp = remote(
                    self.src.at[pl.ds(j * GH, GH), :], self.dst.at[pl.ds(land, GH), :],
                    self.ss(j), self.rs(j), peer, s)

                @pl.when(peer != d)
                def _():
                    cp.wait_recv()
                    cp.wait_send()

    gather_nodes = Gather(tbl, lambda q: q * N, N)
    gather_nodes.start(nodes_hbm)
    for i in (8, 0, 1):
        loads[i].start()

    def permuted(values):
        ghost = values - PN
        part = ghost // GH
        place = PN + (part % S) * SLAB + (part // S) * GH + ghost % GH
        return jnp.where(values >= PN, place, values)

    def column(row):
        size = row.shape[1]
        hit = lax.broadcasted_iota(jnp.int32, (size, size), 0) == lax.broadcasted_iota(
            jnp.int32, (size, size), 1)
        return jnp.sum(jnp.where(hit, row.astype(F32), 0.0), axis=1, keepdims=True).astype(jnp.int32)

    def hot(mask):
        return jnp.where(mask, 1.0, 0.0).astype(BF)

    send_r = permuted(snd_row[...])
    recv_r = rcv_row[...]
    send_c = column(send_r)
    recv_c = column(recv_r)

    def build_t(r0):
        ids = lax.broadcasted_iota(jnp.int32, (256, E), 0) + r0
        pst[pl.ds(r0, 256), :] = hot(ids == send_r)

    rows_loop(PN + S * SLAB, 256, build_t)

    for near in range(2):
        for dx in range(NX):
            r0 = (near * NX + dx) * N
            ids = lax.broadcasted_iota(jnp.int32, (N, E), 0) + target(near, dx) * N
            prt[r0:r0 + N, :] = hot(ids == recv_r)
    for c0 in range(0, PN + S * SLAB, 256):
        ids = lax.broadcasted_iota(jnp.int32, (E, 256), 1) + c0
        ps[:, c0:c0 + 256] = hot(ids == send_c)
        if c0 < PN:
            pr[:, c0:c0 + 256] = hot(ids == recv_c)

    lists = snd_lists[0]
    slot = lax.broadcasted_iota(jnp.int32, (S * SLAB, DOM), 0)
    part = slot // SLAB + (slot // GH) % NJ * S
    rows = hot(lax.broadcasted_iota(jnp.int32, (S * SLAB, DOM), 1) == part)
    high = dot_nt(rows, (lists // 32).astype(F32).astype(BF))
    low = dot_nt(rows, (lists % 32).astype(F32).astype(BF))
    slot = lax.broadcasted_iota(jnp.int32, (S * SLAB, GH), 0)
    here = lax.broadcasted_iota(jnp.int32, (S * SLAB, GH), 1) == slot % GH
    lists_c = jnp.sum(
        jnp.where(here, high * 32.0 + low, 0.0), axis=1, keepdims=True).astype(jnp.int32)

    loads[0].wait()
    loads[1].wait()

    def edge_part(r0):
        rows = pl.ds(r0, BLOCK)
        pre[rows, :] = dot(edges[rows, :], ein[0])

    rows_loop(E, BLOCK, edge_part)

    loads[8].wait()
    gather_nodes.relay()
    gather_nodes.finish()
    for i in (2, 6, 3, 4, 7, 5):
        loads[i].start()

    hit = jnp.zeros((SLAB, 1), jnp.int32)
    for t in range(S):
        hit = jnp.where(t_mine == t, lists_c[t * SLAB:(t + 1) * SLAB, :], hit)
    pick = hot(lax.broadcasted_iota(jnp.int32, (SLAB, PN), 1) == hit)
    gsend[...] = dot(pick, tbl[:PN, :]).astype(BF)
    ghosts = tbl.at[pl.ds(PN, S * SLAB), :]
    swap_ghost = Swap(gsend, ghosts)
    swap_ghost.start()

    def gather_recv(r0):
        rows = pl.ds(r0, BLOCK)
        got = dot(pr[rows, :], tbl[:PN, :]).astype(BF)
        recv[rows, :] = got
        pre[rows, :] = pre[rows, :] + dot(got, ein[2])

    rows_loop(E, BLOCK, gather_recv)
    swap_ghost.finish()
    gather_ghost = Gather(ghosts, lambda q: ((q - d + DOM) % S) * SLAB, SLAB)
    gather_ghost.start(ghosts.at[pl.ds(pl.multiple_of(t_mine * SLAB, SLAB), SLAB), :])

    def gather_sent(r0):
        rows = pl.ds(r0, BLOCK)
        sent_acc[rows, :] = dot(ps[rows, :PN], tbl[:PN, :])

    rows_loop(E, BLOCK, gather_sent)
    gather_ghost.relay()
    gather_ghost.finish()

    loads[2].wait()
    edge_gain = egain[...]

    def edge_forward(r0):
        rows = pl.ds(r0, BLOCK)
        got = (sent_acc[rows, :] + dot(ps[rows, PN:], tbl[PN:, :])).astype(BF)
        sent[rows, :] = got
        act = pre[rows, :] + dot(got, ein[1])
        pre[rows, :] = act
        hidden = swish(act).astype(BF)
        hid[rows, :] = hidden
        message = dot(hidden, eout[...])
        msg[rows, :] = message
        edges_out_v[rows, :] = (edges[rows, :].astype(F32) + normalize(message, edge_gain)).astype(BF)

    rows_loop(E, BLOCK, edge_forward)

    NH = N // 2

    agg_all = [None, None]

    def agg_block(half):
        def block(near, dx):
            if agg_all[near] is None:
                agg_all[near] = dot(prt[near * NX * N:(near + 1) * NX * N, :], edges_out_v[...])
            return agg_all[near][dx * N + half * NH:dx * N + (half + 1) * NH, :]

        return block

    reduce_agg = [
        Scatter(agg_block(h), agg_own.at[h], aggs_send.at[h], aggs_recv.at[h], aggx_send.at[h],
                aggx_recv.at[h])
        for h in range(2)
    ]
    gather_dagg = [
        Gather(dagg, functools.partial(lambda h, q: q * N + h * NH, h), NH) for h in range(2)
    ]
    for h in range(2):
        reduce_agg[h].start()
    for h in range(2):
        reduce_agg[h].middle()
    stores[0].start()
    loads[3].wait()
    loads[4].wait()
    loads[5].wait()
    loads[6].wait()
    loads[7].wait()
    npre[...] = dot(nodes_in[...], nin[0])
    node_gain = ngain[...]

    for h in range(2):
        rows = slice(h * NH, (h + 1) * NH)
        sums = reduce_agg[h].finish().astype(BF)
        agg[rows, :] = sums
        act = npre[rows, :] + dot(sums, nin[1])
        npre[rows, :] = act
        hidden = swish(act).astype(BF)
        nhid[rows, :] = hidden
        message = dot(hidden, nout[...])
        nmsg[rows, :] = message
        upstream = ncot[rows, :].astype(F32)
        grad_message = normalize_back(message, node_gain, upstream).astype(BF)
        dnmsg[rows, :] = grad_message
        grad_pre = (dot_nt(grad_message, nout[...]) * swish_slope(act)).astype(BF)
        dnpre[rows, :] = grad_pre
        dagg_own[rows, :] = dot_nt(grad_pre, nin[1]).astype(BF)
        dagg[pl.ds(pl.multiple_of(s * N + h * NH, NH), NH), :] = dagg_own[rows, :]
        gather_dagg[h].start(dagg_own.at[rows, :])
    gdirect[...] = ncot[...].astype(F32) + dot_nt(dnpre[...], nin[0])
    nodes_out_v[...] = (
        nodes_in[...].astype(F32) + normalize(nmsg[...], node_gain)).astype(BF)
    stores[1].start()

    mine_cols = pl.ds(pl.multiple_of(c * HALF, HALF), HALF)
    sib_cols = pl.ds(pl.multiple_of((1 - c) * HALF, HALF), HALF)

    class Products:
        def __init__(self, pairs, ssend, srecv, own):
            self.pairs, self.ssend, self.srecv, self.own = pairs, ssend, srecv, own
            self.s0, self.r0 = sems.take(len(pairs)), sems.take(len(pairs))

        def sib_copy(self, i):
            return remote(self.ssend.at[i], self.srecv.at[i], self.s0(i), self.r0(i), d, sib)

        def products(self, i):
            left, right = self.pairs[i]
            columns = jnp.concatenate([right[:, sib_cols], right[:, mine_cols]], axis=1)
            grad = dot_tn(left[...], columns)
            self.ssend[i] = grad[:, :HALF].astype(BF)
            cp = self.sib_copy(i)
            cp.start()
            pending.append(cp)
            self.own[i] = grad[:, HALF:]

        def chip_sum(self, i, rows):
            return self.own[i, rows, :] + self.srecv[i, rows, :].astype(F32)

    class Peers:
        def __init__(self, count, send, recv, to):
            self.count, self.sbuf, self.rbuf, self.to = count, send, recv, to
            self.ss, self.rs = sems.take(count - 1), sems.take(count - 1)

        def copy(self, k):
            return remote(
                self.sbuf.at[k - 1], self.rbuf.at[k - 1], self.ss(k - 1), self.rs(k - 1),
                *self.to(k))

        def send(self, k, value):
            self.sbuf[k - 1] = value.astype(BF)
            cp = self.copy(k)
            cp.start()
            pending.append(cp)

        def total(self, mine):
            for k in range(1, self.count):
                self.copy(k).wait_recv()
                mine = mine + self.rbuf[k - 1].astype(F32)
            return mine

    def on_y(k):
        return (y + k) % NY * NZ + z, s

    def on_z(k):
        return y * NZ + (z + k) % NZ, s

    Z_ORDER = (4, 3, 5, 2, 6, 1, 7)

    class Weights(Products):
        def __init__(self, pairs, ssend, srecv, own, ysend, yrecv, ysum, zsend, zrecv, zsum, xsend, xrecv):
            super().__init__(pairs, ssend, srecv, own)
            self.y = [Peers(NY, ysend.at[i], yrecv.at[i], on_y) for i in range(3)]
            self.z = [Peers(NZ, zsend.at[i], zrecv.at[i], on_z) for i in range(3)]
            self.ysum, self.zsum, self.xsend, self.xrecv = ysum, zsum, xsend, xrecv
            self.sx, self.rx = sems.take(NX - 1), sems.take(NX - 1)

        def to_y(self, i):
            self.sib_copy(i).wait_recv()
            for k in (2, 1, 3):
                rows = pl.ds(pl.multiple_of((y + k) % NY * 128, 128), 128)
                self.y[i].send(k, self.chip_sum(i, rows))

        def to_z(self, i):
            rows = pl.ds(pl.multiple_of(y * 128, 128), 128)
            self.ysum[i] = self.y[i].total(self.chip_sum(i, rows))
            for k in Z_ORDER:
                rows = pl.ds(pl.multiple_of((z + k) % NZ * 16, 16), 16)
                self.z[i].send(k, self.ysum[i, rows, :])

        def x_copy(self, k):
            return remote(
                self.xsend.at[k - 1], self.xrecv.at[k - 1], self.sx(k - 1), self.rx(k - 1),
                d, on_x(k))

        def to_x(self):
            rows = pl.ds(pl.multiple_of(z * 16, 16), 16)
            for i in range(3):
                self.zsum[i] = self.z[i].total(self.ysum[i, rows, :])
            for k in (2, 1, 3):
                @pl.when((x + k) % NX < 3)
                def _():
                    self.xsend[k - 1] = self.zsum[(x + k) % NX].astype(BF)
                    self.x_copy(k).start()

        def finish(self):
            total = self.zsum[jnp.minimum(x, 2)]
            for k in (1, 3, 2):
                self.x_copy(k).wait_recv()
                total = total + self.xrecv[k - 1].astype(F32)
            return total

        def drain(self):
            for k in (2, 1, 3):
                pl.when((x + k) % NX < 3)(self.x_copy(k).wait_send)

    class LastWeights(Products):
        def __init__(self, pairs, ssend, srecv, own, zsend, zrecv, zsum, ysend, yrecv, ysum, xsend, xrecv):
            super().__init__(pairs, ssend, srecv, own)
            self.zsum, self.ysum, self.xsend, self.xrecv = zsum, ysum, xsend, xrecv
            self.z = Peers(NZ, zsend, zrecv, on_z)
            self.y = Peers(NY, ysend, yrecv, on_y)
            self.sx, self.rx = sems.take(1), sems.take(3)

        def to_z(self):
            self.sib_copy(0).wait_recv()
            for k in Z_ORDER:
                rows = pl.ds(pl.multiple_of((z + k) % NZ * 64, 64), 64)
                self.z.send(k, self.chip_sum(0, rows))

        def to_y(self):
            rows = pl.ds(pl.multiple_of(z * 64, 64), 64)
            self.zsum[...] = self.z.total(self.chip_sum(0, rows))
            for k in (2, 1, 3):
                rows = pl.ds(pl.multiple_of((y + k) % NY * 16, 16), 16)
                self.y.send(k, self.zsum[rows, :])

        def x_copy(self, k):
            return remote(self.xsend, self.xrecv.at[k], self.sx(0), self.rx(k), d, 6 + c)

        def to_x(self):
            total = self.y.total(self.zsum[pl.ds(pl.multiple_of(y * 16, 16), 16), :])
            self.ysum[...] = total
            self.xsend[...] = total.astype(BF)
            for k in range(3):
                pl.when(x == k)(self.x_copy(k).start)

        def finish(self):
            total = self.ysum[...]
            for k in range(3):
                self.x_copy(k).wait_recv()
                total = total + self.xrecv[k].astype(F32)
            return total

        def drain(self):
            pl.when(x < 3)(self.x_copy(0).wait_send)

    node_weights = Weights(
        ((nodes_in, dnpre), (agg, dnpre), (nhid, dnmsg)),
        fn_ssend, fn_srecv, fn_own, fn_ysend, fn_yrecv, fn_ysum, fn_zsend, fn_zrecv, fn_zsum,
        fn_xsend, fn_xrecv)
    edge_weights = Weights(
        ((edges, dpre), (sent, dpre), (recv, dpre)),
        fe_ssend, fe_srecv, fe_own, fe_ysend, fe_yrecv, fe_ysum, fe_zsend, fe_zrecv, fe_zsum,
        fe_xsend, fe_xrecv)
    out_weights = LastWeights(
        ((hid, dmsg),),
        fo_ssend, fo_srecv, fo_own, fo_zsend, fo_zrecv, fo_zsum, fo_ysend, fo_yrecv, fo_ysum,
        fo_xsend, fo_xrecv)

    for i in range(3):
        node_weights.products(i)
    for i in range(3):
        node_weights.to_y(i)
    for h in range(2):
        gather_dagg[h].relay()
    for h in range(2):
        gather_dagg[h].forward(2)
    for h in range(2):
        gather_dagg[h].near()

    def chip_part(dx):
        rows = pl.ds(pl.multiple_of((x + dx) % NX * 2 * N, 2 * N), 2 * N)
        return dot(pr[:, rows], dagg[rows, :])

    gedge[...] = ecot[...].astype(F32) + chip_part(0)
    gedge[...] = gedge[...] + chip_part(1)
    gedge[...] = gedge[...] + chip_part(3)
    for h in range(2):
        gather_dagg[h].far()

    def edge_backward(r0):
        rows = pl.ds(r0, BLOCK)
        up = gedge[rows, :] + chip_part(2)
        gedge[rows, :] = up
        grad_msg = normalize_back(msg[rows, :], edge_gain, up).astype(BF)
        dmsg[rows, :] = grad_msg
        grad = (dot_nt(grad_msg, eout[...]) * swish_slope(pre[rows, :])).astype(BF)
        dpre[rows, :] = grad

    rows_loop(E, BLOCK, edge_backward)

    def ghost_block(near, dx):
        place = PN + ((target(near, dx) - d + DOM) % S) * SLAB
        return dot(pst[pl.ds(pl.multiple_of(place, SLAB), SLAB), :], dsent[...])

    edge_weights.products(0)
    out_weights.products(0)

    def send_grad(r0):
        rows = pl.ds(r0, BLOCK)
        dsent[rows, :] = dot_nt(dpre[rows, :], ein[1]).astype(BF)

    rows_loop(E, BLOCK, send_grad)
    reduce_ghost = Scatter(ghost_block, gg_own, gg_ssend, gg_srecv, gg_xsend, gg_xrecv)
    reduce_ghost.start()
    edge_weights.to_y(0)
    edge_weights.products(1)
    out_weights.to_z()
    reduce_ghost.middle()
    edge_weights.to_y(1)
    edge_weights.products(2)

    def recv_grad(r0):
        rows = pl.ds(r0, BLOCK)
        drecv[rows, :] = dot_nt(dpre[rows, :], ein[2]).astype(BF)

    rows_loop(E, BLOCK, recv_grad)
    edge_weights.to_y(2)

    def own_block(near, dx):
        rows = pl.ds(pl.multiple_of(target(near, dx) * N, N), N)
        r0 = (near * NX + dx) * N
        return dot(pst[rows, :], dsent[...]) + dot(prt[r0:r0 + N, :], drecv[...])

    reduce_own = Scatter(own_block, own_own, own_ssend, own_srecv, own_xsend, own_xrecv)
    reduce_own.start()
    reduce_own.middle()
    a2_send[...] = reduce_ghost.finish().astype(BF)
    swap_back = Swap(a2_send, retg)
    swap_back.start()
    for i in range(3):
        node_weights.to_z(i)

    def edge_grad(r0):
        rows = pl.ds(r0, BLOCK)
        egrad_v[rows, :] = (gedge[rows, :] + dot_nt(dpre[rows, :], ein[0])).astype(BF)

    rows_loop(E, BLOCK, edge_grad)
    stores[2].start()
    place = hot(lax.broadcasted_iota(jnp.int32, (S * SLAB, N), 1) + s * N == lists_c)
    swap_back.finish()
    gather_back = Gather(retg, lambda q: ((q - d + DOM) % S) * SLAB, SLAB)
    gather_back.start(retg.at[pl.ds(pl.multiple_of(t_mine * SLAB, SLAB), SLAB), :])
    edge_weights.to_z(0)
    out_weights.to_y()
    node_weights.to_x()
    edge_weights.to_z(1)
    edge_weights.to_z(2)
    s_fin, r_fin = sems.take(6), sems.take(4)

    def fin_copy(group, i, slot, half):
        to = jnp.minimum(owner(group, i)[0], DOM * S - 1)
        return remote(
            fin.at[group], rows_in.at[slot, half], s_fin(3 * group + i), r_fin(2 * slot + half),
            to // S, to % S)

    def hand_out(group):
        for i in range(3):
            to, at, valid = owner(group, i)
            for slot in range(2):
                for half in range(2):
                    here = valid & (at == slot) & (c == half)
                    pl.when(here & (to != lin))(fin_copy(group, i, slot, half).start)

                    @pl.when(here & (to == lin))
                    def _():
                        rows_in[slot, half] = fin[group]

    out_weights.to_x()
    edge_weights.to_x()
    gather_back.relay()
    @pl.when(x < 3)
    def _():
        fin[1] = node_weights.finish()

    hand_out(1)

    gather_back.finish()
    direct = gdirect[...] + dot_tn(place, retg[...])
    ngrad[...] = (direct + reduce_own.finish()).astype(BF)

    @pl.when(x < 3)
    def _():
        fin[0] = edge_weights.finish()

    @pl.when(x == 3)
    def _():
        fin[0] = out_weights.finish()

    hand_out(0)
    for slot in range(2):
        for half in range(2):
            pl.when(from_other(slot, half))(fin_copy(0, 0, slot, half).wait_recv)
    shift = first_row % 16
    for choice in range(0, 16, 2):
        @pl.when(shift == choice)
        def _():
            split = min(16 - choice, OUT_ROWS)
            for half in range(2):
                cols = slice(half * HALF, (half + 1) * HALF)
                wout[:split, cols] = rows_in[0, half, choice:choice + split, :]
                if split < OUT_ROWS:
                    wout[split:, cols] = rows_in[1, half, :OUT_ROWS - split, :]

    for store in stores:
        store.wait()
    for cp in pending:
        cp.wait_send()
    node_weights.drain()
    edge_weights.drain()
    out_weights.drain()
    for group in range(2):
        for i in range(3):
            to, _, valid = owner(group, i)
            pl.when(valid & (to != lin))(fin_copy(group, i, 0, 0).wait_send)


def scratch():
    def bf(*shape):
        return pltpu.VMEM(shape, BF)

    def f32(*shape):
        return pltpu.VMEM(shape, F32)

    T = PN + S * SLAB

    def scatter(rows, *lead):
        return [
            bf(*lead, NX, rows, D), bf(*lead, NX, rows, D), bf(*lead, NX - 1, rows, D),
            bf(*lead, NX - 1, rows, D), f32(*lead, rows, D),
        ]

    def products(count):
        return [bf(count, D, HALF), bf(count, D, HALF), f32(count, D, HALF)]

    def weights():
        return [
            *products(3), bf(3, NY - 1, 128, HALF), bf(3, NY - 1, 128, HALF), f32(3, 128, HALF),
            bf(3, NZ - 1, 16, HALF), bf(3, NZ - 1, 16, HALF), f32(3, 16, HALF),
            bf(NX - 1, 16, HALF), bf(NX - 1, 16, HALF),
        ]

    return [
        bf(N, D), bf(N, D), bf(N, D), bf(E, D), bf(E, D),
        bf(E, D), bf(3, D, D), bf(D, D), bf(2, D, D), bf(D, D), bf(E, D),
        bf(E, T), bf(E, PN), bf(T, E), bf(PN, E), bf(T, D), f32(E, D), bf(E, D), bf(E, D),
        f32(E, D), f32(E, D), bf(E, D),
        bf(SLAB, D), *scatter(N // 2, 2),
        bf(N, D), f32(N, D), f32(N, D), bf(N, D), f32(N, D), bf(N, D), bf(N, D), bf(N, D), bf(PN, D),
        f32(E, D), bf(E, D), bf(E, D), bf(E, D), bf(E, D),
        *scatter(SLAB), bf(SLAB, D), bf(S * SLAB, D), *scatter(N),
        *weights(), *weights(),
        *products(1), bf(NZ - 1, 64, HALF), bf(NZ - 1, 64, HALF), f32(64, HALF),
        bf(NY - 1, 16, HALF), bf(NY - 1, 16, HALF), f32(16, HALF), bf(16, HALF), bf(NX - 1, 16, HALF),
        f32(2, 16, HALF), f32(2, 2, 16, HALF),
        pltpu.SemaphoreType.DMA((N_SEM,)),
    ]


def hand_over(a0, a1, a2, a3, w_in, b0, b1, b2, b3, w_out):
    for src, dst in ((a0, b0), (a1, b1), (a2, b2), (a3, b3)):
        dst[...] = src[...]
    for i in range(OUT_ROWS):
        w_out[:, i * D:(i + 1) * D] = w_in[i:i + 1, :]


def body(
    node_state, edge_state, senders, receivers, send_rows, edge_in, edge_out, edge_gain,
    node_in, node_out, node_gain, node_cot, edge_cot,
):
    vmem = pl.BlockSpec(memory_space=pltpu.VMEM)
    hbm = pl.BlockSpec(memory_space=pl.ANY)
    states = (
        jax.ShapeDtypeStruct((N, D), BF),
        jax.ShapeDtypeStruct((E, D), BF),
        jax.ShapeDtypeStruct((N, D), BF),
        jax.ShapeDtypeStruct((E, D), BF),
    )
    results = pl.pallas_call(
        kernel,
        out_shape=states + (jax.ShapeDtypeStruct((OUT_ROWS, D), F32),),
        in_specs=[vmem] * 5 + [hbm] * 8,
        out_specs=[hbm, hbm, vmem, hbm, vmem],
        scratch_shapes=scratch(),
        compiler_params=pltpu.CompilerParams(
            collective_id=0, has_side_effects=True, vmem_limit_bytes=60 * 1024 * 1024),
    )(
        senders.reshape(1, E), receivers.reshape(1, E), send_rows.transpose(0, 2, 1),
        edge_gain, node_gain,
        node_state, node_cot, edge_state, edge_in[0], edge_out[0], node_in[0], node_out[0], edge_cot,
    )
    return pl.pallas_call(
        hand_over,
        out_shape=states + (jax.ShapeDtypeStruct((1, OUT_ROWS * D), F32),),
        in_specs=[vmem] * 5,
        out_specs=[vmem] * 5,
    )(*results)


def solution(mesh):
    both = P(("dom", "esplit"), None)
    in_specs = (
        both, both, P(("dom", "esplit")), P(("dom", "esplit")), P("dom", None, None),
        P(), P(), P(), P(), P(), P(), both, both,
    )
    out_specs = (both, both, both, both, P(None, ("dom", "esplit")))
    return jax.shard_map(body, mesh=mesh, in_specs=in_specs, out_specs=out_specs, check_vma=False)
```

```python
import functools

import jax
import jax.numpy as jnp
from jax import lax
from jax.experimental import pallas as pl
from jax.experimental.pallas import tpu as pltpu
from jax.sharding import PartitionSpec as P

EPSILON = 1e-05
BF = jnp.bfloat16
F32 = jnp.float32
MESH = pl.DeviceIdType.MESH

NZ = 8
NY = 4
NX = 4
DOM = NY * NZ
S = NX * 2
D = 512
N = 128
PN = N * S
E = 512
GH = 16
SLAB = DOM // S * GH
NJ = DOM // S
HALF = D // 2
NMAT = 7
OUT_ROWS = 14
BLOCK = 512


def dot(a, b):
    return lax.dot_general(a, b, (((1,), (0,)), ((), ())), preferred_element_type=F32)


def dot_nt(a, b):
    return lax.dot_general(a, b, (((1,), (1,)), ((), ())), preferred_element_type=F32)


def dot_tn(a, b):
    return lax.dot_general(a, b, (((0,), (0,)), ((), ())), preferred_element_type=F32)


def normalize(values, gain):
    average = jnp.mean(values, axis=-1, keepdims=True)
    centered = values - average
    inv_scale = lax.rsqrt(jnp.mean(centered * centered, axis=-1, keepdims=True) + EPSILON)
    return gain * centered * inv_scale


def normalize_back(values, gain, upstream):
    average = jnp.mean(values, axis=-1, keepdims=True)
    centered = values - average
    inv_scale = lax.rsqrt(jnp.mean(centered * centered, axis=-1, keepdims=True) + EPSILON)
    scaled = centered * inv_scale
    grad_scaled = upstream * gain
    first = jnp.mean(grad_scaled, axis=-1, keepdims=True)
    second = jnp.mean(grad_scaled * scaled, axis=-1, keepdims=True)
    return inv_scale * (grad_scaled - first - scaled * second)


def swish(values):
    return values * jax.nn.sigmoid(values)


def swish_slope(values):
    sigma = jax.nn.sigmoid(values)
    return sigma * (1.0 + values * (1.0 - sigma))


def rows_loop(total, step, fn):
    def one(i, carry):
        fn(pl.multiple_of(i * step, step))
        return carry

    lax.fori_loop(0, total // step, one, 0)


class Sems:
    def __init__(self, ref):
        self.ref = ref
        self.used = 0

    def take(self, count):
        base = self.used
        self.used += count
        return lambda i: self.ref.at[base + i]


N_SEM = 340


def kernel(
    snd_row, rcv_row, snd_lists, egain, ngain,
    nodes_hbm, ncot_hbm, edges_hbm, ein_hbm, eout_hbm, nin_hbm, nout_hbm, ecot_hbm,
    nodes_out, edges_out, ngrad, egrad, wout,
    nodes_in, ncot, nodes_out_v, edges_out_v, egrad_v, edges, ein, eout, nin, nout, ecot,
    ps, pr, pst, prt, tbl, sent_acc, sent, recv, pre, msg, hid,
    gsend, aggs_send, aggs_recv, aggx_send, aggx_recv, agg_own,
    agg, npre, nmsg, nhid, gdirect, dnpre, dnmsg, dagg_own, dagg,
    gedge, dmsg, dpre, dsent, drecv,
    gg_ssend, gg_srecv, gg_xsend, gg_xrecv, gg_own, a2_send, retg,
    own_ssend, own_srecv, own_xsend, own_xrecv, own_own,
    fn_ssend, fn_srecv, fn_own, fn_ysend, fn_yrecv, fn_ysum, fn_zsend, fn_zrecv, fn_zsum, fn_xsend, fn_xrecv,
    fe_ssend, fe_srecv, fe_own, fe_ysend, fe_yrecv, fe_ysum, fe_zsend, fe_zrecv, fe_zsum, fe_xsend, fe_xrecv,
    fo_ssend, fo_srecv, fo_own, fo_zsend, fo_zrecv, fo_zsum, fo_ysend, fo_yrecv, fo_ysum, fo_xsend, fo_xrecv,
    fin, rows_in,
    sem_ref,
):
    d = lax.axis_index("dom")
    s = lax.axis_index("esplit")
    y = d // NZ
    z = d % NZ
    x = s // 2
    c = s % 2
    lin = d * S + s
    sib = s + 1 - 2 * c
    t_mine = (s - d + DOM) % S
    sems = Sems(sem_ref)
    pending = []

    def remote(src, dst, send_sem, recv_sem, dom, split):
        return pltpu.make_async_remote_copy(
            src_ref=src, dst_ref=dst, send_sem=send_sem, recv_sem=recv_sem,
            device_id=(dom, split), device_id_type=MESH,
        )

    bar = pltpu.get_barrier_semaphore()

    def greet(dom, split):
        pl.semaphore_signal(bar, inc=1, device_id=(dom, split), device_id_type=MESH)

    for k in range(1, S):
        greet(d, (s + k) % S)
    for k in range(1, NY):
        greet((y + k) % NY * NZ + z, s)
    for k in range(1, NZ):
        greet(y * NZ + (z + k) % NZ, s)
    for j in range(NJ):
        pl.when(t_mine + S * j != d)(functools.partial(greet, t_mine + S * j, s))
    first_row = OUT_ROWS * lin
    b_first = first_row // 16
    b_last = (first_row + OUT_ROWS - 1) // 16

    def holder(b, half):
        r = b % DOM
        return jnp.where(b // DOM == 3, r % NY * NZ + r // NY, r), (b // DOM) % NX * 2 + half

    def from_other(slot, half):
        dom, split = holder(b_first + slot, half)
        here = dom * S + split != lin
        return here if slot == 0 else here & (b_last != b_first)

    for slot in range(2):
        for half in range(2):
            dom, split = holder(b_first + slot, half)
            pl.when(from_other(slot, half))(functools.partial(greet, dom, split))

    lsem = sems.take(9)
    loads = [
        pltpu.make_async_copy(a, b, lsem(i))
        for i, (a, b) in enumerate(
            ((edges_hbm, edges), (ein_hbm, ein), (eout_hbm, eout), (nin_hbm, nin),
             (nout_hbm, nout), (ecot_hbm, ecot), (nodes_hbm, nodes_in), (ncot_hbm, ncot),
             (nodes_hbm, tbl.at[pl.ds(pl.multiple_of(s * N, N), N), :])))
    ]
    ssem = sems.take(3)
    stores = [
        pltpu.make_async_copy(a, b, ssem(i))
        for i, (a, b) in enumerate(
            ((edges_out_v, edges_out), (nodes_out_v, nodes_out), (egrad_v, egrad)))
    ]

    def owner(group, i):
        b = DOM * (x + NX * group) + (d if group else jnp.where(x == 3, z * NY + y, d))
        to = (16 * b) // OUT_ROWS + i
        valid = to <= (16 * b + 15) // OUT_ROWS
        if group:
            valid = valid & (x < NMAT - NX)
        return to, b - (OUT_ROWS * to) // 16, valid

    arrivals = (S - 1) + (NY - 1) + (NZ - 1)
    for j in range(NJ):
        arrivals = arrivals + jnp.where(t_mine + S * j != d, 1, 0)
    for group in range(2):
        for i in range(3):
            to, _, valid = owner(group, i)
            arrivals = arrivals + jnp.where(valid & (to != lin), 1, 0)
    pl.semaphore_wait(bar, arrivals)

    def on_x(dx):
        return (x + dx + NX) % NX * 2 + c

    class Gather:
        def __init__(self, buf, offset, rows):
            self.buf, self.offset, self.rows = buf, offset, rows
            self.ss, self.rs = sems.take(7), sems.take(7)

        def copy(self, k, origin, split, src=None):
            there = self.buf.at[pl.ds(pl.multiple_of(self.offset(origin), self.rows), self.rows), :]
            here = there if src is None else src
            return remote(here, there, self.ss(k), self.rs(k), d, split)

        def send(self, k, origin, split, src=None):
            cp = self.copy(k, origin, split, src)
            cp.start()
            pending.append(cp)

        def start(self, src):
            for dx in (2, 1, 3):
                self.send(dx - 1, s, on_x(dx), src)
            self.send(3, s, sib, src)

        def forward(self, dx):
            origin = on_x(-dx)
            self.copy(dx - 1, origin, sib).wait_recv()
            self.send(3 + dx, origin, sib)

        def relay(self):
            self.forward(1)
            self.forward(3)

        def near(self):
            self.copy(3, sib, sib).wait_recv()
            for dx in (1, 3):
                self.copy(3 + dx, on_x(-dx) + 1 - 2 * c, sib).wait_recv()

        def far(self):
            self.copy(5, on_x(2) + 1 - 2 * c, sib).wait_recv()

        def finish(self):
            self.forward(2)
            self.near()
            self.far()

    def target(near, dx):
        return (x + dx) % NX * 2 + (c if near else 1 - c)

    class Scatter:
        def __init__(self, compute, own, ssend, srecv, xsend, xrecv):
            self.compute, self.own = compute, own
            self.ssend, self.srecv, self.xsend, self.xrecv = ssend, srecv, xsend, xrecv
            self.s1, self.r1 = sems.take(4), sems.take(4)
            self.s2, self.r2 = sems.take(3), sems.take(3)

        def to_sib(self, dx):
            return remote(self.ssend.at[dx], self.srecv.at[dx], self.s1(dx), self.r1(dx), d, sib)

        def to_chip(self, dx):
            return remote(
                self.xsend.at[dx - 1], self.xrecv.at[dx - 1], self.s2(dx - 1), self.r2(dx - 1),
                d, on_x(dx))

        def start(self):
            for dx in (2, 1, 3, 0):
                self.ssend[dx] = self.compute(0, dx).astype(BF)
                cp = self.to_sib(dx)
                cp.start()
                pending.append(cp)

        def middle(self):
            for dx in (2, 1, 3):
                mine = self.compute(1, dx)
                self.to_sib(dx).wait_recv()
                self.xsend[dx - 1] = (mine + self.srecv[dx].astype(F32)).astype(BF)
                cp = self.to_chip(dx)
                cp.start()
                pending.append(cp)
            mine = self.compute(1, 0)
            self.to_sib(0).wait_recv()
            self.own[...] = mine + self.srecv[0].astype(F32)

        def finish(self):
            total = self.own[...]
            for dx in (1, 3, 2):
                self.to_chip(dx).wait_recv()
                total = total + self.xrecv[dx - 1].astype(F32)
            return total

    class Swap:
        def __init__(self, src, dst):
            self.src, self.dst = src, dst
            self.ss, self.rs = sems.take(NJ), sems.take(NJ)

        def start(self):
            for j in range(NJ):
                peer = t_mine + S * j
                land = pl.multiple_of((d % S) * SLAB + (d // S) * GH, GH)
                cp = remote(
                    self.src.at[pl.ds(j * GH, GH), :], self.dst.at[pl.ds(land, GH), :],
                    self.ss(j), self.rs(d // S), peer, s)
                pl.when(peer != d)(cp.start)

                @pl.when(peer == d)
                def _():
                    self.dst[pl.ds(land, GH), :] = self.src[pl.ds(j * GH, GH), :]

        def finish(self):
            for j in range(NJ):
                peer = t_mine + S * j
                land = pl.multiple_of(t_mine * SLAB + j * GH, GH)
                cp = remote(
                    self.src.at[pl.ds(j * GH, GH), :], self.dst.at[pl.ds(land, GH), :],
                    self.ss(j), self.rs(j), peer, s)

                @pl.when(peer != d)
                def _():
                    cp.wait_recv()
                    cp.wait_send()

    gather_nodes = Gather(tbl, lambda q: q * N, N)
    gather_nodes.start(nodes_hbm)
    for i in (8, 0, 1):
        loads[i].start()

    def permuted(values):
        ghost = values - PN
        part = ghost // GH
        place = PN + (part % S) * SLAB + (part // S) * GH + ghost % GH
        return jnp.where(values >= PN, place, values)

    def column(row):
        size = row.shape[1]
        hit = lax.broadcasted_iota(jnp.int32, (size, size), 0) == lax.broadcasted_iota(
            jnp.int32, (size, size), 1)
        return jnp.sum(jnp.where(hit, row.astype(F32), 0.0), axis=1, keepdims=True).astype(jnp.int32)

    def hot(mask):
        return jnp.where(mask, 1.0, 0.0).astype(BF)

    send_r = permuted(snd_row[...])
    recv_r = rcv_row[...]
    send_c = column(send_r)
    recv_c = column(recv_r)

    def build_t(r0):
        ids = lax.broadcasted_iota(jnp.int32, (256, E), 0) + r0
        pst[pl.ds(r0, 256), :] = hot(ids == send_r)

    rows_loop(PN + S * SLAB, 256, build_t)

    for near in range(2):
        for dx in range(NX):
            r0 = (near * NX + dx) * N
            ids = lax.broadcasted_iota(jnp.int32, (N, E), 0) + target(near, dx) * N
            prt[r0:r0 + N, :] = hot(ids == recv_r)
    for c0 in range(0, PN + S * SLAB, 256):
        ids = lax.broadcasted_iota(jnp.int32, (E, 256), 1) + c0
        ps[:, c0:c0 + 256] = hot(ids == send_c)
        if c0 < PN:
            pr[:, c0:c0 + 256] = hot(ids == recv_c)

    lists = snd_lists[0]
    slot = lax.broadcasted_iota(jnp.int32, (S * SLAB, DOM), 0)
    part = slot // SLAB + (slot // GH) % NJ * S
    rows = hot(lax.broadcasted_iota(jnp.int32, (S * SLAB, DOM), 1) == part)
    high = dot_nt(rows, (lists // 32).astype(F32).astype(BF))
    low = dot_nt(rows, (lists % 32).astype(F32).astype(BF))
    slot = lax.broadcasted_iota(jnp.int32, (S * SLAB, GH), 0)
    here = lax.broadcasted_iota(jnp.int32, (S * SLAB, GH), 1) == slot % GH
    lists_c = jnp.sum(
        jnp.where(here, high * 32.0 + low, 0.0), axis=1, keepdims=True).astype(jnp.int32)

    loads[0].wait()
    loads[1].wait()

    def edge_part(r0):
        rows = pl.ds(r0, BLOCK)
        pre[rows, :] = dot(edges[rows, :], ein[0])

    rows_loop(E, BLOCK, edge_part)

    loads[8].wait()
    gather_nodes.relay()
    gather_nodes.finish()
    for i in (2, 6, 3, 4, 7, 5):
        loads[i].start()

    hit = jnp.zeros((SLAB, 1), jnp.int32)
    for t in range(S):
        hit = jnp.where(t_mine == t, lists_c[t * SLAB:(t + 1) * SLAB, :], hit)
    pick = hot(lax.broadcasted_iota(jnp.int32, (SLAB, PN), 1) == hit)
    gsend[...] = dot(pick, tbl[:PN, :]).astype(BF)
    ghosts = tbl.at[pl.ds(PN, S * SLAB), :]
    swap_ghost = Swap(gsend, ghosts)
    swap_ghost.start()

    def gather_recv(r0):
        rows = pl.ds(r0, BLOCK)
        got = dot(pr[rows, :], tbl[:PN, :]).astype(BF)
        recv[rows, :] = got
        pre[rows, :] = pre[rows, :] + dot(got, ein[2])

    rows_loop(E, BLOCK, gather_recv)
    swap_ghost.finish()
    gather_ghost = Gather(ghosts, lambda q: ((q - d + DOM) % S) * SLAB, SLAB)
    gather_ghost.start(ghosts.at[pl.ds(pl.multiple_of(t_mine * SLAB, SLAB), SLAB), :])

    def gather_sent(r0):
        rows = pl.ds(r0, BLOCK)
        sent_acc[rows, :] = dot(ps[rows, :PN], tbl[:PN, :])

    rows_loop(E, BLOCK, gather_sent)
    gather_ghost.relay()
    gather_ghost.finish()

    loads[2].wait()
    edge_gain = egain[...]

    def edge_forward(r0):
        rows = pl.ds(r0, BLOCK)
        got = (sent_acc[rows, :] + dot(ps[rows, PN:], tbl[PN:, :])).astype(BF)
        sent[rows, :] = got
        act = pre[rows, :] + dot(got, ein[1])
        pre[rows, :] = act
        hidden = swish(act).astype(BF)
        hid[rows, :] = hidden
        message = dot(hidden, eout[...])
        msg[rows, :] = message
        edges_out_v[rows, :] = (edges[rows, :].astype(F32) + normalize(message, edge_gain)).astype(BF)

    rows_loop(E, BLOCK, edge_forward)

    NH = N // 2

    agg_all = [None, None]

    def agg_block(half):
        def block(near, dx):
            if agg_all[near] is None:
                agg_all[near] = dot(prt[near * NX * N:(near + 1) * NX * N, :], edges_out_v[...])
            return agg_all[near][dx * N + half * NH:dx * N + (half + 1) * NH, :]

        return block

    reduce_agg = [
        Scatter(agg_block(h), agg_own.at[h], aggs_send.at[h], aggs_recv.at[h], aggx_send.at[h],
                aggx_recv.at[h])
        for h in range(2)
    ]
    gather_dagg = [
        Gather(dagg, functools.partial(lambda h, q: q * N + h * NH, h), NH) for h in range(2)
    ]
    for h in range(2):
        reduce_agg[h].start()
    for h in range(2):
        reduce_agg[h].middle()
    stores[0].start()
    loads[3].wait()
    loads[4].wait()
    loads[5].wait()
    loads[6].wait()
    loads[7].wait()
    npre[...] = dot(nodes_in[...], nin[0])
    node_gain = ngain[...]

    for h in range(2):
        rows = slice(h * NH, (h + 1) * NH)
        sums = reduce_agg[h].finish().astype(BF)
        agg[rows, :] = sums
        act = npre[rows, :] + dot(sums, nin[1])
        npre[rows, :] = act
        hidden = swish(act).astype(BF)
        nhid[rows, :] = hidden
        message = dot(hidden, nout[...])
        nmsg[rows, :] = message
        upstream = ncot[rows, :].astype(F32)
        grad_message = normalize_back(message, node_gain, upstream).astype(BF)
        dnmsg[rows, :] = grad_message
        grad_pre = (dot_nt(grad_message, nout[...]) * swish_slope(act)).astype(BF)
        dnpre[rows, :] = grad_pre
        dagg_own[rows, :] = dot_nt(grad_pre, nin[1]).astype(BF)
        dagg[pl.ds(pl.multiple_of(s * N + h * NH, NH), NH), :] = dagg_own[rows, :]
        gather_dagg[h].start(dagg_own.at[rows, :])
    gdirect[...] = ncot[...].astype(F32) + dot_nt(dnpre[...], nin[0])
    nodes_out_v[...] = (
        nodes_in[...].astype(F32) + normalize(nmsg[...], node_gain)).astype(BF)
    stores[1].start()

    mine_cols = pl.ds(pl.multiple_of(c * HALF, HALF), HALF)
    sib_cols = pl.ds(pl.multiple_of((1 - c) * HALF, HALF), HALF)

    class Products:
        def __init__(self, pairs, ssend, srecv, own):
            self.pairs, self.ssend, self.srecv, self.own = pairs, ssend, srecv, own
            self.s0, self.r0 = sems.take(len(pairs)), sems.take(len(pairs))

        def sib_copy(self, i):
            return remote(self.ssend.at[i], self.srecv.at[i], self.s0(i), self.r0(i), d, sib)

        def products(self, i):
            left, right = self.pairs[i]
            columns = jnp.concatenate([right[:, sib_cols], right[:, mine_cols]], axis=1)
            grad = dot_tn(left[...], columns)
            self.ssend[i] = grad[:, :HALF].astype(BF)
            cp = self.sib_copy(i)
            cp.start()
            pending.append(cp)
            self.own[i] = grad[:, HALF:]

        def chip_sum(self, i, rows):
            return self.own[i, rows, :] + self.srecv[i, rows, :].astype(F32)

    class Peers:
        def __init__(self, count, send, recv, to):
            self.count, self.sbuf, self.rbuf, self.to = count, send, recv, to
            self.ss, self.rs = sems.take(count - 1), sems.take(count - 1)

        def copy(self, k):
            return remote(
                self.sbuf.at[k - 1], self.rbuf.at[k - 1], self.ss(k - 1), self.rs(k - 1),
                *self.to(k))

        def send(self, k, value):
            self.sbuf[k - 1] = value.astype(BF)
            cp = self.copy(k)
            cp.start()
            pending.append(cp)

        def total(self, mine):
            for k in range(1, self.count):
                self.copy(k).wait_recv()
                mine = mine + self.rbuf[k - 1].astype(F32)
            return mine

    def on_y(k):
        return (y + k) % NY * NZ + z, s

    def on_z(k):
        return y * NZ + (z + k) % NZ, s

    Z_ORDER = (4, 3, 5, 2, 6, 1, 7)

    class Weights(Products):
        def __init__(self, pairs, ssend, srecv, own, ysend, yrecv, ysum, zsend, zrecv, zsum, xsend, xrecv):
            super().__init__(pairs, ssend, srecv, own)
            self.y = [Peers(NY, ysend.at[i], yrecv.at[i], on_y) for i in range(3)]
            self.z = [Peers(NZ, zsend.at[i], zrecv.at[i], on_z) for i in range(3)]
            self.ysum, self.zsum, self.xsend, self.xrecv = ysum, zsum, xsend, xrecv
            self.sx, self.rx = sems.take(NX - 1), sems.take(NX - 1)

        def to_y(self, i):
            self.sib_copy(i).wait_recv()
            for k in (2, 1, 3):
                rows = pl.ds(pl.multiple_of((y + k) % NY * 128, 128), 128)
                self.y[i].send(k, self.chip_sum(i, rows))

        def to_z(self, i):
            rows = pl.ds(pl.multiple_of(y * 128, 128), 128)
            self.ysum[i] = self.y[i].total(self.chip_sum(i, rows))
            for k in Z_ORDER:
                rows = pl.ds(pl.multiple_of((z + k) % NZ * 16, 16), 16)
                self.z[i].send(k, self.ysum[i, rows, :])

        def x_copy(self, k):
            return remote(
                self.xsend.at[k - 1], self.xrecv.at[k - 1], self.sx(k - 1), self.rx(k - 1),
                d, on_x(k))

        def to_x(self):
            rows = pl.ds(pl.multiple_of(z * 16, 16), 16)
            for i in range(3):
                self.zsum[i] = self.z[i].total(self.ysum[i, rows, :])
            for k in (2, 1, 3):
                @pl.when((x + k) % NX < 3)
                def _():
                    self.xsend[k - 1] = self.zsum[(x + k) % NX].astype(BF)
                    self.x_copy(k).start()

        def finish(self):
            total = self.zsum[jnp.minimum(x, 2)]
            for k in (1, 3, 2):
                self.x_copy(k).wait_recv()
                total = total + self.xrecv[k - 1].astype(F32)
            return total

        def drain(self):
            for k in (2, 1, 3):
                pl.when((x + k) % NX < 3)(self.x_copy(k).wait_send)

    class LastWeights(Products):
        def __init__(self, pairs, ssend, srecv, own, zsend, zrecv, zsum, ysend, yrecv, ysum, xsend, xrecv):
            super().__init__(pairs, ssend, srecv, own)
            self.zsum, self.ysum, self.xsend, self.xrecv = zsum, ysum, xsend, xrecv
            self.z = Peers(NZ, zsend, zrecv, on_z)
            self.y = Peers(NY, ysend, yrecv, on_y)
            self.sx, self.rx = sems.take(1), sems.take(3)

        def to_z(self):
            self.sib_copy(0).wait_recv()
            for k in Z_ORDER:
                rows = pl.ds(pl.multiple_of((z + k) % NZ * 64, 64), 64)
                self.z.send(k, self.chip_sum(0, rows))

        def to_y(self):
            rows = pl.ds(pl.multiple_of(z * 64, 64), 64)
            self.zsum[...] = self.z.total(self.chip_sum(0, rows))
            for k in (2, 1, 3):
                rows = pl.ds(pl.multiple_of((y + k) % NY * 16, 16), 16)
                self.y.send(k, self.zsum[rows, :])

        def x_copy(self, k):
            return remote(self.xsend, self.xrecv.at[k], self.sx(0), self.rx(k), d, 6 + c)

        def to_x(self):
            total = self.y.total(self.zsum[pl.ds(pl.multiple_of(y * 16, 16), 16), :])
            self.ysum[...] = total
            self.xsend[...] = total.astype(BF)
            for k in range(3):
                pl.when(x == k)(self.x_copy(k).start)

        def finish(self):
            total = self.ysum[...]
            for k in range(3):
                self.x_copy(k).wait_recv()
                total = total + self.xrecv[k].astype(F32)
            return total

        def drain(self):
            pl.when(x < 3)(self.x_copy(0).wait_send)

    node_weights = Weights(
        ((nodes_in, dnpre), (agg, dnpre), (nhid, dnmsg)),
        fn_ssend, fn_srecv, fn_own, fn_ysend, fn_yrecv, fn_ysum, fn_zsend, fn_zrecv, fn_zsum,
        fn_xsend, fn_xrecv)
    edge_weights = Weights(
        ((edges, dpre), (sent, dpre), (recv, dpre)),
        fe_ssend, fe_srecv, fe_own, fe_ysend, fe_yrecv, fe_ysum, fe_zsend, fe_zrecv, fe_zsum,
        fe_xsend, fe_xrecv)
    out_weights = LastWeights(
        ((hid, dmsg),),
        fo_ssend, fo_srecv, fo_own, fo_zsend, fo_zrecv, fo_zsum, fo_ysend, fo_yrecv, fo_ysum,
        fo_xsend, fo_xrecv)

    for i in range(3):
        node_weights.products(i)
    for i in range(3):
        node_weights.to_y(i)
    for h in range(2):
        gather_dagg[h].relay()
    for h in range(2):
        gather_dagg[h].forward(2)
    for h in range(2):
        gather_dagg[h].near()

    def chip_part(dx):
        rows = pl.ds(pl.multiple_of((x + dx) % NX * 2 * N, 2 * N), 2 * N)
        return dot(pr[:, rows], dagg[rows, :])

    gedge[...] = ecot[...].astype(F32) + chip_part(0)
    gedge[...] = gedge[...] + chip_part(1)
    gedge[...] = gedge[...] + chip_part(3)
    for h in range(2):
        gather_dagg[h].far()

    def edge_backward(r0):
        rows = pl.ds(r0, BLOCK)
        up = gedge[rows, :] + chip_part(2)
        gedge[rows, :] = up
        grad_msg = normalize_back(msg[rows, :], edge_gain, up).astype(BF)
        dmsg[rows, :] = grad_msg
        grad = (dot_nt(grad_msg, eout[...]) * swish_slope(pre[rows, :])).astype(BF)
        dpre[rows, :] = grad

    rows_loop(E, BLOCK, edge_backward)

    def ghost_block(near, dx):
        place = PN + ((target(near, dx) - d + DOM) % S) * SLAB
        return dot(pst[pl.ds(pl.multiple_of(place, SLAB), SLAB), :], dsent[...])


    def send_grad(r0):
        rows = pl.ds(r0, BLOCK)
        dsent[rows, :] = dot_nt(dpre[rows, :], ein[1]).astype(BF)

    rows_loop(E, BLOCK, send_grad)
    reduce_ghost = Scatter(ghost_block, gg_own, gg_ssend, gg_srecv, gg_xsend, gg_xrecv)
    reduce_ghost.start()
    edge_weights.products(0)
    out_weights.products(0)
    reduce_ghost.middle()
    edge_weights.to_y(0)
    edge_weights.products(1)
    out_weights.to_z()
    edge_weights.to_y(1)
    edge_weights.products(2)

    def recv_grad(r0):
        rows = pl.ds(r0, BLOCK)
        drecv[rows, :] = dot_nt(dpre[rows, :], ein[2]).astype(BF)

    rows_loop(E, BLOCK, recv_grad)
    edge_weights.to_y(2)

    def own_block(near, dx):
        rows = pl.ds(pl.multiple_of(target(near, dx) * N, N), N)
        r0 = (near * NX + dx) * N
        return dot(pst[rows, :], dsent[...]) + dot(prt[r0:r0 + N, :], drecv[...])

    reduce_own = Scatter(own_block, own_own, own_ssend, own_srecv, own_xsend, own_xrecv)
    reduce_own.start()
    reduce_own.middle()
    a2_send[...] = reduce_ghost.finish().astype(BF)
    swap_back = Swap(a2_send, retg)
    swap_back.start()
    for i in range(3):
        node_weights.to_z(i)

    def edge_grad(r0):
        rows = pl.ds(r0, BLOCK)
        egrad_v[rows, :] = (gedge[rows, :] + dot_nt(dpre[rows, :], ein[0])).astype(BF)

    rows_loop(E, BLOCK, edge_grad)
    stores[2].start()
    place = hot(lax.broadcasted_iota(jnp.int32, (S * SLAB, N), 1) + s * N == lists_c)
    swap_back.finish()
    gather_back = Gather(retg, lambda q: ((q - d + DOM) % S) * SLAB, SLAB)
    gather_back.start(retg.at[pl.ds(pl.multiple_of(t_mine * SLAB, SLAB), SLAB), :])
    edge_weights.to_z(0)
    out_weights.to_y()
    node_weights.to_x()
    edge_weights.to_z(1)
    edge_weights.to_z(2)
    s_fin, r_fin = sems.take(6), sems.take(4)

    def fin_copy(group, i, slot, half):
        to = jnp.minimum(owner(group, i)[0], DOM * S - 1)
        return remote(
            fin.at[group], rows_in.at[slot, half], s_fin(3 * group + i), r_fin(2 * slot + half),
            to // S, to % S)

    def hand_out(group):
        for i in range(3):
            to, at, valid = owner(group, i)
            for slot in range(2):
                for half in range(2):
                    here = valid & (at == slot) & (c == half)
                    pl.when(here & (to != lin))(fin_copy(group, i, slot, half).start)

                    @pl.when(here & (to == lin))
                    def _():
                        rows_in[slot, half] = fin[group]

    out_weights.to_x()
    edge_weights.to_x()
    gather_back.relay()
    @pl.when(x < 3)
    def _():
        fin[1] = node_weights.finish()

    hand_out(1)

    gather_back.finish()
    direct = gdirect[...] + dot_tn(place, retg[...])
    ngrad[...] = (direct + reduce_own.finish()).astype(BF)

    @pl.when(x < 3)
    def _():
        fin[0] = edge_weights.finish()

    @pl.when(x == 3)
    def _():
        fin[0] = out_weights.finish()

    hand_out(0)
    for slot in range(2):
        for half in range(2):
            pl.when(from_other(slot, half))(fin_copy(0, 0, slot, half).wait_recv)
    shift = first_row % 16
    for choice in range(0, 16, 2):
        @pl.when(shift == choice)
        def _():
            split = min(16 - choice, OUT_ROWS)
            for half in range(2):
                cols = slice(half * HALF, (half + 1) * HALF)
                wout[:split, cols] = rows_in[0, half, choice:choice + split, :]
                if split < OUT_ROWS:
                    wout[split:, cols] = rows_in[1, half, :OUT_ROWS - split, :]

    for store in stores:
        store.wait()
    for cp in pending:
        cp.wait_send()
    node_weights.drain()
    edge_weights.drain()
    out_weights.drain()
    for group in range(2):
        for i in range(3):
            to, _, valid = owner(group, i)
            pl.when(valid & (to != lin))(fin_copy(group, i, 0, 0).wait_send)


def scratch():
    def bf(*shape):
        return pltpu.VMEM(shape, BF)

    def f32(*shape):
        return pltpu.VMEM(shape, F32)

    T = PN + S * SLAB

    def scatter(rows, *lead):
        return [
            bf(*lead, NX, rows, D), bf(*lead, NX, rows, D), bf(*lead, NX - 1, rows, D),
            bf(*lead, NX - 1, rows, D), f32(*lead, rows, D),
        ]

    def products(count):
        return [bf(count, D, HALF), bf(count, D, HALF), f32(count, D, HALF)]

    def weights():
        return [
            *products(3), bf(3, NY - 1, 128, HALF), bf(3, NY - 1, 128, HALF), f32(3, 128, HALF),
            bf(3, NZ - 1, 16, HALF), bf(3, NZ - 1, 16, HALF), f32(3, 16, HALF),
            bf(NX - 1, 16, HALF), bf(NX - 1, 16, HALF),
        ]

    return [
        bf(N, D), bf(N, D), bf(N, D), bf(E, D), bf(E, D),
        bf(E, D), bf(3, D, D), bf(D, D), bf(2, D, D), bf(D, D), bf(E, D),
        bf(E, T), bf(E, PN), bf(T, E), bf(PN, E), bf(T, D), f32(E, D), bf(E, D), bf(E, D),
        f32(E, D), f32(E, D), bf(E, D),
        bf(SLAB, D), *scatter(N // 2, 2),
        bf(N, D), f32(N, D), f32(N, D), bf(N, D), f32(N, D), bf(N, D), bf(N, D), bf(N, D), bf(PN, D),
        f32(E, D), bf(E, D), bf(E, D), bf(E, D), bf(E, D),
        *scatter(SLAB), bf(SLAB, D), bf(S * SLAB, D), *scatter(N),
        *weights(), *weights(),
        *products(1), bf(NZ - 1, 64, HALF), bf(NZ - 1, 64, HALF), f32(64, HALF),
        bf(NY - 1, 16, HALF), bf(NY - 1, 16, HALF), f32(16, HALF), bf(16, HALF), bf(NX - 1, 16, HALF),
        f32(2, 16, HALF), f32(2, 2, 16, HALF),
        pltpu.SemaphoreType.DMA((N_SEM,)),
    ]


def hand_over(a0, a1, a2, a3, w_in, b0, b1, b2, b3, w_out):
    for src, dst in ((a0, b0), (a1, b1), (a2, b2), (a3, b3)):
        dst[...] = src[...]
    for i in range(OUT_ROWS):
        w_out[:, i * D:(i + 1) * D] = w_in[i:i + 1, :]


def body(
    node_state, edge_state, senders, receivers, send_rows, edge_in, edge_out, edge_gain,
    node_in, node_out, node_gain, node_cot, edge_cot,
):
    vmem = pl.BlockSpec(memory_space=pltpu.VMEM)
    hbm = pl.BlockSpec(memory_space=pl.ANY)
    states = (
        jax.ShapeDtypeStruct((N, D), BF),
        jax.ShapeDtypeStruct((E, D), BF),
        jax.ShapeDtypeStruct((N, D), BF),
        jax.ShapeDtypeStruct((E, D), BF),
    )
    results = pl.pallas_call(
        kernel,
        out_shape=states + (jax.ShapeDtypeStruct((OUT_ROWS, D), F32),),
        in_specs=[vmem] * 5 + [hbm] * 8,
        out_specs=[hbm, hbm, vmem, hbm, vmem],
        scratch_shapes=scratch(),
        compiler_params=pltpu.CompilerParams(
            collective_id=0, has_side_effects=True, vmem_limit_bytes=60 * 1024 * 1024),
    )(
        senders.reshape(1, E), receivers.reshape(1, E), send_rows.transpose(0, 2, 1),
        edge_gain, node_gain,
        node_state, node_cot, edge_state, edge_in[0], edge_out[0], node_in[0], node_out[0], edge_cot,
    )
    return pl.pallas_call(
        hand_over,
        out_shape=states + (jax.ShapeDtypeStruct((1, OUT_ROWS * D), F32),),
        in_specs=[vmem] * 5,
        out_specs=[vmem] * 5,
    )(*results)


def solution(mesh):
    both = P(("dom", "esplit"), None)
    in_specs = (
        both, both, P(("dom", "esplit")), P(("dom", "esplit")), P("dom", None, None),
        P(), P(), P(), P(), P(), P(), both, both,
    )
    out_specs = (both, both, both, both, P(None, ("dom", "esplit")))
    return jax.shard_map(body, mesh=mesh, in_specs=in_specs, out_specs=out_specs, check_vma=False)
```
